32 devices in a mesh: head: 4 (over y, x), seq: 8 (over z, core).
Axes of the slice: x: 2, y: 2, z: 4, core: 2. Of those that a mesh axis runs over, the one named last changes fastest.
Arguments:
- tokens: bfloat16 [8192, 1024], P(('seq', 'head')), may hold values from -6 to 6
- cotangent: bfloat16 [8192, 1024], P(('seq', 'head')), may hold values from -6 to 6
- segments: int32 [8192], replicated, may hold values from 0 to 42, as said below
- w_query: bfloat16 [1024, 1024], P(('head', 'seq')), may hold values from -0.1875 to 0.1875
- w_key: bfloat16 [1024, 1024], P(('head', 'seq')), may hold values from -0.1875 to 0.1875
- w_value: bfloat16 [1024, 1024], P(('head', 'seq')), may hold values from -0.1875 to 0.1875
- w_out: bfloat16 [1024, 1024], P(('head', 'seq')), may hold values from -0.75 to 0.75
- w_up: bfloat16 [1024, 4096], P(('head', 'seq')), may hold values from -0.1875 to 0.1875
- w_down: bfloat16 [4096, 1024], P(('head', 'seq')), may hold values from -0.09375 to 0.09375
- norm_one: bfloat16 [1024], P(('head', 'seq')), may hold values from 0.5 to 1.5
- norm_two: bfloat16 [1024], P(('head', 'seq')), may hold values from 0.5 to 1.5
- rel_table: float32 [8, 32], P('head'), may hold values from -4 to 4
- decay_rate: float32 [8], P('head'), may hold values from 0.0001 to 0.06
Outputs:
- output: bfloat16 [8192, 1024], P(('seq', 'head'))
- input_grad: bfloat16 [8192, 1024], P(('seq', 'head'))
- grad_query: float32 [1024, 1024], P(('head', 'seq'))
- grad_key: float32 [1024, 1024], P(('head', 'seq'))
- grad_value: float32 [1024, 1024], P(('head', 'seq'))
- grad_out: float32 [1024, 1024], P(('head', 'seq'))
- grad_up: float32 [1024, 4096], P(('head', 'seq'))
- grad_down: float32 [4096, 1024], P(('head', 'seq'))
- grad_norm_one: float32 [1024], P(('head', 'seq'))
- grad_norm_two: float32 [1024], P(('head', 'seq'))
- grad_rel_table: float32 [8, 32], P('head')
- grad_decay_rate: float32 [8], P('head')
The draws below stay inside these ranges and needn't reach their ends.
Inputs may be any that keep to these rules, and one draw needn't show every extreme that they name: `segments`: document numbers never fall and are distinct between documents; no document spans two sequences. The documents of sequence s carry numbers from s * 43 to (s + 1) * 43 - 1, its first document the lowest of them and its last document the highest, with gaps allowed between. Within a sequence every document has 200 to 2000 tokens except the first and the last, which may be shorter, and one document of each sequence has exactly 2000.
All inputs are finite; a program needn't handle non-finite values.
Results may differ from the reference program's by a relative error of at most 0.013.
Values may be sent and summed in bfloat16 or wider, within the bound.
A program may use at most 256 MiB of HBM per device.

```python
import math
import jax
import jax.numpy as jnp
import numpy as np
from jax import lax

D = 1024
HEADS = 8
HD = 128
FF = 4096
BUCKETS = 32
WIN = 512
DOC_MIN = 200
DOC_MAX = 2000
TOKENS = 8192
LENGTH = 8192
SEQS = 1


def draw_segments(key, part):
    seq_count = TOKENS // LENGTH
    doc_slots = LENGTH // DOC_MIN + 3
    side_slots = LENGTH // DOC_MIN + 1
    key_after, key_before = jax.random.split(jax.random.fold_in(key, 11))
    pivot = LENGTH // 2 - DOC_MAX // 2
    after_len = jax.random.randint(key_after, (seq_count, side_slots), DOC_MIN, DOC_MAX + 1)
    before_len = jax.random.randint(key_before, (seq_count, side_slots), DOC_MIN, DOC_MAX + 1)
    after_starts = pivot + DOC_MAX + jnp.cumsum(after_len, axis=1) - after_len
    before_starts = pivot - jnp.cumsum(before_len, axis=1)
    far_mark = LENGTH + 1
    after_starts = jnp.where(after_starts < LENGTH, after_starts, far_mark)
    before_starts = jnp.where(before_starts > 0, before_starts, far_mark)
    pivot_col = jnp.full((seq_count, 1), pivot, jnp.int32)
    starts = jnp.concatenate([before_starts, pivot_col, after_starts], axis=1)
    starts = jnp.where(starts > 0, starts, far_mark)
    starts = jnp.sort(starts, axis=1)
    position = jnp.arange(LENGTH)
    local_ids = jax.vmap(lambda row: jnp.searchsorted(row, position, side='right'))(starts).astype(jnp.int32)
    doc_counts = jnp.sum((starts < LENGTH).astype(jnp.int32), axis=1) + 1
    final_doc = local_ids == doc_counts[:, None] - 1
    local_ids = jnp.where(final_doc, doc_slots - 1, local_ids)
    offsets = jnp.arange(seq_count) * doc_slots
    return (local_ids + offsets[:, None]).reshape(TOKENS).astype(jnp.int32)


def level_of(stream_key, extent, cuts, least, high):
    def one(axis_at, parts):
        steps = jax.random.uniform(jax.random.fold_in(jax.random.fold_in(stream_key, 6), axis_at), (parts,), jnp.float32, least / len(cuts), high / len(cuts))
        return jnp.repeat(jnp.exp(steps), extent[axis_at] // parts).reshape((-1,) + (1,) * (len(extent) - axis_at - 1))

    loudness = one(*cuts[0])
    for cut in cuts[1:]:
        loudness = loudness * one(*cut)
    return loudness


def bell_draw(rng, extent, deviation, limit, shards=(), kind=jnp.bfloat16):
    loudness = level_of(rng, extent, shards, -0.22, 0.18) if shards else 1.0
    entries = jax.random.normal(rng, extent, jnp.float32) * deviation * loudness
    return jnp.minimum(jnp.maximum(entries, -limit), limit).astype(kind)


def setup_inputs(seed: int = 0) -> dict:
    seeds = jax.random.split(jax.random.key(seed), 14)
    return {
        "tokens": bell_draw(seeds[0], (TOKENS, D), 1.0, 6.0, ((0, 32),)),
        "cotangent": bell_draw(seeds[1], (TOKENS, D), 1.0, 6.0, ((0, 32),)),
        "segments": draw_segments(jax.random.fold_in(seeds[13], 71), 0),
        "w_query": bell_draw(seeds[3], (D, D), D ** -0.5, 0.1875, ((0, 32),)),
        "w_key": bell_draw(seeds[4], (D, D), D ** -0.5, 0.1875, ((0, 32),)),
        "w_value": bell_draw(seeds[5], (D, D), D ** -0.5, 0.1875, ((0, 32),)),
        "w_out": bell_draw(seeds[6], (D, D), (D // 16) ** -0.5, 0.75, ((0, 32),)),
        "w_up": bell_draw(seeds[7], (D, FF), D ** -0.5, 0.1875, ((0, 32),)),
        "w_down": bell_draw(seeds[8], (FF, D), FF ** -0.5, 0.09375, ((0, 32),)),
        "norm_one": jnp.clip(1.0 + 0.1 * jax.random.normal(seeds[9], (D,), jnp.float32), 0.5, 1.5).astype(jnp.bfloat16),
        "norm_two": jnp.clip(1.0 + 0.1 * jax.random.normal(seeds[10], (D,), jnp.float32), 0.5, 1.5).astype(jnp.bfloat16),
        "rel_table": bell_draw(seeds[11], (HEADS, BUCKETS), 1.0, 4.0, ((0, 4),), jnp.float32),
        "decay_rate": jnp.clip(jnp.exp(math.log(0.06) - 6.3969297 * jax.random.uniform(seeds[12], (HEADS,), jnp.float32) ** level_of(seeds[12], (HEADS,), ((0, 4),), -0.2, 0.2)), 0.0001, 0.06),
    }


epsilon = 1e-06
negative = -1e+30
state_scale = 1.0 / 1024.0
highest = lax.Precision.HIGHEST

@jax.custom_vjp
def low(v):
    return lax.optimization_barrier(v.astype(jnp.bfloat16)).astype(jnp.float32)

@jax.custom_vjp
def low_back(v):
    return v

def low_keep(v):
    return (low(v), None)

def low_pass(kept, grad):
    return (grad,)

def back_keep(v):
    return (v, None)

def back_low(kept, grad):
    return (low(grad),)
low.defvjp(low_keep, low_pass)
low_back.defvjp(back_keep, back_low)

def bucket_onehot(window_len, bucket_count):
    distance = np.arange(window_len)
    scaled = np.floor(np.log(np.maximum(distance, 1) / 16.0) / np.log(8.0) * 16.0)
    larger = np.minimum(16 + np.maximum(scaled, 0), bucket_count - 1)
    bucket = np.where(distance < 16, distance, larger).astype(np.int32)
    return (bucket[:, None] == np.arange(bucket_count)[None, :]).astype(np.float32)

def skewed(extended, row_count, col_count):
    head_count = extended.shape[0]
    span = row_count + col_count
    flipped = jnp.concatenate([extended[:, ::-1], jnp.zeros((head_count, 1), extended.dtype)], axis=1)
    tiled = jnp.broadcast_to(flipped[:, None, :], (head_count, row_count, span)).reshape(head_count, row_count * span)
    tiled = tiled[:, :row_count * (span - 1)].reshape(head_count, row_count, span - 1)
    return tiled[:, :, row_count - 1:row_count - 1 + col_count]

def rms_scale(values, gain):
    return values * lax.rsqrt(lax.optimization_barrier(jnp.mean(values * values, axis=-1, keepdims=True)) + epsilon) * gain

def product(left, right):
    return jnp.dot(left, right, precision=highest, preferred_element_type=jnp.float32)

def group_state(carried_state, query_c, key_c, value_c, seg_group, seg_before, decay_rate):
    length_c = query_c.shape[0]
    position = jnp.arange(length_c).astype(jnp.float32)
    distance = position[:, None] - position[None, :]
    inside = (distance >= 0) & (seg_group[:, None] == seg_group[None, :])
    decay_w = jnp.where(inside[None], jnp.exp(-decay_rate[:, None, None] * jnp.maximum(distance, 0.0)[None]), 0.0)
    affinity = jnp.einsum('ihd,jhd->hij', query_c, key_c, precision=highest) * state_scale
    readout = jnp.einsum('hij,jhd->ihd', affinity * decay_w, value_c, precision=highest)
    live_mask = (seg_group == seg_before).astype(jnp.float32)
    entering = jnp.exp(-decay_rate[None, :] * (position[:, None] + 1.0)) * live_mask[:, None] * state_scale
    readout = readout + jnp.einsum('ihd,hde->ihe', query_c, carried_state, precision=highest) * entering[:, :, None]
    keeping = (seg_group == seg_group[-1]).astype(jnp.float32)
    leaving = jnp.exp(-decay_rate[None, :] * (length_c - 1.0 - position[:, None])) * keeping[:, None]
    carry_keep = jnp.exp(-decay_rate * length_c) * (seg_group[-1] == seg_before).astype(jnp.float32)
    updated = jnp.einsum('jhd,jhe->hde', key_c * leaving[:, :, None], value_c, precision=highest)
    updated = updated + carry_keep[:, None, None] * carried_state
    return (updated, readout)

def attend(queries, keys, values, seg_seq, table):
    length_s, head_count, head_width = queries.shape
    scale = 1.0 / math.sqrt(head_width)
    onehot_table = jnp.asarray(bucket_onehot(WIN, BUCKETS))
    by_distance = jnp.dot(table, onehot_table.T, precision=highest)
    extended = jnp.concatenate([jnp.zeros((head_count, WIN - 1), jnp.float32), by_distance, jnp.zeros((head_count, WIN), jnp.float32)], axis=1)
    bias_full = skewed(extended, WIN, 2 * WIN)
    front = jnp.zeros((WIN, head_count, head_width), jnp.float32)
    keys_pad = jnp.concatenate([front, keys], axis=0)
    values_pad = jnp.concatenate([front, values], axis=0)
    segs_pad = jnp.concatenate([jnp.full((WIN,), -1, jnp.int32), seg_seq])
    row_pos = jnp.arange(WIN, dtype=jnp.int32)[:, None]
    col_pos = jnp.arange(2 * WIN, dtype=jnp.int32)[None, :]
    near = (row_pos - col_pos + WIN >= 0) & (row_pos - col_pos + WIN < WIN)

    def one_block(number):
        start = number * WIN
        query_b = lax.dynamic_slice_in_dim(queries, start, WIN, 0)
        key_b = lax.dynamic_slice_in_dim(keys_pad, start, 2 * WIN, 0)
        value_b = lax.dynamic_slice_in_dim(values_pad, start, 2 * WIN, 0)
        seg_q = lax.dynamic_slice_in_dim(seg_seq, start, WIN, 0)
        seg_k = lax.dynamic_slice_in_dim(segs_pad, start, 2 * WIN, 0)
        raw = jnp.einsum('ihd,jhd->hij', query_b, key_b, precision=highest) * scale
        scores = low_back(raw + bias_full)
        visible = near & (seg_q[:, None] == seg_k[None, :])
        scores = jnp.where(visible[None], scores, negative)
        softmax_w = jax.nn.softmax(scores, axis=-1)
        return jnp.einsum('hij,jhd->ihd', low(softmax_w), value_b, precision=highest)
    numbers = jnp.arange(length_s // WIN, dtype=jnp.int32)
    blocks = lax.map(jax.checkpoint(one_block), numbers)
    return blocks.reshape(length_s, head_count, head_width)

def recur(queries, keys, values, seg_seq, decay_rate):
    length_s, head_count, head_width = queries.shape
    count = length_s // WIN
    items = (queries.reshape(count, WIN, head_count, head_width), keys.reshape(count, WIN, head_count, head_width), values.reshape(count, WIN, head_count, head_width), seg_seq.reshape(count, WIN))

    def step(carry, item):
        carried_state, prior = carry
        updated, readout = group_state(carried_state, item[0], item[1], item[2], item[3], prior, decay_rate)
        return ((updated, item[3][-1]), readout)
    start_carry = (jnp.zeros((head_count, head_width, head_width), jnp.float32), jnp.int32(-1))
    _, readouts = lax.scan(jax.checkpoint(step), start_carry, items)
    return readouts.reshape(length_s, head_count, head_width)

def layer_seq(inputs, seg_seq, wq_full, wk_full, wv_full, wo_full, wu_full, wd_full, gain_one, gain_two, table, decay_rate):
    length_s = inputs.shape[0]
    head_count = table.shape[0]
    normed = low(rms_scale(inputs, gain_one))
    queries = low(low_back(product(normed, wq_full))).reshape(length_s, head_count, HD)
    keys = low(low_back(product(normed, wk_full))).reshape(length_s, head_count, HD)
    values = low(low_back(product(normed, wv_full))).reshape(length_s, head_count, HD)
    attended = attend(queries, keys, values, seg_seq, table)
    readout = recur(queries, keys, values, seg_seq, decay_rate)
    mixed = low(low_back((attended + readout).reshape(length_s, D)))
    resid_one = inputs + low_back(product(mixed, wo_full))
    normed_two = low(rms_scale(resid_one, gain_two))
    up_proj = low_back(product(normed_two, wu_full))
    activated = low(jax.nn.gelu(up_proj))
    return resid_one + low_back(product(activated, wd_full))

def reference(tokens, cotangent, segments, w_query, w_key, w_value, w_out, w_up, w_down, norm_one, norm_two, rel_table, decay_rate):

    def forward(inputs, wq_full, wk_full, wv_full, wo_full, wu_full, wd_full, gain_one, gain_two, table, rates):
        seq_inputs = inputs.reshape(SEQS, LENGTH, D)
        seq_segs = segments.reshape(SEQS, LENGTH)

        def one_seq(carry, item):
            return (carry, layer_seq(item[0], item[1], wq_full, wk_full, wv_full, wo_full, wu_full, wd_full, gain_one, gain_two, table, rates))
        _, results = lax.scan(jax.checkpoint(one_seq), jnp.int32(0), (seq_inputs, seq_segs))
        return results.reshape(TOKENS, D)
    floats = (tokens.astype(jnp.float32), w_query.astype(jnp.float32), w_key.astype(jnp.float32), w_value.astype(jnp.float32), w_out.astype(jnp.float32), w_up.astype(jnp.float32), w_down.astype(jnp.float32), norm_one.astype(jnp.float32), norm_two.astype(jnp.float32), rel_table.astype(jnp.float32), decay_rate.astype(jnp.float32))
    result, back_fn = jax.vjp(forward, *floats)
    grads = back_fn(cotangent.astype(jnp.float32))
    return (result.astype(jnp.bfloat16), grads[0].astype(jnp.bfloat16), grads[1], grads[2], grads[3], grads[4], grads[5], grads[6], grads[7], grads[8], grads[9], grads[10])
```

```python
import functools
import math

import jax
import jax.numpy as jnp
import numpy as np
from jax import lax
from jax.experimental import pallas as pl
from jax.experimental.pallas import tpu as pltpu
from jax.sharding import PartitionSpec as P

HD = 128
BUCKETS = 32
WIN = 512
TILE = 256

epsilon = 1e-06
negative = -1e30
state_scale = 1.0 / 1024.0
MESH = pl.DeviceIdType.MESH
f32 = jnp.float32
bf16 = jnp.bfloat16


def dot(a, b):
    return jnp.dot(a, b, preferred_element_type=f32)


def dot_t(a, b):
    return lax.dot_general(a, b, (((1,), (1,)), ((), ())), preferred_element_type=f32)


def t_dot(a, b):
    return lax.dot_general(a, b, (((0,), (0,)), ((), ())), preferred_element_type=f32)


class Place:
    def __init__(self):
        self.h = lax.axis_index("head")
        self.s = lax.axis_index("seq")
        self.n = lax.axis_size("seq")
        self.nz = self.n // 2
        self.z = self.s // 2
        self.core = self.s % 2
        x, y = self.h % 2, self.h // 2
        self.heads = [2 * y + 1 - x, 2 * (1 - y) + x, 2 * (1 - y) + 1 - x]

    def head_dev(self, k):
        return (self.heads[k], self.s)

    def z_to(self, k):
        return ((self.z + k) % self.nz) * 2 + self.core

    def z_from(self, k):
        return ((self.z + self.nz - k) % self.nz) * 2 + self.core

    def z_dev(self, k):
        return (self.h, self.z_to(k))

    def other(self):
        return self.z * 2 + 1 - self.core

    def core_dev(self):
        return (self.h, self.other())

    def seq_dev(self, by):
        return (self.h, (self.s + self.n + by) % self.n)


def greet(devices):
    barrier = pltpu.get_barrier_semaphore()
    for device in devices:
        pl.semaphore_signal(barrier, inc=1, device_id=device, device_id_type=MESH)
    pl.semaphore_wait(barrier, len(devices))


class Sends:
    def __init__(self, send_sems, recv_sems):
        self.send_sems, self.recv_sems = send_sems, recv_sems
        self.at, self.all = 0, []

    def put(self, src, dst, device, start=True):
        copy = pltpu.make_async_remote_copy(
            src_ref=src,
            dst_ref=dst,
            send_sem=self.send_sems.at[self.at],
            recv_sem=self.recv_sems.at[self.at],
            device_id=device,
            device_id_type=MESH,
        )
        self.at += 1
        self.all.append(copy)
        if start:
            copy.start()
        return copy

    def finish(self):
        for copy in self.all:
            copy.wait_send()


def rms(x):
    return lax.rsqrt(jnp.mean(x * x, axis=-1, keepdims=True) + epsilon)


def kernel_one(
    tok_ref, p1_ref, wo_ref, hall_ref, qkv_ref, wb_ref, woz_ref, gains_ref,
    xa, a1, send_sems, recv_sems,
):
    me = Place()
    nz, rows = me.nz, wo_ref.shape[0]
    tok = tok_ref.shape[0]
    peers = [me.head_dev(k) for k in range(3)]
    greet(peers + [me.z_dev(k) for k in range(1, nz)] + [me.core_dev()])
    sends = Sends(send_sems, recv_sems)
    first = [sends.put(p1_ref.at[me.heads[k]], a1.at[me.h], peers[k]) for k in range(3)]
    wo_z = [sends.put(wo_ref, woz_ref.at[me.s], me.z_dev(k)) for k in range(1, nz)]
    toks = [sends.put(tok_ref, xa.at[me.h], peers[k]) for k in range(3)]
    wo_c = [sends.put(wo_ref, woz_ref.at[me.s], me.core_dev())]
    woz_ref[me.s] = wo_ref[...]
    a1[me.h] = p1_ref[me.h]
    xa[me.h] = tok_ref[...]
    for copy in first:
        copy.wait_recv()
    w_z = [sends.put(a1, wb_ref.at[:, me.s], me.z_dev(k)) for k in range(1, nz)]
    w_c = [sends.put(a1, wb_ref.at[:, me.s], me.core_dev())]
    wb_ref[:, me.s] = a1[...]
    for k in range(1, nz):
        wo_z[k - 1].wait_recv()
        piece = woz_ref.at[me.z_from(k)]
        wo_c.append(sends.put(piece, piece, me.core_dev()))
    for k in range(1, nz):
        w_z[k - 1].wait_recv()
        piece = wb_ref.at[:, me.z_from(k)]
        w_c.append(sends.put(piece, piece, me.core_dev()))
    for copy in wo_c + w_c:
        copy.wait_recv()
    group = 128 // rows
    lanes = []
    for h in range(4):
        for s in range(0, me.n, group):
            lanes.append(sum(wb_ref[h, s + i, :, 768:896].astype(f32) for i in range(group)))
    gains = jnp.concatenate(lanes, axis=1)[0:8]
    gains_ref[...] = gains
    gain_one = gains[0:1]
    for copy in toks:
        copy.wait_recv()

    def block(b, _):
        x = xa[b].astype(f32)
        hb = (x * rms(x) * gain_one).astype(bf16)
        at = pl.ds(pl.multiple_of(b * tok, tok), tok)
        hall_ref[at] = hb
        w = wb_ref[...].reshape(4 * me.n * rows, 896)
        for j in range(3):
            out = dot(hb, w[:, j * 256 : j * 256 + 256]).astype(bf16)
            qkv_ref[2 * j, at] = out[:, :HD]
            qkv_ref[2 * j + 1, at] = out[:, HD:]
        return 0

    lax.fori_loop(0, 4, block, 0)
    sends.finish()


def call(kernel, collective_id, outs, scratch, copies, name, *args, scalars=0):
    return pl.pallas_call(
        kernel,
        out_shape=[jax.ShapeDtypeStruct(shape, kind) for shape, kind in outs],
        in_specs=[pl.BlockSpec(memory_space=pltpu.SMEM)] * scalars
        + [pl.BlockSpec(memory_space=pltpu.VMEM)] * (len(args) - scalars),
        out_specs=[pl.BlockSpec(memory_space=pltpu.VMEM)] * len(outs),
        scratch_shapes=[pltpu.VMEM(shape, kind) for shape, kind in scratch]
        + [pltpu.SemaphoreType.DMA((copies,)), pltpu.SemaphoreType.DMA((copies,))],
        compiler_params=pltpu.CompilerParams(
            collective_id=collective_id, has_side_effects=True, vmem_limit_bytes=60 << 20
        ),
        name=name,
    )(*args)


def packed_rows(w_query, w_key, w_value, norm_one, norm_two):
    rows = w_query.shape[0]
    group = 128 // rows
    lane = np.arange(128) // rows
    mine = jnp.asarray(lane) == lax.axis_index("seq") % group
    gains = [jnp.where(mine, jnp.tile(g, group), 0)[None] for g in (norm_one, norm_two)]
    gains = jnp.concatenate(gains + [jnp.zeros((rows - 2, 128), bf16)], axis=0)
    gains = jnp.broadcast_to(gains[:, None], (rows, 4, 128))
    parts = [w.reshape(rows, 4, 256) for w in (w_query, w_key, w_value)]
    return jnp.concatenate(parts + [gains], axis=2).transpose(1, 0, 2)


def stage_one(tokens, w_query, w_key, w_value, w_out, norm_one, norm_two):
    n = lax.axis_size("seq")
    rows = w_query.shape[0]
    p1 = packed_rows(w_query, w_key, w_value, norm_one, norm_two)
    tok = tokens.shape[0]
    outs = [
        ((4 * tok, 1024), bf16),
        ((6, 4 * tok, HD), bf16),
        ((4, n, rows, 896), bf16),
        ((n, rows, 1024), bf16),
        ((8, 1024), f32),
    ]
    scratch = [((4, tok, 1024), bf16), ((4, rows, 896), bf16)]
    copies = 6 + 2 * (n // 2 - 1) + 2 * (n // 2)
    return call(kernel_one, 0, outs, scratch, copies, "gather_qkv", tokens, p1, w_out)


LOG2E = math.log2(math.e)
KEY_SCALE = LOG2E / math.sqrt(HD)


def bucket_starts():
    distance = np.arange(WIN)
    scaled = np.floor(np.log(np.maximum(distance, 1) / 16.0) / np.log(8.0) * 16.0)
    larger = np.minimum(16 + np.maximum(scaled, 0), BUCKETS - 1)
    bucket = np.where(distance < 16, distance, larger).astype(np.int32)
    return [int(np.argmax(bucket == b)) for b in range(BUCKETS)]


STARTS = bucket_starts()


def grid_of(axis, shape=(TILE, TILE)):
    return lax.broadcasted_iota(jnp.int32, shape, axis)


def column(row):
    eye = grid_of(0) == grid_of(1)
    return jnp.sum(jnp.where(eye, row, 0.0), axis=1, keepdims=True)


class Segs:
    def __init__(self, me, seg_ref, rows, cols):
        total = 4 * me.n
        self.rows, self.cols = rows, cols

        def row_at(offset):
            return seg_ref[pl.ds((4 * me.s + total + offset) % total, 1)].astype(f32)

        for j in range(6):
            row = row_at(j - 2)
            rows[j] = row
            if j >= 2:
                cols[j - 2] = column(row)
        last = lambda offset: row_at(offset)[:, TILE - 1 : TILE]
        self.last = [last(j - 2) for j in range(6)]
        same = lambda a, b: (a == b).astype(f32)
        self.keep = [same(self.last[t + 2], self.last[t + 1]) for t in range(4)]
        self.keep_before = same(last(-1), last(-5))
        self.keep_after = same(last(7), last(3))

    def live(self, t):
        return (self.cols[t] == self.last[t + 1]).astype(f32)

    def kept(self, t):
        return (self.cols[t] == self.last[t + 2]).astype(f32)


def fill_tables(table_ref, decay_ref, near, far, decay, enter, leave):
    gap = grid_of(0) - grid_of(1)
    place = grid_of(0, (TILE, 1)).astype(f32)
    for head in range(2):
        rate = decay_ref[0, head]
        for out, shift in ((near, 0), (far, TILE)):
            bias = jnp.full((TILE, TILE), table_ref[head, 0] * LOG2E, f32)
            for b in range(1, BUCKETS):
                bias = jnp.where(gap + shift >= STARTS[b], table_ref[head, b] * LOG2E, bias)
            out[head] = jnp.where(gap + shift >= 0, bias, negative)
        fall = jnp.exp(-rate * jnp.maximum(gap, 0).astype(f32)) * state_scale
        decay[head] = jnp.where(gap >= 0, fall, 0.0)
        enter[head] = jnp.exp(-rate * (place + 1.0)) * state_scale
        leave[head] = jnp.exp(-rate * (TILE - 1.0 - place))


def power(rate, steps):
    return jnp.exp(jnp.full((1, HD), -rate * steps, f32))


def tile_scores(raw, head, t, table_ref, near, far, segs):
    col = segs.cols[t]
    same = [col == segs.rows[t + j] for j in range(3)]
    reach = grid_of(0) < grid_of(1)
    rest = table_ref[head, BUCKETS - 1] * LOG2E
    s0 = jnp.where(same[0] & reach, raw[:, :TILE] * KEY_SCALE + rest, negative)
    s1 = jnp.where(same[1], raw[:, TILE : 2 * TILE] * KEY_SCALE + far[head], negative)
    s2 = jnp.where(same[2], raw[:, 2 * TILE :] * KEY_SCALE + near[head], negative)
    return s0, s1, s2, same[2]


def kernel_two(
    table_ref, decay_ref, seg_ref, qkv_ref, wup_ref, wdn_ref, cot_ref, woz_ref,
    y_ref, lse_ref, state_ref, kvx, call_ref, up_ref, dn_ref, wo_ref,
    u1, near, far, decay, enter, leave, rows, cols, yacc, local, sent, got,
    send_sems, recv_sems,
):
    me = Place()
    nz = me.nz
    peers = [me.head_dev(k) for k in range(3)]
    greet(
        peers
        + [me.z_dev(k) for k in range(1, nz)]
        + [me.core_dev(), me.seq_dev(-1), me.seq_dev(-2)]
    )
    sends = Sends(send_sems, recv_sems)
    half = pl.ds(me.core * nz, nz)
    other_half = pl.ds((1 - me.core) * nz, nz)
    width = up_ref.shape[-1]
    halo = sends.put(qkv_ref.at[2:6, 2 * TILE :], kvx.at[:, : 2 * TILE], me.seq_dev(1))
    first = []
    for k in range(3):
        columns = pl.ds(pl.multiple_of(me.heads[k] * width, width), width)
        first.append(sends.put(wup_ref.at[:, columns], u1.at[me.h], peers[k]))
    wo_h = [sends.put(woz_ref.at[half], wo_ref.at[me.h, half], peers[k]) for k in range(3)]
    cots = [sends.put(cot_ref, call_ref.at[me.h], peers[k]) for k in range(3)]
    kvx[:, 2 * TILE :] = qkv_ref[2:6]
    u1[me.h] = wup_ref[:, pl.ds(pl.multiple_of(me.h * width, width), width)]
    wo_ref[me.h] = woz_ref[...]
    call_ref[me.h] = cot_ref[...]
    segs = Segs(me, seg_ref, rows, cols)
    fill_tables(table_ref, decay_ref, near, far, decay, enter, leave)
    for head in range(2):
        fall = power(decay_ref[0, head], float(TILE))
        state = jnp.zeros((HD, HD), f32)
        for t in range(4):
            at = pl.ds(t * TILE, TILE)
            key = (qkv_ref[2 + head, at].astype(f32) * (leave[head] * segs.kept(t))).astype(bf16)
            add = t_dot(key, qkv_ref[4 + head, at])
            local[4 * head + t] = add
            state = fall * segs.keep[t] * state + add
        sent[head] = state.astype(bf16)
    carry = [sends.put(sent, got.at[k - 1], me.seq_dev(k)) for k in (1, 2)]
    for copy in first:
        copy.wait_recv()
    up_z = [sends.put(u1, up_ref.at[:, me.s], me.z_dev(k)) for k in range(1, nz)]
    core = [sends.put(u1, up_ref.at[:, me.s], me.core_dev())]
    up_ref[:, me.s] = u1[...]
    dn_z = [sends.put(wdn_ref, dn_ref.at[me.s], me.z_dev(k)) for k in range(1, nz)]
    core.append(sends.put(wdn_ref, dn_ref.at[me.s], me.core_dev()))
    dn_ref[me.s] = wdn_ref[...]

    def tile(index, base):
        head, t = index // 2, base + index % 2
        at = pl.ds(pl.multiple_of(t * TILE, TILE), TILE)
        wide = pl.ds(pl.multiple_of(t * TILE, TILE), 3 * TILE)
        raw = dot_t(qkv_ref[head, at], kvx[head, wide])
        s0, s1, s2, same = tile_scores(raw, head, t, table_ref, near, far, segs)
        top = jnp.maximum(jnp.maximum(s0, s1), s2).max(axis=1, keepdims=True)
        e0, e1, e2 = jnp.exp2(s0 - top), jnp.exp2(s1 - top), jnp.exp2(s2 - top)
        mass = (e0 + e1 + e2).sum(axis=1, keepdims=True)
        lse_ref[4 * head + t] = top + jnp.log2(mass)
        mix = jnp.concatenate([e0.astype(bf16), e1.astype(bf16), e2.astype(bf16)], axis=1)
        att = dot(mix, kvx[2 + head, wide]) / mass
        weight = jnp.where(same, raw[:, 2 * TILE :] * decay[head], 0.0).astype(bf16)
        yacc[head, at] = att + dot(weight, qkv_ref[4 + head, at])
        return base

    lax.fori_loop(0, 4, tile, 2)
    halo.wait_recv()
    lax.fori_loop(0, 4, tile, 0)
    for copy in wo_h:
        copy.wait_recv()
    for k in range(3):
        piece = wo_ref.at[me.heads[k], half]
        core.append(sends.put(piece, piece, me.core_dev()))
    for copy in carry:
        copy.wait_recv()
    for head in range(2):
        rate = decay_ref[0, head]
        fall = power(rate, float(TILE))
        past = power(rate, 4.0 * TILE) * segs.keep_before
        state = got[0, head].astype(f32) + past * got[1, head].astype(f32)
        for t in range(4):
            at = pl.ds(t * TILE, TILE)
            state_ref[4 * head + t] = state
            reach = enter[head] * segs.live(t)
            y = yacc[head, at] + dot(qkv_ref[head, at], state.astype(bf16)) * reach
            y_ref[at, head * HD : head * HD + HD] = y.astype(bf16)
            state = fall * segs.keep[t] * state + local[4 * head + t]
    for k in range(1, nz):
        up_z[k - 1].wait_recv()
        piece = up_ref.at[:, me.z_from(k)]
        core.append(sends.put(piece, piece, me.core_dev()))
    for k in range(1, nz):
        dn_z[k - 1].wait_recv()
        piece = dn_ref.at[me.z_from(k)]
        core.append(sends.put(piece, piece, me.core_dev()))
    for copy in cots + core:
        copy.wait_recv()
    sends.finish()


def stage_two(table, decay, segments, qkv, w_up, w_down, cotangent, woz):
    n = lax.axis_size("seq")
    nz = n // 2
    rows = w_up.shape[0]
    tok = cotangent.shape[0]
    outs = [
        ((4 * tok, 2 * HD), bf16),
        ((8, TILE, 1), f32),
        ((8, HD, HD), f32),
        ((4, 6 * TILE, HD), bf16),
        ((4, tok, 1024), bf16),
        ((4, n, rows, w_up.shape[1] // 4), bf16),
        ((n,) + w_down.shape, bf16),
        ((4, n, rows, 1024), bf16),
    ]
    scratch = [
        ((4, rows, w_up.shape[1] // 4), bf16),
        ((2, TILE, TILE), f32),
        ((2, TILE, TILE), f32),
        ((2, TILE, TILE), f32),
        ((2, TILE, 1), f32),
        ((2, TILE, 1), f32),
        ((6, 1, TILE), f32),
        ((4, TILE, 1), f32),
        ((2, 4 * TILE, HD), f32),
        ((8, HD, HD), f32),
        ((2, HD, HD), bf16),
        ((2, 2, HD, HD), bf16),
    ]
    copies = 1 + 3 + 3 + 3 + 2 + 2 * (nz - 1) + 2 * nz + 3
    return call(
        kernel_two, 1, outs, scratch, copies, "attention_forward",
        table, decay.reshape(1, 2), segments.reshape(-1, TILE), qkv, w_up, w_down, cotangent, woz,
        scalars=2,
    )


GELU_C = math.sqrt(2.0 / math.pi)
GELU_A = 0.044715


def part(i, size):
    return pl.ds(pl.multiple_of(i * size, size), size)


class Reduce:
    def __init__(self, me, sends, own, given, core_in, z_in):
        self.me, self.sends = me, sends
        self.own, self.given, self.core_in, self.z_in = own, given, core_in, z_in

    def start(self):
        self.core = self.sends.put(self.given, self.core_in, self.me.core_dev())

    def along(self):
        me = self.me
        self.core.wait_recv()
        self.core.wait_send()
        self.sends.all = [c for c in self.sends.all if c is not self.core]
        self.copies = []
        for k in range(1, me.nz):
            to = (me.z + k) % me.nz
            self.given[to] = (self.own[to] + self.core_in[to].astype(f32)).astype(bf16)
            self.copies.append(
                self.sends.put(self.given.at[to], self.z_in.at[k - 1], me.z_dev(k))
            )

    def total(self):
        me = self.me
        total = self.own[me.z] + self.core_in[me.z].astype(f32)
        for k, copy in enumerate(self.copies):
            copy.wait_recv()
            total = total + self.z_in[k].astype(f32)
        return total


def kernel_three(
    tok_ref, y_ref, wo_ref, up_ref, dn_ref, cot_ref, gains_ref,
    base_ref, outp_ref, ymix_ref, da_ref, dx1_ref, dyh_ref, gdown_ref, gupo_ref, gupg_ref, gnorm_ref,
    h2all, act, du, dn2s, dn2in, dyt, tile, gown, ggiven, gcore, gz,
    send_sems, recv_sems,
):
    me = Place()
    nz = me.nz
    tok = tok_ref.shape[0]
    peers = [me.head_dev(k) for k in range(3)]
    greet(peers + [me.z_dev(k) for k in range(1, nz)] + [me.core_dev()])
    sends = Sends(send_sems, recv_sems)
    ys = []
    for k in range(3):
        src = y_ref.at[part(me.heads[k], tok)]
        ys.append(sends.put(src, ymix_ref.at[:, part(me.h, 2 * HD)], peers[k]))
    ymix_ref[:, part(me.h, 2 * HD)] = y_ref[part(me.h, tok)]
    for copy in ys:
        copy.wait_recv()
    gain = gains_ref[1:2]
    x1 = dx1_ref

    def out_tile(j, _):
        cols = part(j, 256)
        x1[:, cols] = tok_ref[:, cols].astype(f32) + dot(ymix_ref[...], wo_ref[:, cols])
        return 0

    lax.fori_loop(0, 4, out_tile, 0)
    scale = rms(x1[...])
    h2all[part(me.h, tok)] = (x1[...] * scale * gain).astype(bf16)
    h2s = []
    for k in range(3):
        own = h2all.at[part(me.h, tok)]
        h2s.append(sends.put(own, own, peers[k]))
    base_ref[...] = x1[...]
    dn2_copies = []
    for k in range(-1, 3):
        b = me.h if k < 0 else me.heads[k]
        if k >= 0:
            h2s[k].wait_recv()
        rows = part(b, tok)

        def hidden(j, _):
            cols = part(j, 256)
            u = dot(h2all[rows], up_ref[:, cols])
            dg = dot_t(cot_ref[rows], dn_ref[cols])
            uu = u * u
            t = jnp.tanh(GELU_C * u * (1.0 + GELU_A * uu))
            act[rows, cols] = (0.5 * u * (1.0 + t)).astype(bf16)
            slope = 0.5 * (1.0 + t) + (0.5 * GELU_C) * u * (1.0 - t * t) * (1.0 + 3.0 * GELU_A * uu)
            du[rows, cols] = (slope * dg).astype(bf16)
            return 0

        lax.fori_loop(0, 4, hidden, 0)

        def back(j, _):
            cols = part(j, 256)
            dn2s[k + 1, :, cols] = dot_t(du[rows], up_ref[cols]).astype(bf16)
            return 0

        lax.fori_loop(0, 4, back, 0)
        if k >= 0:
            dn2_copies.append(sends.put(dn2s.at[k + 1], dn2in.at[k], peers[k]))

        def ahead(j, _):
            cols = part(j, 256)
            out = dot(act[rows], dn_ref[:, cols])
            if k < 0:
                base_ref[:, cols] = base_ref[:, cols] + out
            else:
                outp_ref[k, :, cols] = out.astype(bf16)
            return 0

        lax.fori_loop(0, 4, ahead, 0)

    half = 128

    def down_tile(j, _):
        tile[...] = t_dot(act[:, part(j, 256)], cot_ref[...])
        gown[j] = tile[part(me.core, half)]
        ggiven[j] = tile[part(1 - me.core, half)].astype(bf16)
        return 0

    lax.fori_loop(0, 4, down_tile, 0)
    down = Reduce(me, sends, gown, ggiven, gcore, gz)
    down.start()

    def up_tile(j, _):
        tile[...] = t_dot(h2all[:, part(j, 256)], du[...])
        for z in range(nz):
            gupo_ref[z, part(j, 32)] = tile[part(2 * z + me.core, 32)]
            gupg_ref[z, part(j, 32)] = tile[part(2 * z + 1 - me.core, 32)].astype(bf16)
        return 0

    lax.fori_loop(0, 4, up_tile, 0)
    down.along()
    for copy in dn2_copies:
        copy.wait_recv()
    dn2 = dn2s[0].astype(f32) + dn2in[0].astype(f32) + dn2in[1].astype(f32) + dn2in[2].astype(f32)
    n2 = x1[...] * scale
    gnorm_ref[...] = jnp.broadcast_to(jnp.sum(dn2 * n2, axis=0, keepdims=True), gnorm_ref.shape)
    wide = dn2 * gain
    dx1 = cot_ref[part(me.h, tok)].astype(f32) + scale * (
        wide - n2 * jnp.mean(wide * n2, axis=-1, keepdims=True)
    )
    dx1_ref[...] = dx1
    da_ref[...] = dx1.astype(bf16)

    def back_tile(j, _):
        out = dot_t(da_ref[...], wo_ref[part(j, 256)]).astype(bf16)
        dyt[2 * j] = out[:, :HD]
        dyt[2 * j + 1] = out[:, HD:]
        return 0

    lax.fori_loop(0, 4, back_tile, 0)
    dys = []
    for k in range(3):
        src = dyt.at[pl.ds(2 * me.heads[k], 2)]
        dys.append(sends.put(src, dyh_ref.at[:, part(me.h, tok)], peers[k]))
    dyh_ref[:, part(me.h, tok)] = dyt[pl.ds(2 * me.h, 2)]
    gdown_ref[...] = down.total()
    for copy in dys:
        copy.wait_recv()
    sends.finish()


def stage_three(tokens, y, wo, up, dn, cots, gains):
    nz = lax.axis_size("seq") // 2
    tok = tokens.shape[0]
    outs = [
        ((tok, 1024), f32),
        ((3, tok, 1024), bf16),
        ((tok, 1024), bf16),
        ((tok, 1024), bf16),
        ((tok, 1024), f32),
        ((2, 4 * tok, HD), bf16),
        ((128, 1024), f32),
        ((nz, 128, 1024), f32),
        ((nz, 128, 1024), bf16),
        ((8, 1024), f32),
    ]
    scratch = [
        ((4 * tok, 1024), bf16),
        ((4 * tok, 1024), bf16),
        ((4 * tok, 1024), bf16),
        ((4, tok, 1024), bf16),
        ((3, tok, 1024), bf16),
        ((8, tok, HD), bf16),
        ((256, 1024), f32),
        ((nz, 128, 1024), f32),
        ((nz, 128, 1024), bf16),
        ((nz, 128, 1024), bf16),
        ((nz - 1, 128, 1024), bf16),
    ]
    copies = 12 + 1 + nz - 1
    square = lambda a: a.reshape(1024, 1024)
    return call(
        kernel_three, 2, outs, scratch, copies, "feed_forward",
        tokens, y, square(wo), square(up), square(dn), cots.reshape(4 * tok, 1024), gains,
    )


def kernel_four(
    table_ref, decay_ref, seg_ref, q_ref, kvx, dy_ref, lse_ref, state_ref,
    base_ref, outp_ref, ymix_ref, da_ref, gupo_ref, gupg_ref,
    dqkv_ref, out_ref, gout_ref, gup_ref, small_ref,
    near, far, decay, enter, leave, rows, cols, dqs, dks, dvs, local, sent, got, halo_out, halo_in,
    diag, below, rest, sums, outin, ocore, oown, ogiven, ohead, ohin, ozin, ucore, uz, usum, tile,
    send_sems, recv_sems,
):
    me = Place()
    nz = me.nz
    tok = base_ref.shape[0]
    peers = [me.head_dev(k) for k in range(3)]
    greet(
        peers
        + [me.z_dev(k) for k in range(1, nz)]
        + [me.core_dev(), me.seq_dev(1), me.seq_dev(2)]
    )
    sends = Sends(send_sems, recv_sems)
    up = Reduce(me, sends, gupo_ref, gupg_ref, ucore, uz)
    up.start()
    outs = [sends.put(outp_ref.at[k], outin.at[k], peers[k]) for k in range(3)]
    segs = Segs(me, seg_ref, rows, cols)
    fill_tables(table_ref, decay_ref, near, far, decay, enter, leave)
    sums[...] = jnp.zeros_like(sums)
    dks[...] = jnp.zeros_like(dks)
    dvs[...] = jnp.zeros_like(dvs)
    diag[...] = jnp.zeros_like(diag)
    below[...] = jnp.zeros_like(below)
    rest[...] = jnp.zeros_like(rest)
    falls = [power(decay_ref[0, head], float(TILE)) for head in range(2)]
    for head in range(2):
        grad = jnp.zeros((HD, HD), f32)
        for t in range(3, -1, -1):
            at = pl.ds(t * TILE, TILE)
            query = (q_ref[head, at].astype(f32) * (enter[head] * segs.live(t))).astype(bf16)
            add = t_dot(query, dy_ref[head, at])
            local[4 * head + t] = add
            grad = falls[head] * segs.keep[t] * grad + add
        sent[head] = grad.astype(bf16)
    carry = [sends.put(sent, got.at[k - 1], me.seq_dev(-k)) for k in (1, 2)]

    def out_tile(j, _):
        tile[...] = t_dot(ymix_ref[:, part(j, 256)], da_ref[...])
        for z in range(nz):
            oown[j, part(z, 32)] = tile[part(2 * z + me.core, 32)]
            ogiven[j, part(z, 32)] = tile[part(2 * z + 1 - me.core, 32)].astype(bf16)
        return 0

    lax.fori_loop(0, 4, out_tile, 0)
    o_core = sends.put(ogiven, ocore, me.core_dev())
    up.along()
    gap = (grid_of(0) - grid_of(1)).astype(f32)

    def tiles(index, base):
        head, t = index // 2, base + index % 2
        at, wide = part(t, TILE), pl.ds(pl.multiple_of(t * TILE, TILE), 3 * TILE)
        query, dy = q_ref[head, at], dy_ref[head, at]
        keys, values = kvx[head, wide], kvx[2 + head, wide]
        raw = dot_t(query, keys)
        s0, s1, s2, same = tile_scores(raw, head, t, table_ref, near, far, segs)
        lse = lse_ref[4 * head + t]
        p0, p1, p2 = jnp.exp2(s0 - lse), jnp.exp2(s1 - lse), jnp.exp2(s2 - lse)
        dp = dot_t(dy, values)
        dp0, dp1, dp2 = dp[:, :TILE], dp[:, TILE : 2 * TILE], dp[:, 2 * TILE :]
        mean = (p0 * dp0 + p1 * dp1 + p2 * dp2).sum(axis=1, keepdims=True)
        d0, d1, d2 = p0 * (dp0 - mean), p1 * (dp1 - mean), p2 * (dp2 - mean)
        diag[head] += d2[:HD, :HD] + d2[HD:, HD:]
        below[head] += d2[HD:, :HD] + d1[:HD, HD:]
        rest[head] += (
            (d0[:, :HD] + d0[:, HD:]).sum(axis=0, keepdims=True)
            + d1[:, :HD].sum(axis=0, keepdims=True)
            + d1[HD:, HD:].sum(axis=0, keepdims=True)
        )
        weight = jnp.where(same, decay[head], 0.0)
        mixed = weight * raw[:, 2 * TILE :]
        turn = weight * dp2
        slope = mixed * dp2 * gap
        sums[head] -= (slope[:, :HD] + slope[:, HD:]).sum(axis=0, keepdims=True)
        scale = 1.0 / math.sqrt(HD)
        x = jnp.concatenate(
            [(d0 * scale).astype(bf16), (d1 * scale).astype(bf16), (d2 * scale + turn).astype(bf16)],
            axis=1,
        )
        p = jnp.concatenate([p0.astype(bf16), p1.astype(bf16), (p2 + mixed).astype(bf16)], axis=1)
        dqs[head, at] = dot(x, keys)
        dks[head, wide] += t_dot(x, query)
        dvs[head, wide] += t_dot(p, dy)
        return base

    lax.fori_loop(0, 4, tiles, 0)
    for head in range(2):
        halo_out[head] = dks[head, : 2 * TILE].astype(bf16)
        halo_out[2 + head] = dvs[head, : 2 * TILE].astype(bf16)
    halo = sends.put(halo_out, halo_in, me.seq_dev(-1))
    o_core.wait_recv()
    o_core.wait_send()
    sends.all = [c for c in sends.all if c is not o_core]
    o_head = []
    for k in range(3):
        to = me.heads[k]
        ohead[k] = (oown[to] + ocore[to].astype(f32)).astype(bf16)
        o_head.append(sends.put(ohead.at[k], ohin.at[k], peers[k]))
    lax.fori_loop(0, 4, tiles, 2)
    for copy in outs:
        copy.wait_recv()
    out_ref[...] = (
        base_ref[...] + outin[0].astype(f32) + outin[1].astype(f32) + outin[2].astype(f32)
    ).astype(bf16)
    for copy in o_head:
        copy.wait_recv()
    o_sum = oown[me.h] + ocore[me.h].astype(f32)
    for k in range(3):
        o_sum = o_sum + ohin[k].astype(f32)
    tile[0:128] = o_sum
    ogiven[0] = o_sum.astype(bf16)
    o_z = []
    for k in range(1, nz):
        src = ogiven.at[0, part((me.z + k) % nz, 32)]
        o_z.append(sends.put(src, ozin.at[k - 1], me.z_dev(k)))
    for copy in carry:
        copy.wait_recv()
    place = grid_of(0, (TILE, 1)).astype(f32)
    halo.wait_recv()
    for head in range(2):
        rate = decay_ref[0, head]
        past = power(rate, 4.0 * TILE) * segs.keep_after
        grad = got[0, head].astype(f32) + past * got[1, head].astype(f32)
        fall = falls[head]
        total = jnp.zeros((1, HD), f32)
        for t in range(3, -1, -1):
            at = pl.ds(t * TILE, TILE)
            ext = pl.ds((t + 2) * TILE, TILE)
            low = grad.astype(bf16)
            state = state_ref[4 * head + t]
            give = leave[head] * segs.kept(t)
            take = enter[head] * segs.live(t)
            query, key, value = q_ref[head, at], kvx[head, ext], kvx[2 + head, ext]
            dq = dot_t(dy_ref[head, at], state.astype(bf16)) * take
            dv = dot(key, low) * give
            dk = dot_t(value, low) * give + dks[head, ext]
            slope = dq * query.astype(f32) * (place + 1.0)
            slope = slope + dv * value.astype(f32) * (TILE - 1.0 - place)
            crossing = fall * segs.keep[t]
            total = total - slope.sum(axis=0, keepdims=True)
            total = total - TILE * crossing * (grad * state).sum(axis=0, keepdims=True)
            dv = dv + dvs[head, ext]
            if t >= 2:
                back = pl.ds((t - 2) * TILE, TILE)
                dk = dk + halo_in[head, back].astype(f32)
                dv = dv + halo_in[2 + head, back].astype(f32)
            dqkv_ref[head, at] = (dqs[head, at] + dq).astype(bf16)
            dqkv_ref[2 + head, at] = dk.astype(bf16)
            dqkv_ref[4 + head, at] = dv.astype(bf16)
            grad = local[4 * head + t] + crossing * grad
        sums[head] += total
    gap_near = grid_of(0, (HD, HD)) - grid_of(1, (HD, HD))
    gap_far = gap_near + HD
    table = []
    for head in range(2):
        last = rest[head]
        for b in range(BUCKETS):
            up_to = STARTS[b + 1] if b + 1 < BUCKETS else 2 * WIN
            inside = lambda g: (g >= STARTS[b]) & (g < up_to)
            total = jnp.where(inside(gap_near), diag[head], 0.0)
            total = total + jnp.where(inside(gap_far), below[head], 0.0)
            total = total.sum(axis=0, keepdims=True)
            table.append(total + last if b == BUCKETS - 1 else total)
    table += [sums[0], sums[1], jnp.zeros((HD - 2 * BUCKETS - 2, HD), f32)]
    small_ref[...] = lax.dot_general(
        jnp.ones((8, HD), f32), jnp.concatenate(table, axis=0), (((1,), (1,)), ((), ())),
        precision=lax.Precision.HIGHEST, preferred_element_type=f32,
    )
    usum[...] = up.total()
    width = usum.shape[1]
    ups = []
    for k in range(3):
        src = usum.at[part(me.heads[k], 32)]
        ups.append(sends.put(src, gup_ref.at[:, part(me.h, width)], peers[k]))
    gup_ref[:, part(me.h, width)] = usum[part(me.h, 32)]
    total = tile[part(me.z, 32)]
    for k in range(nz - 1):
        o_z[k].wait_recv()
        total = total + ozin[k].astype(f32)
    gout_ref[...] = total
    for copy in ups:
        copy.wait_recv()
    sends.finish()


def stage_four(table, decay, segments, qkv, kvx, dy, lse, states, base, outp, ymix, da, gupo, gupg):
    nz = lax.axis_size("seq") // 2
    tok = base.shape[0]
    outs = [
        ((6, 4 * tok, HD), bf16),
        ((tok, 1024), bf16),
        ((32, 1024), f32),
        ((32, 4096), f32),
        ((8, HD), f32),
    ]
    scratch = [
        ((2, TILE, TILE), f32),
        ((2, TILE, TILE), f32),
        ((2, TILE, TILE), f32),
        ((2, TILE, 1), f32),
        ((2, TILE, 1), f32),
        ((6, 1, TILE), f32),
        ((4, TILE, 1), f32),
        ((2, 4 * TILE, HD), f32),
        ((2, 6 * TILE, HD), f32),
        ((2, 6 * TILE, HD), f32),
        ((8, HD, HD), f32),
        ((2, HD, HD), bf16),
        ((2, 2, HD, HD), bf16),
        ((4, 2 * TILE, HD), bf16),
        ((4, 2 * TILE, HD), bf16),
        ((2, HD, HD), f32),
        ((2, HD, HD), f32),
        ((2, 1, HD), f32),
        ((2, 1, HD), f32),
        ((3, tok, 1024), bf16),
        ((4, 128, 1024), bf16),
        ((4, 128, 1024), f32),
        ((4, 128, 1024), bf16),
        ((3, 128, 1024), bf16),
        ((3, 128, 1024), bf16),
        ((nz - 1, 32, 1024), bf16),
        ((nz, 128, 1024), bf16),
        ((nz - 1, 128, 1024), bf16),
        ((128, 1024), f32),
        ((256, 1024), f32),
    ]
    copies = 1 + 3 + 2 + 1 + (nz - 1) + 1 + 3 + (nz - 1) + 3
    return call(
        kernel_four, 3, outs, scratch, copies, "attention_backward",
        table, decay.reshape(1, 2), segments.reshape(-1, TILE), qkv[0:2], kvx, dy, lse, states,
        base, outp, ymix, da, gupo, gupg, scalars=2,
    )


def kernel_five(
    dqkv_ref, hall_ref, w_ref, gains_ref, tok_ref, dx1_ref, gnorm_ref, small_ref,
    in_ref, gq_ref, gk_ref, gv_ref, norms_ref, sums_ref,
    dall, dsend, din, own_dn, gown, ggiven, gcore, gz, gsum, gin, tile, nsend, ncore, nz_in, nhead,
    send_sems, recv_sems,
):
    me = Place()
    nz = me.nz
    tok = tok_ref.shape[0]
    peers = [me.head_dev(k) for k in range(3)]
    greet(peers + [me.z_dev(k) for k in range(1, nz)] + [me.core_dev()])
    sends = Sends(send_sems, recv_sems)
    for j in range(6):
        dall[:, j * HD : j * HD + HD] = dqkv_ref[j]
    wide = 6 * HD
    backs = []
    for k in range(3):
        rows = part(me.heads[k], tok)

        def back(j, _):
            dsend[k, :, part(j, 256)] = dot_t(dall[rows], w_ref[part(j, 256), 0:wide]).astype(bf16)
            return 0

        lax.fori_loop(0, 4, back, 0)
        backs.append(sends.put(dsend.at[k], din.at[k], peers[k]))

    def grad_tile(j, _):
        tile[...] = t_dot(hall_ref[:, part(j, 256)], dall[...])
        for z in range(nz):
            gown[z, part(j, 32)] = tile[part(2 * z + me.core, 32)]
            ggiven[z, part(j, 32)] = tile[part(2 * z + 1 - me.core, 32)].astype(bf16)
        return 0

    lax.fori_loop(0, 4, grad_tile, 0)
    grads = Reduce(me, sends, gown, ggiven, gcore, gz)
    grads.start()

    def own(j, _):
        own_dn[:, part(j, 256)] = dot_t(dall[part(me.h, tok)], w_ref[part(j, 256), 0:wide])
        return 0

    lax.fori_loop(0, 4, own, 0)
    grads.along()
    gain = gains_ref[0:1]
    x = tok_ref[...].astype(f32)
    scale = rms(x)
    n1 = x * scale
    for copy in backs:
        copy.wait_recv()
    dn1 = own_dn[...] + din[0].astype(f32) + din[1].astype(f32) + din[2].astype(f32)
    nsend[...] = jnp.zeros_like(nsend)
    nsend[0:1] = jnp.sum(dn1 * n1, axis=0, keepdims=True)
    nsend[1:2] = gnorm_ref[0:1]
    nsend[2:3, 0:HD] = small_ref[0:1]
    n_core = sends.put(nsend, ncore, me.core_dev())
    dn1 = dn1 * gain
    dx = dx1_ref[...] + scale * (dn1 - n1 * jnp.mean(dn1 * n1, axis=-1, keepdims=True))
    in_ref[...] = dx.astype(bf16)
    n_core.wait_recv()
    n_core.wait_send()
    sends.all = [c for c in sends.all if c is not n_core]
    nsend[...] = nsend[...] + ncore[...]
    n_z = [sends.put(nsend, nz_in.at[k - 1], me.z_dev(k)) for k in range(1, nz)]
    gsum[...] = grads.total()
    g_head = []
    for k in range(3):
        src = gsum.at[part(me.heads[k], 32)]
        g_head.append(sends.put(src, gin.at[me.h], peers[k]))
    gin[me.h] = gsum[part(me.h, 32)]
    total = nsend[...]
    for k in range(nz - 1):
        n_z[k].wait_recv()
        total = total + nz_in[k]
    ncore[...] = total
    n_head = [sends.put(ncore, nhead.at[k], peers[k]) for k in range(3)]
    sums_ref[...] = total[:, 0:HD]
    for copy in g_head:
        copy.wait_recv()
    for h in range(4):
        for out, at in ((gq_ref, 0), (gk_ref, 1), (gv_ref, 2)):
            out[:, h * 256 : h * 256 + 256] = gin[h, :, at * 256 : at * 256 + 256]
    for copy in n_head:
        copy.wait_recv()
    norms_ref[...] = ncore[...] + nhead[0] + nhead[1] + nhead[2]
    sends.finish()


def stage_five(dqkv, hall, wb, gains, tokens, dx1, gnorm, small):
    nz = lax.axis_size("seq") // 2
    tok = tokens.shape[0]
    wide = 6 * HD
    outs = [
        ((tok, 1024), bf16),
        ((32, 1024), f32),
        ((32, 1024), f32),
        ((32, 1024), f32),
        ((8, 1024), f32),
        ((8, HD), f32),
    ]
    scratch = [
        ((4 * tok, wide), bf16),
        ((3, tok, 1024), bf16),
        ((3, tok, 1024), bf16),
        ((tok, 1024), f32),
        ((nz, 128, wide), f32),
        ((nz, 128, wide), bf16),
        ((nz, 128, wide), bf16),
        ((nz - 1, 128, wide), bf16),
        ((128, wide), f32),
        ((4, 32, wide), f32),
        ((256, wide), f32),
        ((8, 1024), f32),
        ((8, 1024), f32),
        ((nz - 1, 8, 1024), f32),
        ((3, 8, 1024), f32),
    ]
    copies = 3 + 1 + (nz - 1) + 1 + (nz - 1) + 3 + 3
    return call(
        kernel_five, 4, outs, scratch, copies, "input_gradient",
        dqkv, hall, wb.reshape(1024, 896), gains, tokens, dx1, gnorm, small,
    )


def shards(
    tokens, cotangent, segments, w_query, w_key, w_value, w_out, w_up, w_down,
    norm_one, norm_two, rel_table, decay_rate,
):
    hall, qkv, wb, woz, gains = stage_one(
        tokens, w_query, w_key, w_value, w_out, norm_one, norm_two
    )
    y, lse, states, kvx, cots, up, dn, wo = stage_two(
        rel_table, decay_rate, segments, qkv, w_up, w_down, cotangent, woz
    )
    base, outp, ymix, da, dx1, dyh, grad_down, gupo, gupg, gnorm = stage_three(
        tokens, y, wo, up, dn, cots, gains
    )
    dqkv, output, grad_out, grad_up, small = stage_four(
        rel_table, decay_rate, segments, qkv, kvx, dyh, lse, states, base, outp, ymix, da, gupo, gupg
    )
    input_grad, grad_query, grad_key, grad_value, norms, sums = stage_five(
        dqkv, hall, wb, gains, tokens, dx1, gnorm, small
    )
    rows = w_query.shape[0]
    at = lax.axis_index("head") * 256 + lax.axis_index("seq") * rows
    mine = lax.dynamic_slice(norms, (0, at), (2, rows))
    sums = sums[2]
    return (
        output, input_grad, grad_query, grad_key, grad_value, grad_out, grad_up, grad_down,
        mine[0], mine[1], sums[: 2 * BUCKETS].reshape(2, BUCKETS), sums[2 * BUCKETS : 2 * BUCKETS + 2],
    )


highest = lax.Precision.HIGHEST


def from_behind(value, axis, by):
    size = lax.axis_size(axis)
    pairs = [(i, i + by) for i in range(size) if 0 <= i + by < size]
    return lax.ppermute(value, axis, pairs)


def prefix(value, axis, join, neutral, backward):
    count = lax.axis_size(axis)
    place = lax.axis_index(axis)
    ahead = count - 1 - place if backward else place
    gathered = jax.tree.map(
        lambda a, kind: lax.all_gather(a.astype(kind), axis), value, (jnp.bfloat16, jnp.bfloat16)
    )
    state = jax.tree.map(lambda a, e: jnp.zeros_like(a) + jnp.asarray(e, a.dtype), value, neutral)

    def one(lap, state):
        source = count - 1 - lap if backward else lap
        return join(
            state,
            jax.tree.map(
                lambda a, own: lax.dynamic_index_in_dim(a, source, 0, False).astype(own.dtype),
                gathered,
                value,
            ),
        )

    return lax.fori_loop(0, ahead, one, state)


def bucket_onehot(window_len, bucket_count):
    distance = np.arange(window_len)
    scaled = np.floor(np.log(np.maximum(distance, 1) / 16.0) / np.log(8.0) * 16.0)
    larger = np.minimum(16 + np.maximum(scaled, 0), bucket_count - 1)
    bucket = np.where(distance < 16, distance, larger).astype(np.int32)
    return (bucket[:, None] == np.arange(bucket_count)[None, :]).astype(np.float32)


def skewed(extended, row_count, col_count):
    head_count = extended.shape[0]
    span = row_count + col_count
    flipped = jnp.concatenate(
        [extended[:, ::-1], jnp.zeros((head_count, 1), extended.dtype)], axis=1
    )
    tiled = jnp.broadcast_to(flipped[:, None, :], (head_count, row_count, span)).reshape(
        head_count, row_count * span
    )
    tiled = tiled[:, : row_count * (span - 1)].reshape(head_count, row_count, span - 1)
    return tiled[:, :, row_count - 1 : row_count - 1 + col_count]


def rms_scale(values, gain):
    return values * lax.rsqrt(jnp.mean(values * values, axis=-1, keepdims=True) + epsilon) * gain


def times_transposed(left, right):
    return lax.dot_general(
        left, right, (((1,), (1,)), ((), ())), preferred_element_type=jnp.float32
    )


def transposed_times(left, right):
    return lax.dot_general(
        left, right, (((0,), (0,)), ((), ())), preferred_element_type=jnp.float32
    )


def compose(earlier, later):
    return (earlier[0] * later[0], later[0][:, None, None] * earlier[1] + later[1])


def group_state(carried_state, query_c, key_c, value_c, seg_group, seg_before, decay_rate):
    length_c = query_c.shape[0]
    position = jnp.arange(length_c).astype(jnp.float32)
    distance = position[:, None] - position[None, :]
    inside = (distance >= 0) & (seg_group[:, None] == seg_group[None, :])
    decay_w = jnp.where(
        inside[None], jnp.exp(-decay_rate[:, None, None] * jnp.maximum(distance, 0.0)[None]), 0.0
    )
    affinity = jnp.einsum("ihd,jhd->hij", query_c, key_c, precision=highest) * state_scale
    readout = jnp.einsum("hij,jhd->ihd", affinity * decay_w, value_c, precision=highest)
    live_mask = (seg_group == seg_before).astype(jnp.float32)
    entering = (
        jnp.exp(-decay_rate[None, :] * (position[:, None] + 1.0)) * live_mask[:, None] * state_scale
    )
    readout = (
        readout
        + jnp.einsum("ihd,hde->ihe", query_c, carried_state, precision=highest)
        * entering[:, :, None]
    )
    keeping = (seg_group == seg_group[-1]).astype(jnp.float32)
    leaving = (
        jnp.exp(-decay_rate[None, :] * (length_c - 1.0 - position[:, None])) * keeping[:, None]
    )
    carry_keep = jnp.exp(-decay_rate * length_c) * (seg_group[-1] == seg_before).astype(jnp.float32)
    updated = jnp.einsum("jhd,jhe->hde", key_c * leaving[:, :, None], value_c, precision=highest)
    updated = updated + carry_keep[:, None, None] * carried_state
    return (updated, readout)


def local_states(query_f, key_f, value_f, decay_rate, seg_block, seg_before):
    block_len, head_count, head_width = query_f.shape
    count = block_len // WIN
    items = (
        query_f.reshape(count, WIN, head_count, head_width),
        key_f.reshape(count, WIN, head_count, head_width),
        value_f.reshape(count, WIN, head_count, head_width),
        seg_block.reshape(count, WIN),
    )

    def step(carry, item):
        carried_state, prior = carry
        updated, readout = group_state(
            carried_state, item[0], item[1], item[2], item[3], prior, decay_rate
        )
        return ((updated, item[3][-1]), readout)

    start_carry = (jnp.zeros((head_count, head_width, head_width), jnp.float32), seg_before)
    (final_state, _), readouts = lax.scan(step, start_carry, items)
    return (readouts.reshape(block_len, head_count, head_width), final_state)


def general_shards(
    tokens,
    cotangent,
    segments,
    w_query,
    w_key,
    w_value,
    w_out,
    w_up,
    w_down,
    norm_one,
    norm_two,
    rel_table,
    decay_rate,
):
    heads_here = rel_table.shape[0]
    head_width = HD
    tok_here = tokens.shape[0]
    block_len = lax.axis_size("head") * tok_here
    block_count = block_len // WIN
    pair_width = heads_here * head_width
    scale = 1.0 / math.sqrt(head_width)
    gathered = (
        lax.all_gather(w_query, ("head", "seq"), axis=0, tiled=True),
        lax.all_gather(w_key, ("head", "seq"), axis=0, tiled=True),
        lax.all_gather(w_value, ("head", "seq"), axis=0, tiled=True),
        lax.all_gather(w_out, ("head", "seq"), axis=0, tiled=True),
        lax.all_gather(w_up, ("head", "seq"), axis=0, tiled=True),
        lax.all_gather(w_down, ("head", "seq"), axis=0, tiled=True),
        lax.all_gather(norm_one, ("head", "seq"), axis=0, tiled=True),
        lax.all_gather(norm_two, ("head", "seq"), axis=0, tiled=True),
    )
    full_query, full_key, full_value, full_out, full_up, full_down, gain_one, gain_two = gathered
    inputs_f = tokens.astype(jnp.float32)
    scaled_one, norm_back_one = jax.vjp(rms_scale, inputs_f, gain_one.astype(jnp.float32))
    normed = scaled_one.astype(jnp.bfloat16)
    projected = jnp.stack(
        [
            jnp.dot(normed, full_query, preferred_element_type=jnp.float32),
            jnp.dot(normed, full_key, preferred_element_type=jnp.float32),
            jnp.dot(normed, full_value, preferred_element_type=jnp.float32),
        ]
    ).astype(jnp.bfloat16)
    regrouped = lax.all_to_all(projected, "head", split_axis=2, concat_axis=1, tiled=True)
    prior_pairs = from_behind(regrouped[1:, block_len - WIN :], "seq", 1)
    pairs_ext = jnp.concatenate([prior_pairs, regrouped[1:]], axis=1)
    query_heads = regrouped[0].reshape(block_len, heads_here, head_width)
    key_ext = pairs_ext[0].reshape(block_len + WIN, heads_here, head_width)
    value_ext = pairs_ext[1].reshape(block_len + WIN, heads_here, head_width)
    block_base = lax.axis_index("seq") * block_len
    padded_segs = jnp.concatenate([jnp.full((WIN,), -1, jnp.int32), segments])
    seg_ext = lax.dynamic_slice_in_dim(padded_segs, block_base, block_len + WIN, 0)
    seg_block = seg_ext[WIN:]
    seg_before = seg_ext[WIN - 1]
    onehot_table = jnp.asarray(bucket_onehot(WIN, BUCKETS))
    by_distance = jnp.dot(rel_table, onehot_table.T, precision=highest)
    bias_ext = jnp.concatenate(
        [
            jnp.zeros((heads_here, WIN - 1), jnp.float32),
            by_distance,
            jnp.zeros((heads_here, WIN), jnp.float32),
        ],
        axis=1,
    )
    bias_full, skew_back = jax.vjp(lambda extended: skewed(extended, WIN, 2 * WIN), bias_ext)
    row_pos = jnp.arange(WIN, dtype=jnp.int32)[:, None]
    col_pos = jnp.arange(2 * WIN, dtype=jnp.int32)[None, :]
    near = (row_pos - col_pos + WIN >= 0) & (row_pos - col_pos + WIN < WIN)

    def block_inputs(number):
        start = number * WIN
        query_b = lax.dynamic_slice_in_dim(query_heads, start, WIN, 0)
        key_b = lax.dynamic_slice_in_dim(key_ext, start, 2 * WIN, 0)
        value_b = lax.dynamic_slice_in_dim(value_ext, start, 2 * WIN, 0)
        seg_q = lax.dynamic_slice_in_dim(seg_block, start, WIN, 0)
        seg_k = lax.dynamic_slice_in_dim(seg_ext, start, 2 * WIN, 0)
        visible = near & (seg_q[:, None] == seg_k[None, :])
        raw = jnp.einsum("ihd,jhd->hij", query_b, key_b, preferred_element_type=jnp.float32) * scale
        scores = jnp.where(visible[None], raw + bias_full, negative)
        return (query_b, key_b, value_b, scores)

    def forward_block(number):
        query_b, key_b, value_b, scores = block_inputs(number)
        top_score = jnp.max(scores, axis=-1, keepdims=True)
        exp_scores = jnp.exp(scores - top_score)
        total_mass = jnp.sum(exp_scores, axis=-1, keepdims=True)
        softmax_w = exp_scores / total_mass
        attended_b = jnp.einsum(
            "hij,jhd->ihd",
            softmax_w.astype(jnp.bfloat16),
            value_b,
            preferred_element_type=jnp.float32,
        )
        return (attended_b, (top_score + jnp.log(total_mass))[..., 0])

    numbers = jnp.arange(block_count, dtype=jnp.int32)
    attended_blocks, log_mass = lax.map(forward_block, numbers)
    attended = attended_blocks.reshape(block_len, heads_here, head_width)
    query_f = query_heads.astype(jnp.float32)
    key_f = key_ext[WIN:].astype(jnp.float32)
    value_f = value_ext[WIN:].astype(jnp.float32)

    def states_here(query_a, key_a, value_a, rates):
        return local_states(query_a, key_a, value_a, rates, seg_block, seg_before)

    (readout_local, state_local), states_back = jax.vjp(
        states_here, query_f, key_f, value_f, decay_rate
    )
    position = jnp.arange(block_len).astype(jnp.float32)
    live_mask = (seg_block == seg_before).astype(jnp.float32)
    enter_decay = (
        jnp.exp(-decay_rate[None, :] * (position[:, None] + 1.0)) * live_mask[:, None] * state_scale
    )
    carry_keep = jnp.exp(-decay_rate * block_len) * (seg_block[-1] == seg_before).astype(
        jnp.float32
    )
    identity = (jnp.ones_like(carry_keep), jnp.zeros_like(state_local))
    carried = prefix((carry_keep, state_local), "seq", compose, identity, False)
    carry_in = carried[1]
    carry_term = (
        jnp.einsum("ihd,hde->ihe", query_f, carry_in, precision=highest) * enter_decay[:, :, None]
    )
    mixed_heads = (
        (attended + readout_local + carry_term).astype(jnp.bfloat16).reshape(block_len, pair_width)
    )
    mixed_tok = lax.all_to_all(mixed_heads, "head", split_axis=0, concat_axis=1, tiled=True)
    resid_one = inputs_f + jnp.dot(mixed_tok, full_out, preferred_element_type=jnp.float32)
    scaled_two, norm_back_two = jax.vjp(rms_scale, resid_one, gain_two.astype(jnp.float32))
    normed_two = scaled_two.astype(jnp.bfloat16)
    up_proj = jnp.dot(normed_two, full_up, preferred_element_type=jnp.float32)
    activated, gelu_back = jax.vjp(jax.nn.gelu, up_proj)
    act_low = activated.astype(jnp.bfloat16)
    output = (resid_one + jnp.dot(act_low, full_down, preferred_element_type=jnp.float32)).astype(
        jnp.bfloat16
    )
    back_query, back_key, back_value = (full_query, full_key, full_value)
    back_out, back_up, back_down = (full_out, full_up, full_down)
    grad_down_w = transposed_times(act_low, cotangent)
    act_grad = times_transposed(cotangent, back_down)
    up_grad = gelu_back(act_grad)[0].astype(jnp.bfloat16)
    grad_up_w = transposed_times(normed_two, up_grad)
    normed_two_grad = times_transposed(up_grad, back_up)
    resid_grad_n, grad_gain_two = norm_back_two(normed_two_grad)
    resid_grad = cotangent.astype(jnp.float32) + resid_grad_n
    attn_grad = resid_grad.astype(jnp.bfloat16)
    grad_out_w = transposed_times(mixed_tok, attn_grad)
    mixed_grad = times_transposed(attn_grad, back_out).astype(jnp.bfloat16)
    heads_grad = lax.all_to_all(mixed_grad, "head", split_axis=1, concat_axis=0, tiled=True)
    heads_grad3 = heads_grad.reshape(block_len, heads_here, head_width)

    def backward_block(item):
        number, log_block = item
        query_b, key_b, value_b, scores = block_inputs(number)
        out_grad_b = lax.dynamic_slice_in_dim(heads_grad3, number * WIN, WIN, 0)
        softmax_w = jnp.exp(scores - log_block[..., None])
        prob_grad = jnp.einsum(
            "ihd,jhd->hij", out_grad_b, value_b, preferred_element_type=jnp.float32
        )
        score_grad = softmax_w * (
            prob_grad - jnp.sum(softmax_w * prob_grad, axis=-1, keepdims=True)
        )
        score_low = score_grad.astype(jnp.bfloat16)
        query_grad_b = (
            jnp.einsum("hij,jhd->ihd", score_low, key_b, preferred_element_type=jnp.float32) * scale
        )
        key_grad_b = (
            jnp.einsum("hij,ihd->jhd", score_low, query_b, preferred_element_type=jnp.float32)
            * scale
        )
        value_grad_b = jnp.einsum(
            "hij,ihd->jhd",
            softmax_w.astype(jnp.bfloat16),
            out_grad_b,
            preferred_element_type=jnp.float32,
        )
        ext_grad_b = skew_back(score_low.astype(jnp.float32))[0]
        return (query_grad_b, key_grad_b, value_grad_b, ext_grad_b)

    query_grads, key_grads, value_grads, ext_grads = lax.map(backward_block, (numbers, log_mass))
    query_grad_att = query_grads.reshape(block_len, heads_here, head_width)

    def fold_pairs(pieces):
        zero_edge = jnp.zeros_like(pieces[:1, :WIN])
        return jnp.concatenate([pieces[:, :WIN], zero_edge], axis=0) + jnp.concatenate(
            [zero_edge, pieces[:, WIN:]], axis=0
        )

    key_folded = fold_pairs(key_grads)
    value_folded = fold_pairs(value_grads)
    sent_pairs = jnp.stack([key_folded[0], value_folded[0]]).reshape(2, WIN, pair_width)
    received = from_behind(sent_pairs.astype(jnp.bfloat16), "seq", -1).astype(sent_pairs.dtype)
    tail_pairs = jnp.concatenate(
        [jnp.zeros((2, block_len - WIN, pair_width), jnp.float32), received], axis=1
    )
    tail_pairs = tail_pairs.reshape(2, block_len, heads_here, head_width)
    key_grad_att = key_folded[1:].reshape(block_len, heads_here, head_width) + tail_pairs[0]
    value_grad_att = value_folded[1:].reshape(block_len, heads_here, head_width) + tail_pairs[1]
    heads_grad_f = heads_grad3.astype(jnp.float32)
    grad_local = jnp.einsum(
        "ihd,ihe->hde", query_f * enter_decay[:, :, None], heads_grad_f, precision=highest
    )
    back_chain = prefix((carry_keep, grad_local), "seq", compose, identity, True)
    carry_out_grad = back_chain[1]
    query_grad_s, key_grad_s, value_grad_s, rate_grad_s = states_back(
        (heads_grad_f, carry_out_grad)
    )
    query_grad_c = (
        jnp.einsum("ihe,hde->ihd", heads_grad_f, carry_in, precision=highest)
        * enter_decay[:, :, None]
    )
    rate_grad_c = -jnp.sum(heads_grad_f * carry_term * (position[:, None, None] + 1.0), axis=(0, 2))
    rate_grad_a = -block_len * carry_keep * jnp.sum(carry_out_grad * carry_in, axis=(1, 2))
    rate_grad = rate_grad_s + rate_grad_c + rate_grad_a
    query_grad = query_grad_att + query_grad_s + query_grad_c
    key_grad = key_grad_att + key_grad_s
    value_grad = value_grad_att + value_grad_s
    triple_grad = (
        jnp.stack([query_grad, key_grad, value_grad])
        .reshape(3, block_len, pair_width)
        .astype(jnp.bfloat16)
    )
    token_grads = lax.all_to_all(triple_grad, "head", split_axis=1, concat_axis=2, tiled=True)
    grad_query_w = transposed_times(normed, token_grads[0])
    grad_key_w = transposed_times(normed, token_grads[1])
    grad_value_w = transposed_times(normed, token_grads[2])
    normed_grad = (
        times_transposed(token_grads[0], back_query)
        + times_transposed(token_grads[1], back_key)
        + times_transposed(token_grads[2], back_value)
    )
    input_grad_n, grad_gain_one = norm_back_one(normed_grad)
    input_grad = (resid_grad + input_grad_n).astype(jnp.bfloat16)
    ext_total = jnp.sum(ext_grads, axis=0)
    table_grad = jnp.dot(ext_total[:, WIN - 1 : 2 * WIN - 1], onehot_table, precision=highest)
    table_grad, rate_grad = lax.psum((table_grad, rate_grad), "seq")
    summed = (
        lax.psum_scatter(grad_query_w, ("head", "seq"), scatter_dimension=0, tiled=True),
        lax.psum_scatter(grad_key_w, ("head", "seq"), scatter_dimension=0, tiled=True),
        lax.psum_scatter(grad_value_w, ("head", "seq"), scatter_dimension=0, tiled=True),
        lax.psum_scatter(grad_out_w, ("head", "seq"), scatter_dimension=0, tiled=True),
        lax.psum_scatter(grad_up_w, ("head", "seq"), scatter_dimension=0, tiled=True),
        lax.psum_scatter(grad_down_w, ("head", "seq"), scatter_dimension=0, tiled=True),
        lax.psum_scatter(grad_gain_one, ("head", "seq"), scatter_dimension=0, tiled=True),
        lax.psum_scatter(grad_gain_two, ("head", "seq"), scatter_dimension=0, tiled=True),
    )
    grad_query, grad_key, grad_value, grad_out, grad_up, grad_down, grad_norm_one, grad_norm_two = (
        summed
    )
    return (
        output,
        input_grad,
        grad_query,
        grad_key,
        grad_value,
        grad_out,
        grad_up,
        grad_down,
        grad_norm_one,
        grad_norm_two,
        table_grad,
        rate_grad,
    )


def solution(mesh):
    devices = mesh.shape["head"] * mesh.shape["seq"]
    tiled = mesh.shape["head"] == 4 and 1024 // devices == 32
    return jax.shard_map(
        shards if tiled else general_shards,
        mesh=mesh,
        in_specs=(
            P(("seq", "head"), None),
            P(("seq", "head"), None),
            P(),
            P(("head", "seq"), None),
            P(("head", "seq"), None),
            P(("head", "seq"), None),
            P(("head", "seq"), None),
            P(("head", "seq"), None),
            P(("head", "seq"), None),
            P(("head", "seq")),
            P(("head", "seq")),
            P("head", None),
            P("head"),
        ),
        out_specs=(
            P(("seq", "head"), None),
            P(("seq", "head"), None),
            P(("head", "seq"), None),
            P(("head", "seq"), None),
            P(("head", "seq"), None),
            P(("head", "seq"), None),
            P(("head", "seq"), None),
            P(("head", "seq"), None),
            P(("head", "seq")),
            P(("head", "seq")),
            P("head", None),
            P("head"),
        ),
        check_vma=False,
    )
```

```python
import functools
import math

import jax
import jax.numpy as jnp
import numpy as np
from jax import lax
from jax.experimental import pallas as pl
from jax.experimental.pallas import tpu as pltpu
from jax.sharding import PartitionSpec as P

HD = 128
BUCKETS = 32
WIN = 512
TILE = 256

epsilon = 1e-06
negative = -1e30
state_scale = 1.0 / 1024.0
MESH = pl.DeviceIdType.MESH
f32 = jnp.float32
bf16 = jnp.bfloat16


def dot(a, b):
    return jnp.dot(a, b, preferred_element_type=f32)


def dot_t(a, b):
    return lax.dot_general(a, b, (((1,), (1,)), ((), ())), preferred_element_type=f32)


def t_dot(a, b):
    return lax.dot_general(a, b, (((0,), (0,)), ((), ())), preferred_element_type=f32)


class Place:
    def __init__(self):
        self.h = lax.axis_index("head")
        self.s = lax.axis_index("seq")
        self.n = lax.axis_size("seq")
        self.nz = self.n // 2
        self.z = self.s // 2
        self.core = self.s % 2
        x, y = self.h % 2, self.h // 2
        self.heads = [2 * y + 1 - x, 2 * (1 - y) + x, 2 * (1 - y) + 1 - x]

    def head_dev(self, k):
        return (self.heads[k], self.s)

    def z_to(self, k):
        return ((self.z + k) % self.nz) * 2 + self.core

    def z_from(self, k):
        return ((self.z + self.nz - k) % self.nz) * 2 + self.core

    def z_dev(self, k):
        return (self.h, self.z_to(k))

    def other(self):
        return self.z * 2 + 1 - self.core

    def core_dev(self):
        return (self.h, self.other())

    def seq_dev(self, by):
        return (self.h, (self.s + self.n + by) % self.n)


def greet(devices):
    barrier = pltpu.get_barrier_semaphore()
    for device in devices:
        pl.semaphore_signal(barrier, inc=1, device_id=device, device_id_type=MESH)
    pl.semaphore_wait(barrier, len(devices))


class Sends:
    def __init__(self, send_sems, recv_sems):
        self.send_sems, self.recv_sems = send_sems, recv_sems
        self.at, self.all = 0, []

    def put(self, src, dst, device, start=True):
        copy = pltpu.make_async_remote_copy(
            src_ref=src,
            dst_ref=dst,
            send_sem=self.send_sems.at[self.at],
            recv_sem=self.recv_sems.at[self.at],
            device_id=device,
            device_id_type=MESH,
        )
        self.at += 1
        self.all.append(copy)
        if start:
            copy.start()
        return copy

    def sent(self, copy):
        copy.wait_send()
        self.all = [c for c in self.all if c is not copy]

    def finish(self):
        for copy in self.all:
            copy.wait_send()


def rms(x):
    return lax.rsqrt(jnp.mean(x * x, axis=-1, keepdims=True) + epsilon)


LOG2E = math.log2(math.e)
KEY_SCALE = LOG2E / math.sqrt(HD)


def bucket_starts():
    distance = np.arange(WIN)
    scaled = np.floor(np.log(np.maximum(distance, 1) / 16.0) / np.log(8.0) * 16.0)
    larger = np.minimum(16 + np.maximum(scaled, 0), BUCKETS - 1)
    bucket = np.where(distance < 16, distance, larger).astype(np.int32)
    return [int(np.argmax(bucket == b)) for b in range(BUCKETS)]


STARTS = bucket_starts()


def grid_of(axis, shape=(TILE, TILE)):
    return lax.broadcasted_iota(jnp.int32, shape, axis)


def column(row):
    eye = grid_of(0) == grid_of(1)
    return jnp.sum(jnp.where(eye, row, 0.0), axis=1, keepdims=True)


class Segs:
    def __init__(self, me, seg_ref, rows, cols):
        total = 4 * me.n
        self.rows, self.cols = rows, cols

        def row_at(offset):
            at = 2 * ((4 * me.s + total + offset) % total)
            pair = [seg_ref[pl.ds(at + i, 1)].astype(f32) for i in range(2)]
            return jnp.concatenate(pair, axis=1)

        for j in range(6):
            row = row_at(j - 2)
            rows[j] = row
            if j >= 2:
                cols[j - 2] = column(row)
        last = lambda offset: row_at(offset)[:, TILE - 1 : TILE]
        self.last = [last(j - 2) for j in range(6)]
        same = lambda a, b: (a == b).astype(f32)
        self.keep = [same(self.last[t + 2], self.last[t + 1]) for t in range(4)]
        self.keep_before = same(last(-1), last(-5))
        self.keep_after = same(last(7), last(3))

    def live(self, t):
        return (self.cols[t] == self.last[t + 1]).astype(f32)

    def kept(self, t):
        return (self.cols[t] == self.last[t + 2]).astype(f32)


def fill_tables(table_ref, decay_ref, near, far, decay, enter, leave):
    gap = grid_of(0) - grid_of(1)
    place = grid_of(0, (TILE, 1)).astype(f32)
    for head in range(2):
        rate = decay_ref[0, head]
        for out, shift in ((near, 0), (far, TILE)):
            bias = jnp.full((TILE, TILE), table_ref[head, 0] * LOG2E, f32)
            for b in range(1, BUCKETS):
                bias = jnp.where(gap + shift >= STARTS[b], table_ref[head, b] * LOG2E, bias)
            out[head] = jnp.where(gap + shift >= 0, bias, negative)
        fall = jnp.exp(-rate * jnp.maximum(gap, 0).astype(f32)) * state_scale
        decay[head] = jnp.where(gap >= 0, fall, 0.0)
        enter[head] = jnp.exp(-rate * (place + 1.0)) * state_scale
        leave[head] = jnp.exp(-rate * (TILE - 1.0 - place))


def power(rate, steps):
    return jnp.exp(jnp.full((1, HD), -rate * steps, f32))


def tile_scores(raw, head, t, table_ref, near, far, segs):
    col = segs.cols[t]
    same = [col == segs.rows[t + j] for j in range(3)]
    reach = grid_of(0) < grid_of(1)
    rest = table_ref[head, BUCKETS - 1] * LOG2E
    s0 = jnp.where(same[0] & reach, raw[:, :TILE] * KEY_SCALE + rest, negative)
    s1 = jnp.where(same[1], raw[:, TILE : 2 * TILE] * KEY_SCALE + far[head], negative)
    s2 = jnp.where(same[2], raw[:, 2 * TILE :] * KEY_SCALE + near[head], negative)
    return s0, s1, s2, same[2]


GELU_C = math.sqrt(2.0 / math.pi)
GELU_A = 0.044715


def part(i, size):
    return pl.ds(pl.multiple_of(i * size, size), size)


class Reduce:
    def __init__(self, me, sends, own, given, core_in, z_in, keep):
        self.me, self.sends = me, sends
        self.own, self.given, self.core_in, self.z_in, self.keep = own, given, core_in, z_in, keep
        self.width = keep.shape[-1]

    def start(self):
        self.core = self.sends.put(self.given, self.core_in, self.me.core_dev())

    def along(self):
        me, lanes = self.me, pl.ds(0, self.width)
        self.core.wait_recv()
        self.sends.sent(self.core)
        self.copies = []
        for k in range(1, me.nz):
            to = (me.z + k) % me.nz

            def both(i, at):
                both = self.own[to, at, lanes] + self.core_in[to, at].astype(f32)
                self.given[to, at] = both.astype(bf16)

            each(128, 32, both)
            self.copies.append(
                self.sends.put(self.given.at[to], self.z_in.at[k - 1], me.z_dev(k))
            )

        def mine(i, at):
            self.keep[at] = self.own[me.z, at, lanes] + self.core_in[me.z, at].astype(f32)

        each(128, 32, mine)

    def total(self):
        for copy in self.copies:
            copy.wait_recv()

        def more(i, at):
            self.keep[at] += sum(self.z_in[k, at].astype(f32) for k in range(self.me.nz - 1))

        each(128, 32, more)


def each(count, step, body):
    def one(i, _):
        body(i, part(i, step))
        return 0

    lax.fori_loop(0, count // step, one, 0)


def whole_kernel(ins, outs, b, send_sems, recv_sems):
    me = Place()
    nz, n = me.nz, me.n
    rows, tok = ins.w_out.shape[0], ins.tokens.shape[0]
    peers = [me.head_dev(k) for k in range(3)]
    greet(
        peers
        + [me.z_dev(k) for k in range(1, nz)]
        + [me.core_dev()]
        + [me.seq_dev(k) for k in (1, 2, -1, -2)]
    )
    sends = Sends(send_sems, recv_sems)
    core_dev = me.core_dev()
    half = pl.ds(me.core * nz, nz)
    wide = 6 * HD

    lane = lax.broadcasted_iota(jnp.int32, (rows, 128), 1)
    line = lax.broadcasted_iota(jnp.int32, (rows, 128), 0)
    group = 128 // rows
    gains = jnp.zeros((rows, 128), f32)
    for j, gain in enumerate((ins.norm_one, ins.norm_two)):
        row = jnp.concatenate([gain[...].astype(f32)] * group, axis=1)
        gains = jnp.where((lane // rows == me.s % group) & (line == j), row, gains)
    b.gains[...] = gains.astype(bf16)
    first, first_up, toks = [], [], []
    parts = (ins.w_query, ins.w_key, ins.w_value)
    for k in range(3):
        for j, w in enumerate(parts):
            src = w.at[:, part(me.heads[k], 256)]
            first.append(sends.put(src, b.a1.at[me.h, :, j * 256 : j * 256 + 256], peers[k]))
        first.append(sends.put(b.gains, b.a1.at[me.h, :, wide:], peers[k]))
    for k in range(3):
        own = b.x.at[part(me.h, tok)]
        toks.append(sends.put(ins.tokens, own, peers[k]))
    for k in range(3):
        src = ins.w_up.at[:, part(me.heads[k], 1024)]
        first_up.append(sends.put(src, b.u1.at[me.h], peers[k]))
    for j, w in enumerate(parts):
        b.a1[me.h, :, j * 256 : j * 256 + 256] = w[:, part(me.h, 256)]
    b.a1[me.h, :, wide:] = b.gains[...]
    b.x[part(me.h, tok)] = ins.tokens[...]
    b.u1[me.h] = ins.w_up[:, part(me.h, 1024)]
    b.wo[me.h, me.s] = ins.w_out[...]
    b.dn[me.s] = ins.w_down[...]
    b.cots[part(me.h, tok)] = ins.cotangent[...]
    for copy in first:
        copy.wait_recv()
    w_z = [sends.put(b.a1, b.wb.at[:, me.s], me.z_dev(k)) for k in range(1, nz)]
    w_c = [sends.put(b.a1, b.wb.at[:, me.s], core_dev)]
    b.wb[:, me.s] = b.a1[...]
    own = b.wo.at[me.h, me.s]
    wo_z = [sends.put(ins.w_out, own, me.z_dev(k)) for k in range(1, nz)]
    wo_c = [sends.put(ins.w_out, own, core_dev)]
    segs = Segs(me, ins.segments, b.rows, b.cols)
    fill_tables(ins.table, ins.decay, b.near, b.far, b.decay, b.enter, b.leave)
    for k in range(1, nz):
        w_z[k - 1].wait_recv()
        piece = b.wb.at[:, me.z_from(k)]
        w_c.append(sends.put(piece, piece, core_dev))
    for copy in first_up:
        copy.wait_recv()
    up_z = [sends.put(b.u1, b.up.at[:, me.s], me.z_dev(k)) for k in range(1, nz)]
    up_c = [sends.put(b.u1, b.up.at[:, me.s], core_dev)]
    b.up[:, me.s] = b.u1[...]
    dn_z = [sends.put(ins.w_down, b.dn.at[me.s], me.z_dev(k)) for k in range(1, nz)]
    dn_c = [sends.put(ins.w_down, b.dn.at[me.s], core_dev)]
    for copy in w_c:
        copy.wait_recv()
    lanes = []
    for h in range(4):
        for s in range(0, n, group):
            lanes.append(sum(b.wb[h, s + i, :, wide:].astype(f32) for i in range(group)))
    gains = jnp.concatenate(lanes, axis=1)
    gain_one, gain_two = gains[0:1], gains[1:2]
    for copy in toks:
        copy.wait_recv()

    def norm_one(i, at):
        x = b.x[at].astype(f32)
        b.hall[at] = (x * rms(x) * gain_one).astype(bf16)

    each(4 * tok, 32, norm_one)

    def project(t, _):
        at = part(t, tok)
        for j in range(3):
            w = b.wb[:, :, :, j * 256 : j * 256 + 256].reshape(1024, 256)
            out = dot(b.hall[at], w).astype(bf16)
            for head in range(2):
                mine = out[:, head * HD : head * HD + HD]
                if j == 0:
                    b.q[head, at] = mine
                else:
                    b.kvx[2 * (j - 1) + head, part(t + 2, tok)] = mine
        return 0

    lax.fori_loop(0, 4, project, 0)
    halo = sends.put(b.kvx.at[:, 4 * TILE :], b.kvx.at[:, : 2 * TILE], me.seq_dev(1))

    falls = [power(ins.decay[0, head], float(TILE)) for head in range(2)]
    for head in range(2):
        state = jnp.zeros((HD, HD), f32)
        for t in range(4):
            at = pl.ds((t + 2) * TILE, TILE)
            key = (b.kvx[head, at].astype(f32) * (b.leave[head] * segs.kept(t))).astype(bf16)
            add = t_dot(key, b.kvx[2 + head, at])
            b.local[4 * head + t] = add
            state = falls[head] * segs.keep[t] * state + add
        b.sent[head] = state.astype(bf16)
    carry = [sends.put(b.sent, b.got.at[k - 1], me.seq_dev(k)) for k in (1, 2)]
    for k in range(1, nz):
        wo_z[k - 1].wait_recv()
        piece = b.wo.at[me.h, me.z_from(k)]
        wo_c.append(sends.put(piece, piece, core_dev))
    for copy in wo_c:
        copy.wait_recv()
    own = b.wo.at[me.h, half]
    wo_h = [sends.put(own, own, peers[k]) for k in range(3)]
    own = b.cots.at[part(me.h, tok)]
    cots = [sends.put(ins.cotangent, own, peers[k]) for k in range(3)]

    def forward(index, base):
        head, t = index // 2, base + index % 2
        at, own = part(t, TILE), part(t + 2, TILE)
        wide = pl.ds(pl.multiple_of(t * TILE, TILE), 3 * TILE)
        raw = dot_t(b.q[head, at], b.kvx[head, wide])
        s0, s1, s2, same = tile_scores(raw, head, t, ins.table, b.near, b.far, segs)
        top = jnp.maximum(jnp.maximum(s0, s1), s2).max(axis=1, keepdims=True)
        e0, e1, e2 = jnp.exp2(s0 - top), jnp.exp2(s1 - top), jnp.exp2(s2 - top)
        mass = (e0 + e1 + e2).sum(axis=1, keepdims=True)
        b.lse[4 * head + t] = top + jnp.log2(mass)
        mix = jnp.concatenate([e0.astype(bf16), e1.astype(bf16), e2.astype(bf16)], axis=1)
        att = dot(mix, b.kvx[2 + head, wide]) / mass
        weight = jnp.where(same, raw[:, 2 * TILE :] * b.decay[head], 0.0).astype(bf16)
        b.acc[head, at] = att + dot(weight, b.kvx[2 + head, own])
        return base

    lax.fori_loop(0, 4, forward, 2)
    halo.wait_recv()
    lax.fori_loop(0, 4, forward, 0)
    for copy in wo_h:
        copy.wait_recv()
    for k in range(3):
        piece = b.wo.at[me.heads[k], half]
        wo_c.append(sends.put(piece, piece, core_dev))
    for copy in carry:
        copy.wait_recv()
    for head in range(2):
        past = power(ins.decay[0, head], 4.0 * TILE) * segs.keep_before
        state = b.got[0, head].astype(f32) + past * b.got[1, head].astype(f32)
        for t in range(4):
            at = pl.ds(t * TILE, TILE)
            b.state[4 * head + t] = state
            reach = b.enter[head] * segs.live(t)
            y = b.acc[head, at] + dot(b.q[head, at], state.astype(bf16)) * reach
            b.dyt[2 * t + head] = y.astype(bf16)
            state = falls[head] * segs.keep[t] * state + b.local[4 * head + t]
    ys = []
    for k in range(3):
        for head in range(2):
            src = b.dyt.at[2 * me.heads[k] + head]
            ys.append(sends.put(src, b.ymix.at[:, part(2 * me.h + head, HD)], peers[k]))
    for head in range(2):
        b.ymix[:, part(2 * me.h + head, HD)] = b.dyt[2 * me.h + head]
    for k in range(1, nz):
        up_z[k - 1].wait_recv()
        piece = b.up.at[:, me.z_from(k)]
        up_c.append(sends.put(piece, piece, core_dev))
    for copy in ys + wo_c[-3:]:
        copy.wait_recv()

    def out_tile(j, _):
        cols = part(j, 256)
        w = b.wo[:, :, :, cols].reshape(1024, 256)
        b.x1[:, cols] = ins.tokens[:, cols].astype(f32) + dot(b.ymix[...], w)
        return 0

    lax.fori_loop(0, 4, out_tile, 0)
    def norm_two(i, at):
        x = b.x1[at]
        b.h2all[pl.ds(pl.multiple_of(me.h * tok + i * 32, 32), 32)] = (x * rms(x) * gain_two).astype(bf16)
        b.base[at] = x

    each(tok, 32, norm_two)
    own = b.h2all.at[part(me.h, tok)]
    h2s = [sends.put(own, own, peers[k]) for k in range(3)]
    for k in range(1, nz):
        dn_z[k - 1].wait_recv()
        piece = b.dn.at[me.z_from(k)]
        dn_c.append(sends.put(piece, piece, core_dev))
    for copy in up_c + dn_c + cots:
        copy.wait_recv()
    dn2_copies = []
    for k in range(-1, 3):
        at = part(me.h if k < 0 else me.heads[k], tok)
        if k >= 0:
            h2s[k].wait_recv()

        def hidden(j, _):
            cols = part(j, 256)
            u = dot(b.h2all[at], b.up[:, :, :, cols].reshape(1024, 256))
            dg = dot_t(b.cots[at], b.dn[pl.ds(2 * j, 2)].reshape(256, 1024))
            uu = u * u
            t = jnp.tanh(GELU_C * u * (1.0 + GELU_A * uu))
            b.x[at, cols] = (0.5 * u * (1.0 + t)).astype(bf16)
            slope = 0.5 * (1.0 + t) + (0.5 * GELU_C) * u * (1.0 - t * t) * (1.0 + 3.0 * GELU_A * uu)
            b.du[at, cols] = (slope * dg).astype(bf16)
            return 0

        lax.fori_loop(0, 4, hidden, 0)

        def back(j, _):
            w = b.up[j].reshape(256, 1024)
            b.dn2s[k + 1, :, part(j, 256)] = dot_t(b.du[at], w).astype(bf16)
            return 0

        lax.fori_loop(0, 4, back, 0)
        if k >= 0:
            dn2_copies.append(sends.put(b.dn2s.at[k + 1], b.dnin.at[k], peers[k]))

        def ahead(j, _):
            cols = part(j, 256)
            out = dot(b.x[at], b.dn[:, :, cols].reshape(1024, 256))
            if k < 0:
                b.base[:, cols] = b.base[:, cols] + out
            else:
                b.outp[k, :, cols] = out.astype(bf16)
            return 0

        lax.fori_loop(0, 4, ahead, 0)

    def down_tile(j, _):
        b.tile[...] = t_dot(b.x[:, part(j, 256)], b.cots[...])
        b.own[j] = b.tile[part(me.core, 128)]
        b.given_a[j] = b.tile[part(1 - me.core, 128)].astype(bf16)
        return 0

    lax.fori_loop(0, 4, down_tile, 0)
    down = Reduce(me, sends, b.own, b.given_a, b.core_a, b.z_a, outs.grad_down)
    down.start()

    for copy in dn2_copies:
        copy.wait_recv()
    b.norms[...] = jnp.zeros_like(b.norms)

    def second_norm_back(i, at):
        dn2 = b.dn2s[0, at].astype(f32) + sum(b.dnin[k, at].astype(f32) for k in range(3))
        x = b.x1[at]
        scale = rms(x)
        n2 = x * scale
        b.norms[1:2] += jnp.sum(dn2 * n2, axis=0, keepdims=True)
        spread = dn2 * gain_two
        dx1 = ins.cotangent[at].astype(f32) + scale * (
            spread - n2 * jnp.mean(spread * n2, axis=-1, keepdims=True)
        )
        b.x1[at] = dx1
        b.da[at] = dx1.astype(bf16)

    each(tok, 32, second_norm_back)
    for copy in ys + dn2_copies + dn_c[1:]:
        sends.sent(copy)

    def back_tile(j, _):
        out = dot_t(b.da[...], b.wo[j].reshape(256, 1024)).astype(bf16)
        b.dyt[2 * j] = out[:, :HD]
        b.dyt[2 * j + 1] = out[:, HD:]
        return 0

    lax.fori_loop(0, 4, back_tile, 0)
    dys = []
    for k in range(3):
        src = b.dyt.at[pl.ds(2 * me.heads[k], 2)]
        dys.append(sends.put(src, b.dyh.at[:, part(me.h, tok)], peers[k]))
    b.dyh[:, part(me.h, tok)] = b.dyt[pl.ds(2 * me.h, 2)]
    down.along()

    def up_tile(j, _):
        b.tile[...] = t_dot(b.h2all[:, part(j, 256)], b.du[...])
        for z in range(nz):
            b.own[z, part(j, 32)] = b.tile[part(2 * z + me.core, 32)]
            b.given_b[z, part(j, 32)] = b.tile[part(2 * z + 1 - me.core, 32)].astype(bf16)
        return 0

    lax.fori_loop(0, 4, up_tile, 0)
    up = Reduce(me, sends, b.own, b.given_b, b.core_b, b.z_b, b.up_sum)
    up.start()
    for copy in dys:
        copy.wait_recv()
    for zero in (b.sums, b.dks, b.dvs, b.diag, b.below, b.rest):
        zero[...] = jnp.zeros_like(zero)
    for head in range(2):
        grad = jnp.zeros((HD, HD), f32)
        for t in range(3, -1, -1):
            at = pl.ds(t * TILE, TILE)
            query = (b.q[head, at].astype(f32) * (b.enter[head] * segs.live(t))).astype(bf16)
            add = t_dot(query, b.dyh[head, at])
            b.local[4 * head + t] = add
            grad = falls[head] * segs.keep[t] * grad + add
        b.sent_back[head] = grad.astype(bf16)
    carry = [sends.put(b.sent_back, b.got_back.at[k - 1], me.seq_dev(-k)) for k in (1, 2)]
    up.along()

    def grad_out_tile(j, _):
        b.tile[...] = t_dot(b.ymix[:, part(j, 256)], b.da[...])
        for z in range(nz):
            b.own[j, part(z, 32)] = b.tile[part(2 * z + me.core, 32)]
            b.dn[j, part(z, 32)] = b.tile[part(2 * z + 1 - me.core, 32)].astype(bf16)
        return 0

    lax.fori_loop(0, 4, grad_out_tile, 0)
    o_core = sends.put(b.dn.at[0:4], b.core_o, core_dev)
    outp = [sends.put(b.outp.at[k], b.dnin.at[k], peers[k]) for k in range(3)]

    gap = (grid_of(0) - grid_of(1)).astype(f32)

    def backward(index, base):
        head, t = index // 2, base + index % 2
        at, wide = part(t, TILE), pl.ds(pl.multiple_of(t * TILE, TILE), 3 * TILE)
        query, dy = b.q[head, at], b.dyh[head, at]
        keys, values = b.kvx[head, wide], b.kvx[2 + head, wide]
        raw = dot_t(query, keys)
        s0, s1, s2, same = tile_scores(raw, head, t, ins.table, b.near, b.far, segs)
        lse = b.lse[4 * head + t]
        p0, p1, p2 = jnp.exp2(s0 - lse), jnp.exp2(s1 - lse), jnp.exp2(s2 - lse)
        dp = dot_t(dy, values)
        dp0, dp1, dp2 = dp[:, :TILE], dp[:, TILE : 2 * TILE], dp[:, 2 * TILE :]
        mean = (p0 * dp0 + p1 * dp1 + p2 * dp2).sum(axis=1, keepdims=True)
        d0, d1, d2 = p0 * (dp0 - mean), p1 * (dp1 - mean), p2 * (dp2 - mean)
        b.diag[head] += d2[:HD, :HD] + d2[HD:, HD:]
        b.below[head] += d2[HD:, :HD] + d1[:HD, HD:]
        b.rest[head] += (
            (d0[:, :HD] + d0[:, HD:]).sum(axis=0, keepdims=True)
            + d1[:, :HD].sum(axis=0, keepdims=True)
            + d1[HD:, HD:].sum(axis=0, keepdims=True)
        )
        weight = jnp.where(same, b.decay[head], 0.0)
        mixed = weight * raw[:, 2 * TILE :]
        turn = weight * dp2
        slope = mixed * dp2 * gap
        b.sums[head] -= (slope[:, :HD] + slope[:, HD:]).sum(axis=0, keepdims=True)
        scale = 1.0 / math.sqrt(HD)
        x = jnp.concatenate(
            [(d0 * scale).astype(bf16), (d1 * scale).astype(bf16), (d2 * scale + turn).astype(bf16)],
            axis=1,
        )
        p = jnp.concatenate([p0.astype(bf16), p1.astype(bf16), (p2 + mixed).astype(bf16)], axis=1)
        b.acc[head, at] = dot(x, keys)
        b.dks[head, wide] += t_dot(x, query)
        b.dvs[head, wide] += t_dot(p, dy)
        return base

    lax.fori_loop(0, 4, backward, 0)
    for copy in dys:
        sends.sent(copy)
    for head in range(2):
        for i in range(2):
            at = pl.ds(i * TILE, TILE)
            b.dyt[2 * head + i] = b.dks[head, at].astype(bf16)
            b.dyt[4 + 2 * head + i] = b.dvs[head, at].astype(bf16)
    halo = sends.put(b.dyt, b.halo_in, me.seq_dev(-1))
    o_core.wait_recv()
    for copy in down.copies:
        sends.sent(copy)
    o_head = []
    for k in range(3):
        to = me.heads[k]

        def chip_sum(i, at):
            both = b.own[to, at] + b.core_o[to, at].astype(f32)
            b.given_a[k, at] = both.astype(bf16)

        each(128, 32, chip_sum)
        o_head.append(sends.put(b.given_a.at[k], b.o_in.at[k], peers[k]))

    def keep(i, at):
        b.o_keep[at] = b.own[me.h, at] + b.core_o[me.h, at].astype(f32)

    each(128, 32, keep)
    lax.fori_loop(0, 4, backward, 2)
    for copy in carry:
        copy.wait_recv()
    place = grid_of(0, (TILE, 1)).astype(f32)
    halo.wait_recv()
    for head in range(2):
        past = power(ins.decay[0, head], 4.0 * TILE) * segs.keep_after
        grad = b.got_back[0, head].astype(f32) + past * b.got_back[1, head].astype(f32)
        fall = falls[head]
        total = jnp.zeros((1, HD), f32)
        for t in range(3, -1, -1):
            at = pl.ds(t * TILE, TILE)
            ext = pl.ds((t + 2) * TILE, TILE)
            low = grad.astype(bf16)
            state = b.state[4 * head + t]
            give = b.leave[head] * segs.kept(t)
            take = b.enter[head] * segs.live(t)
            query, key, value = b.q[head, at], b.kvx[head, ext], b.kvx[2 + head, ext]
            dq = dot_t(b.dyh[head, at], state.astype(bf16)) * take
            dv = dot(key, low) * give
            dk = dot_t(value, low) * give + b.dks[head, ext]
            slope = dq * query.astype(f32) * (place + 1.0)
            slope = slope + dv * value.astype(f32) * (TILE - 1.0 - place)
            crossing = fall * segs.keep[t]
            total = total - slope.sum(axis=0, keepdims=True)
            total = total - TILE * crossing * (grad * state).sum(axis=0, keepdims=True)
            dv = dv + b.dvs[head, ext]
            if t >= 2:
                dk = dk + b.halo_in[2 * head + t - 2].astype(f32)
                dv = dv + b.halo_in[4 + 2 * head + t - 2].astype(f32)
            for j, grads in enumerate((b.acc[head, at] + dq, dk, dv)):
                col = (2 * j + head) * HD
                b.x[at, col : col + HD] = grads.astype(bf16)
            grad = b.local[4 * head + t] + crossing * grad
        b.sums[head] += total

    backs = []
    for k in range(3):
        at, to = part(me.heads[k], tok), pl.ds(k * tok, tok)

        def spread_back(j, _):
            w = b.wb[j, :, :, 0:wide].reshape(256, wide)
            b.du[to, part(j, 256)] = dot_t(b.x[at, 0:wide], w).astype(bf16)
            return 0

        lax.fori_loop(0, 4, spread_back, 0)
        backs.append(sends.put(b.du.at[to], b.dn2s.at[k + 1], peers[k]))

    def grad_tile(j, _):
        tile = pl.ds(0, wide)
        b.tile[:, tile] = t_dot(b.hall[:, part(j, 256)], b.x[:, 0:wide])
        for z in range(nz):
            b.own[z, part(j, 32), tile] = b.tile[part(2 * z + me.core, 32), tile]
            b.dn[4 + z, part(j, 32), tile] = b.tile[part(2 * z + 1 - me.core, 32), tile].astype(bf16)
        return 0

    lax.fori_loop(0, 4, grad_tile, 0)
    grads = Reduce(me, sends, b.own, b.dn.at[4:8, :, 0:wide], b.core_q, b.z_q, b.q_sum)
    grads.start()
    for copy in outp:
        copy.wait_recv()

    def output(i, at):
        total = b.base[at] + sum(b.dnin[k, at].astype(f32) for k in range(3))
        outs.output[at] = total.astype(bf16)

    each(tok, 32, output)

    def own_back(j, _):
        w = b.wb[j, :, :, 0:wide].reshape(256, wide)
        b.base[:, part(j, 256)] = dot_t(b.x[part(me.h, tok), 0:wide], w)
        return 0

    lax.fori_loop(0, 4, own_back, 0)
    grads.along()
    for copy in o_head:
        copy.wait_recv()

    def grad_out_sum(i, at):
        total = b.o_keep[at] + sum(b.o_in[k, at].astype(f32) for k in range(3))
        b.o_keep[at] = total
        b.o_low[at] = total.astype(bf16)

    each(128, 32, grad_out_sum)
    o_z = []
    for k in range(1, nz):
        src = b.o_low.at[part((me.z + k) % nz, 32)]
        o_z.append(sends.put(src, b.o_z.at[k - 1], me.z_dev(k)))
    down.total()
    up.total()
    ups = []
    for k in range(3):
        src = b.up_sum.at[part(me.heads[k], 32)]
        ups.append(sends.put(src, outs.grad_up.at[:, part(me.h, 1024)], peers[k]))
    outs.grad_up[:, part(me.h, 1024)] = b.up_sum[part(me.h, 32)]
    gap_near = grid_of(0, (HD, HD)) - grid_of(1, (HD, HD))
    gap_far = gap_near + HD
    table = []
    for head in range(2):
        last = b.rest[head]
        for i in range(BUCKETS):
            up_to = STARTS[i + 1] if i + 1 < BUCKETS else 2 * WIN
            inside = lambda g: (g >= STARTS[i]) & (g < up_to)
            total = jnp.where(inside(gap_near), b.diag[head], 0.0)
            total = total + jnp.where(inside(gap_far), b.below[head], 0.0)
            total = total.sum(axis=0, keepdims=True)
            table.append(total + last if i == BUCKETS - 1 else total)
    table += [b.sums[0], b.sums[1], jnp.zeros((HD - 2 * BUCKETS - 2, HD), f32)]
    small = lax.dot_general(
        jnp.ones((8, HD), f32), jnp.concatenate(table, axis=0), (((1,), (1,)), ((), ())),
        precision=lax.Precision.HIGHEST, preferred_element_type=f32,
    )
    b.norms[2:3, 0:HD] = small[0:1]
    for copy in backs:
        copy.wait_recv()

    def first_norm_back(i, at):
        dn1 = b.base[at] + sum(b.dn2s[k + 1, at].astype(f32) for k in range(3))
        x = ins.tokens[at].astype(f32)
        scale = rms(x)
        n1 = x * scale
        b.norms[0:1] += jnp.sum(dn1 * n1, axis=0, keepdims=True)
        spread = dn1 * gain_one
        dx = b.x1[at] + scale * (spread - n1 * jnp.mean(spread * n1, axis=-1, keepdims=True))
        outs.input_grad[at] = dx.astype(bf16)

    each(tok, 32, first_norm_back)
    n_core = sends.put(b.norms, b.n_core, core_dev)
    n_core.wait_recv()
    b.n_chip[...] = b.norms[...] + b.n_core[...]
    n_z = [sends.put(b.n_chip, b.n_z.at[k - 1], me.z_dev(k)) for k in range(1, nz)]
    grads.total()
    g_head = []
    for k in range(3):
        src = b.q_sum.at[part(me.heads[k], 32)]
        g_head.append(sends.put(src, b.q_in.at[me.h], peers[k]))
    b.q_in[me.h] = b.q_sum[part(me.h, 32)]
    total = b.n_chip[...]
    for k in range(nz - 1):
        n_z[k].wait_recv()
        total = total + b.n_z[k]
    b.n_line[...] = total
    n_head = [sends.put(b.n_line, b.n_head.at[k], peers[k]) for k in range(3)]
    outs.sums[...] = total[:, 0:HD]
    total = b.o_keep[part(me.z, 32)]
    for k in range(nz - 1):
        o_z[k].wait_recv()
        total = total + b.o_z[k].astype(f32)
    outs.grad_out[...] = total
    for copy in g_head:
        copy.wait_recv()
    for h in range(4):
        for j, out in enumerate((outs.grad_query, outs.grad_key, outs.grad_value)):
            out[:, h * 256 : h * 256 + 256] = b.q_in[h, :, j * 256 : j * 256 + 256]
    for copy in n_head + ups:
        copy.wait_recv()
    outs.norms[...] = b.n_line[...] + sum(b.n_head[k] for k in range(3))
    sends.finish()


class Names:
    def __init__(self, names, values):
        self.__dict__.update(zip(names, values))


def shards(
    tokens, cotangent, segments, w_query, w_key, w_value, w_out, w_up, w_down,
    norm_one, norm_two, rel_table, decay_rate,
):
    n = lax.axis_size("seq")
    nz = n // 2
    tok, rows = tokens.shape[0], w_query.shape[0]
    block = 4 * tok
    wide = 6 * HD
    ins = dict(
        table=rel_table, decay=decay_rate.reshape(1, 2), segments=segments.reshape(-1, 128),
        tokens=tokens, cotangent=cotangent, w_query=w_query, w_key=w_key, w_value=w_value,
        w_out=w_out, w_up=w_up, w_down=w_down,
        norm_one=norm_one.reshape(1, rows), norm_two=norm_two.reshape(1, rows),
    )
    outs = dict(
        output=((tok, 1024), bf16), input_grad=((tok, 1024), bf16),
        grad_query=((rows, 1024), f32), grad_key=((rows, 1024), f32),
        grad_value=((rows, 1024), f32), grad_out=((rows, 1024), f32),
        grad_up=((rows, 4096), f32), grad_down=((128, 1024), f32),
        norms=((8, 1024), f32), sums=((8, HD), f32),
    )
    pieces = (4, n, rows, 1024)
    square = ((block, 1024), bf16)
    three = ((3, tok, 1024), bf16)
    tables = ((2, TILE, TILE), f32)
    column = ((2, TILE, 1), f32)
    heads = ((2, HD, HD), f32)
    four = ((nz, 128, 1024), bf16)
    room = dict(
        gains=((rows, 128), bf16), a1=((4, rows, wide + 128), bf16), u1=((4, rows, 1024), bf16),
        x=square, hall=square, wb=((4, n, rows, wide + 128), bf16), up=(pieces, bf16),
        dn=((n, 128, 1024), bf16), wo=(pieces, bf16), cots=square,
        q=((2, block, HD), bf16), kvx=((4, 6 * TILE, HD), bf16),
        near=tables, far=tables, decay=tables, enter=column, leave=column,
        rows=((6, 1, TILE), f32), cols=((4, TILE, 1), f32),
        acc=((2, block, HD), f32), local=((8, HD, HD), f32), state=((8, HD, HD), f32),
        lse=((8, TILE, 1), f32),
        sent=((2, HD, HD), bf16), got=((2, 2, HD, HD), bf16),
        sent_back=((2, HD, HD), bf16), got_back=((2, 2, HD, HD), bf16),
        ymix=((tok, 1024), bf16),
        x1=((tok, 1024), f32), base=((tok, 1024), f32), h2all=square, du=square,
        dn2s=((4, tok, 1024), bf16), dnin=three, outp=three,
        da=((tok, 1024), bf16), dyt=((8, tok, HD), bf16), dyh=((2, block, HD), bf16),
        tile=((256, 1024), f32), own=((nz, 128, 1024), f32), o_keep=((128, 1024), f32),
        given_a=four, core_a=four, z_a=((nz - 1, 128, 1024), bf16),
        given_b=four, core_b=four, z_b=((nz - 1, 128, 1024), bf16), up_sum=((128, 1024), f32),
        core_o=four, o_in=((3, 128, 1024), bf16), o_low=((128, 1024), bf16),
        o_z=((nz - 1, 32, 1024), bf16),
        core_q=((nz, 128, wide), bf16),
        z_q=((nz - 1, 128, wide), bf16), q_sum=((128, wide), f32), q_in=((4, 32, wide), f32),
        diag=heads, below=heads, rest=((2, 1, HD), f32), sums=((2, 1, HD), f32),
        dks=((2, 6 * TILE, HD), f32), dvs=((2, 6 * TILE, HD), f32),
        halo_in=((8, TILE, HD), bf16),
        norms=((8, 1024), f32), n_core=((8, 1024), f32), n_chip=((8, 1024), f32),
        n_z=((nz - 1, 8, 1024), f32), n_line=((8, 1024), f32), n_head=((3, 8, 1024), f32),
    )
    copies = 150

    def kernel(*refs):
        i, o = len(ins), len(ins) + len(outs)
        r = o + len(room)
        whole_kernel(Names(ins, refs[:i]), Names(outs, refs[i:o]), Names(room, refs[o:r]), *refs[r:])

    results = pl.pallas_call(
        kernel,
        out_shape=[jax.ShapeDtypeStruct(shape, kind) for shape, kind in outs.values()],
        in_specs=[pl.BlockSpec(memory_space=pltpu.SMEM)] * 2
        + [pl.BlockSpec(memory_space=pltpu.VMEM)] * (len(ins) - 2),
        out_specs=[pl.BlockSpec(memory_space=pltpu.VMEM)] * len(outs),
        scratch_shapes=[pltpu.VMEM(shape, kind) for shape, kind in room.values()]
        + [pltpu.SemaphoreType.DMA((copies,)), pltpu.SemaphoreType.DMA((copies,))],
        compiler_params=pltpu.CompilerParams(
            collective_id=0, has_side_effects=True, vmem_limit_bytes=63 << 20
        ),
        name="block_layer",
    )(*ins.values())
    r = Names(outs, results)
    at = lax.axis_index("head") * 256 + lax.axis_index("seq") * rows
    mine = lax.dynamic_slice(r.norms, (0, at), (2, rows))
    sums = r.sums[2]
    return (
        r.output, r.input_grad, r.grad_query, r.grad_key, r.grad_value, r.grad_out, r.grad_up,
        r.grad_down, mine[0], mine[1],
        sums[: 2 * BUCKETS].reshape(2, BUCKETS), sums[2 * BUCKETS : 2 * BUCKETS + 2],
    )


highest = lax.Precision.HIGHEST


def from_behind(value, axis, by):
    size = lax.axis_size(axis)
    pairs = [(i, i + by) for i in range(size) if 0 <= i + by < size]
    return lax.ppermute(value, axis, pairs)


def prefix(value, axis, join, neutral, backward):
    count = lax.axis_size(axis)
    place = lax.axis_index(axis)
    ahead = count - 1 - place if backward else place
    gathered = jax.tree.map(
        lambda a, kind: lax.all_gather(a.astype(kind), axis), value, (jnp.bfloat16, jnp.bfloat16)
    )
    state = jax.tree.map(lambda a, e: jnp.zeros_like(a) + jnp.asarray(e, a.dtype), value, neutral)

    def one(lap, state):
        source = count - 1 - lap if backward else lap
        return join(
            state,
            jax.tree.map(
                lambda a, own: lax.dynamic_index_in_dim(a, source, 0, False).astype(own.dtype),
                gathered,
                value,
            ),
        )

    return lax.fori_loop(0, ahead, one, state)


def bucket_onehot(window_len, bucket_count):
    distance = np.arange(window_len)
    scaled = np.floor(np.log(np.maximum(distance, 1) / 16.0) / np.log(8.0) * 16.0)
    larger = np.minimum(16 + np.maximum(scaled, 0), bucket_count - 1)
    bucket = np.where(distance < 16, distance, larger).astype(np.int32)
    return (bucket[:, None] == np.arange(bucket_count)[None, :]).astype(np.float32)


def skewed(extended, row_count, col_count):
    head_count = extended.shape[0]
    span = row_count + col_count
    flipped = jnp.concatenate(
        [extended[:, ::-1], jnp.zeros((head_count, 1), extended.dtype)], axis=1
    )
    tiled = jnp.broadcast_to(flipped[:, None, :], (head_count, row_count, span)).reshape(
        head_count, row_count * span
    )
    tiled = tiled[:, : row_count * (span - 1)].reshape(head_count, row_count, span - 1)
    return tiled[:, :, row_count - 1 : row_count - 1 + col_count]


def rms_scale(values, gain):
    return values * lax.rsqrt(jnp.mean(values * values, axis=-1, keepdims=True) + epsilon) * gain


def times_transposed(left, right):
    return lax.dot_general(
        left, right, (((1,), (1,)), ((), ())), preferred_element_type=jnp.float32
    )


def transposed_times(left, right):
    return lax.dot_general(
        left, right, (((0,), (0,)), ((), ())), preferred_element_type=jnp.float32
    )


def compose(earlier, later):
    return (earlier[0] * later[0], later[0][:, None, None] * earlier[1] + later[1])


def group_state(carried_state, query_c, key_c, value_c, seg_group, seg_before, decay_rate):
    length_c = query_c.shape[0]
    position = jnp.arange(length_c).astype(jnp.float32)
    distance = position[:, None] - position[None, :]
    inside = (distance >= 0) & (seg_group[:, None] == seg_group[None, :])
    decay_w = jnp.where(
        inside[None], jnp.exp(-decay_rate[:, None, None] * jnp.maximum(distance, 0.0)[None]), 0.0
    )
    affinity = jnp.einsum("ihd,jhd->hij", query_c, key_c, precision=highest) * state_scale
    readout = jnp.einsum("hij,jhd->ihd", affinity * decay_w, value_c, precision=highest)
    live_mask = (seg_group == seg_before).astype(jnp.float32)
    entering = (
        jnp.exp(-decay_rate[None, :] * (position[:, None] + 1.0)) * live_mask[:, None] * state_scale
    )
    readout = (
        readout
        + jnp.einsum("ihd,hde->ihe", query_c, carried_state, precision=highest)
        * entering[:, :, None]
    )
    keeping = (seg_group == seg_group[-1]).astype(jnp.float32)
    leaving = (
        jnp.exp(-decay_rate[None, :] * (length_c - 1.0 - position[:, None])) * keeping[:, None]
    )
    carry_keep = jnp.exp(-decay_rate * length_c) * (seg_group[-1] == seg_before).astype(jnp.float32)
    updated = jnp.einsum("jhd,jhe->hde", key_c * leaving[:, :, None], value_c, precision=highest)
    updated = updated + carry_keep[:, None, None] * carried_state
    return (updated, readout)


def local_states(query_f, key_f, value_f, decay_rate, seg_block, seg_before):
    block_len, head_count, head_width = query_f.shape
    count = block_len // WIN
    items = (
        query_f.reshape(count, WIN, head_count, head_width),
        key_f.reshape(count, WIN, head_count, head_width),
        value_f.reshape(count, WIN, head_count, head_width),
        seg_block.reshape(count, WIN),
    )

    def step(carry, item):
        carried_state, prior = carry
        updated, readout = group_state(
            carried_state, item[0], item[1], item[2], item[3], prior, decay_rate
        )
        return ((updated, item[3][-1]), readout)

    start_carry = (jnp.zeros((head_count, head_width, head_width), jnp.float32), seg_before)
    (final_state, _), readouts = lax.scan(step, start_carry, items)
    return (readouts.reshape(block_len, head_count, head_width), final_state)


def general_shards(
    tokens,
    cotangent,
    segments,
    w_query,
    w_key,
    w_value,
    w_out,
    w_up,
    w_down,
    norm_one,
    norm_two,
    rel_table,
    decay_rate,
):
    heads_here = rel_table.shape[0]
    head_width = HD
    tok_here = tokens.shape[0]
    block_len = lax.axis_size("head") * tok_here
    block_count = block_len // WIN
    pair_width = heads_here * head_width
    scale = 1.0 / math.sqrt(head_width)
    gathered = (
        lax.all_gather(w_query, ("head", "seq"), axis=0, tiled=True),
        lax.all_gather(w_key, ("head", "seq"), axis=0, tiled=True),
        lax.all_gather(w_value, ("head", "seq"), axis=0, tiled=True),
        lax.all_gather(w_out, ("head", "seq"), axis=0, tiled=True),
        lax.all_gather(w_up, ("head", "seq"), axis=0, tiled=True),
        lax.all_gather(w_down, ("head", "seq"), axis=0, tiled=True),
        lax.all_gather(norm_one, ("head", "seq"), axis=0, tiled=True),
        lax.all_gather(norm_two, ("head", "seq"), axis=0, tiled=True),
    )
    full_query, full_key, full_value, full_out, full_up, full_down, gain_one, gain_two = gathered
    inputs_f = tokens.astype(jnp.float32)
    scaled_one, norm_back_one = jax.vjp(rms_scale, inputs_f, gain_one.astype(jnp.float32))
    normed = scaled_one.astype(jnp.bfloat16)
    projected = jnp.stack(
        [
            jnp.dot(normed, full_query, preferred_element_type=jnp.float32),
            jnp.dot(normed, full_key, preferred_element_type=jnp.float32),
            jnp.dot(normed, full_value, preferred_element_type=jnp.float32),
        ]
    ).astype(jnp.bfloat16)
    regrouped = lax.all_to_all(projected, "head", split_axis=2, concat_axis=1, tiled=True)
    prior_pairs = from_behind(regrouped[1:, block_len - WIN :], "seq", 1)
    pairs_ext = jnp.concatenate([prior_pairs, regrouped[1:]], axis=1)
    query_heads = regrouped[0].reshape(block_len, heads_here, head_width)
    key_ext = pairs_ext[0].reshape(block_len + WIN, heads_here, head_width)
    value_ext = pairs_ext[1].reshape(block_len + WIN, heads_here, head_width)
    block_base = lax.axis_index("seq") * block_len
    padded_segs = jnp.concatenate([jnp.full((WIN,), -1, jnp.int32), segments])
    seg_ext = lax.dynamic_slice_in_dim(padded_segs, block_base, block_len + WIN, 0)
    seg_block = seg_ext[WIN:]
    seg_before = seg_ext[WIN - 1]
    onehot_table = jnp.asarray(bucket_onehot(WIN, BUCKETS))
    by_distance = jnp.dot(rel_table, onehot_table.T, precision=highest)
    bias_ext = jnp.concatenate(
        [
            jnp.zeros((heads_here, WIN - 1), jnp.float32),
            by_distance,
            jnp.zeros((heads_here, WIN), jnp.float32),
        ],
        axis=1,
    )
    bias_full, skew_back = jax.vjp(lambda extended: skewed(extended, WIN, 2 * WIN), bias_ext)
    row_pos = jnp.arange(WIN, dtype=jnp.int32)[:, None]
    col_pos = jnp.arange(2 * WIN, dtype=jnp.int32)[None, :]
    near = (row_pos - col_pos + WIN >= 0) & (row_pos - col_pos + WIN < WIN)

    def block_inputs(number):
        start = number * WIN
        query_b = lax.dynamic_slice_in_dim(query_heads, start, WIN, 0)
        key_b = lax.dynamic_slice_in_dim(key_ext, start, 2 * WIN, 0)
        value_b = lax.dynamic_slice_in_dim(value_ext, start, 2 * WIN, 0)
        seg_q = lax.dynamic_slice_in_dim(seg_block, start, WIN, 0)
        seg_k = lax.dynamic_slice_in_dim(seg_ext, start, 2 * WIN, 0)
        visible = near & (seg_q[:, None] == seg_k[None, :])
        raw = jnp.einsum("ihd,jhd->hij", query_b, key_b, preferred_element_type=jnp.float32) * scale
        scores = jnp.where(visible[None], raw + bias_full, negative)
        return (query_b, key_b, value_b, scores)

    def forward_block(number):
        query_b, key_b, value_b, scores = block_inputs(number)
        top_score = jnp.max(scores, axis=-1, keepdims=True)
        exp_scores = jnp.exp(scores - top_score)
        total_mass = jnp.sum(exp_scores, axis=-1, keepdims=True)
        softmax_w = exp_scores / total_mass
        attended_b = jnp.einsum(
            "hij,jhd->ihd",
            softmax_w.astype(jnp.bfloat16),
            value_b,
            preferred_element_type=jnp.float32,
        )
        return (attended_b, (top_score + jnp.log(total_mass))[..., 0])

    numbers = jnp.arange(block_count, dtype=jnp.int32)
    attended_blocks, log_mass = lax.map(forward_block, numbers)
    attended = attended_blocks.reshape(block_len, heads_here, head_width)
    query_f = query_heads.astype(jnp.float32)
    key_f = key_ext[WIN:].astype(jnp.float32)
    value_f = value_ext[WIN:].astype(jnp.float32)

    def states_here(query_a, key_a, value_a, rates):
        return local_states(query_a, key_a, value_a, rates, seg_block, seg_before)

    (readout_local, state_local), states_back = jax.vjp(
        states_here, query_f, key_f, value_f, decay_rate
    )
    position = jnp.arange(block_len).astype(jnp.float32)
    live_mask = (seg_block == seg_before).astype(jnp.float32)
    enter_decay = (
        jnp.exp(-decay_rate[None, :] * (position[:, None] + 1.0)) * live_mask[:, None] * state_scale
    )
    carry_keep = jnp.exp(-decay_rate * block_len) * (seg_block[-1] == seg_before).astype(
        jnp.float32
    )
    identity = (jnp.ones_like(carry_keep), jnp.zeros_like(state_local))
    carried = prefix((carry_keep, state_local), "seq", compose, identity, False)
    carry_in = carried[1]
    carry_term = (
        jnp.einsum("ihd,hde->ihe", query_f, carry_in, precision=highest) * enter_decay[:, :, None]
    )
    mixed_heads = (
        (attended + readout_local + carry_term).astype(jnp.bfloat16).reshape(block_len, pair_width)
    )
    mixed_tok = lax.all_to_all(mixed_heads, "head", split_axis=0, concat_axis=1, tiled=True)
    resid_one = inputs_f + jnp.dot(mixed_tok, full_out, preferred_element_type=jnp.float32)
    scaled_two, norm_back_two = jax.vjp(rms_scale, resid_one, gain_two.astype(jnp.float32))
    normed_two = scaled_two.astype(jnp.bfloat16)
    up_proj = jnp.dot(normed_two, full_up, preferred_element_type=jnp.float32)
    activated, gelu_back = jax.vjp(jax.nn.gelu, up_proj)
    act_low = activated.astype(jnp.bfloat16)
    output = (resid_one + jnp.dot(act_low, full_down, preferred_element_type=jnp.float32)).astype(
        jnp.bfloat16
    )
    back_query, back_key, back_value = (full_query, full_key, full_value)
    back_out, back_up, back_down = (full_out, full_up, full_down)
    grad_down_w = transposed_times(act_low, cotangent)
    act_grad = times_transposed(cotangent, back_down)
    up_grad = gelu_back(act_grad)[0].astype(jnp.bfloat16)
    grad_up_w = transposed_times(normed_two, up_grad)
    normed_two_grad = times_transposed(up_grad, back_up)
    resid_grad_n, grad_gain_two = norm_back_two(normed_two_grad)
    resid_grad = cotangent.astype(jnp.float32) + resid_grad_n
    attn_grad = resid_grad.astype(jnp.bfloat16)
    grad_out_w = transposed_times(mixed_tok, attn_grad)
    mixed_grad = times_transposed(attn_grad, back_out).astype(jnp.bfloat16)
    heads_grad = lax.all_to_all(mixed_grad, "head", split_axis=1, concat_axis=0, tiled=True)
    heads_grad3 = heads_grad.reshape(block_len, heads_here, head_width)

    def backward_block(item):
        number, log_block = item
        query_b, key_b, value_b, scores = block_inputs(number)
        out_grad_b = lax.dynamic_slice_in_dim(heads_grad3, number * WIN, WIN, 0)
        softmax_w = jnp.exp(scores - log_block[..., None])
        prob_grad = jnp.einsum(
            "ihd,jhd->hij", out_grad_b, value_b, preferred_element_type=jnp.float32
        )
        score_grad = softmax_w * (
            prob_grad - jnp.sum(softmax_w * prob_grad, axis=-1, keepdims=True)
        )
        score_low = score_grad.astype(jnp.bfloat16)
        query_grad_b = (
            jnp.einsum("hij,jhd->ihd", score_low, key_b, preferred_element_type=jnp.float32) * scale
        )
        key_grad_b = (
            jnp.einsum("hij,ihd->jhd", score_low, query_b, preferred_element_type=jnp.float32)
            * scale
        )
        value_grad_b = jnp.einsum(
            "hij,ihd->jhd",
            softmax_w.astype(jnp.bfloat16),
            out_grad_b,
            preferred_element_type=jnp.float32,
        )
        ext_grad_b = skew_back(score_low.astype(jnp.float32))[0]
        return (query_grad_b, key_grad_b, value_grad_b, ext_grad_b)

    query_grads, key_grads, value_grads, ext_grads = lax.map(backward_block, (numbers, log_mass))
    query_grad_att = query_grads.reshape(block_len, heads_here, head_width)

    def fold_pairs(pieces):
        zero_edge = jnp.zeros_like(pieces[:1, :WIN])
        return jnp.concatenate([pieces[:, :WIN], zero_edge], axis=0) + jnp.concatenate(
            [zero_edge, pieces[:, WIN:]], axis=0
        )

    key_folded = fold_pairs(key_grads)
    value_folded = fold_pairs(value_grads)
    sent_pairs = jnp.stack([key_folded[0], value_folded[0]]).reshape(2, WIN, pair_width)
    received = from_behind(sent_pairs.astype(jnp.bfloat16), "seq", -1).astype(sent_pairs.dtype)
    tail_pairs = jnp.concatenate(
        [jnp.zeros((2, block_len - WIN, pair_width), jnp.float32), received], axis=1
    )
    tail_pairs = tail_pairs.reshape(2, block_len, heads_here, head_width)
    key_grad_att = key_folded[1:].reshape(block_len, heads_here, head_width) + tail_pairs[0]
    value_grad_att = value_folded[1:].reshape(block_len, heads_here, head_width) + tail_pairs[1]
    heads_grad_f = heads_grad3.astype(jnp.float32)
    grad_local = jnp.einsum(
        "ihd,ihe->hde", query_f * enter_decay[:, :, None], heads_grad_f, precision=highest
    )
    back_chain = prefix((carry_keep, grad_local), "seq", compose, identity, True)
    carry_out_grad = back_chain[1]
    query_grad_s, key_grad_s, value_grad_s, rate_grad_s = states_back(
        (heads_grad_f, carry_out_grad)
    )
    query_grad_c = (
        jnp.einsum("ihe,hde->ihd", heads_grad_f, carry_in, precision=highest)
        * enter_decay[:, :, None]
    )
    rate_grad_c = -jnp.sum(heads_grad_f * carry_term * (position[:, None, None] + 1.0), axis=(0, 2))
    rate_grad_a = -block_len * carry_keep * jnp.sum(carry_out_grad * carry_in, axis=(1, 2))
    rate_grad = rate_grad_s + rate_grad_c + rate_grad_a
    query_grad = query_grad_att + query_grad_s + query_grad_c
    key_grad = key_grad_att + key_grad_s
    value_grad = value_grad_att + value_grad_s
    triple_grad = (
        jnp.stack([query_grad, key_grad, value_grad])
        .reshape(3, block_len, pair_width)
        .astype(jnp.bfloat16)
    )
    token_grads = lax.all_to_all(triple_grad, "head", split_axis=1, concat_axis=2, tiled=True)
    grad_query_w = transposed_times(normed, token_grads[0])
    grad_key_w = transposed_times(normed, token_grads[1])
    grad_value_w = transposed_times(normed, token_grads[2])
    normed_grad = (
        times_transposed(token_grads[0], back_query)
        + times_transposed(token_grads[1], back_key)
        + times_transposed(token_grads[2], back_value)
    )
    input_grad_n, grad_gain_one = norm_back_one(normed_grad)
    input_grad = (resid_grad + input_grad_n).astype(jnp.bfloat16)
    ext_total = jnp.sum(ext_grads, axis=0)
    table_grad = jnp.dot(ext_total[:, WIN - 1 : 2 * WIN - 1], onehot_table, precision=highest)
    table_grad, rate_grad = lax.psum((table_grad, rate_grad), "seq")
    summed = (
        lax.psum_scatter(grad_query_w, ("head", "seq"), scatter_dimension=0, tiled=True),
        lax.psum_scatter(grad_key_w, ("head", "seq"), scatter_dimension=0, tiled=True),
        lax.psum_scatter(grad_value_w, ("head", "seq"), scatter_dimension=0, tiled=True),
        lax.psum_scatter(grad_out_w, ("head", "seq"), scatter_dimension=0, tiled=True),
        lax.psum_scatter(grad_up_w, ("head", "seq"), scatter_dimension=0, tiled=True),
        lax.psum_scatter(grad_down_w, ("head", "seq"), scatter_dimension=0, tiled=True),
        lax.psum_scatter(grad_gain_one, ("head", "seq"), scatter_dimension=0, tiled=True),
        lax.psum_scatter(grad_gain_two, ("head", "seq"), scatter_dimension=0, tiled=True),
    )
    grad_query, grad_key, grad_value, grad_out, grad_up, grad_down, grad_norm_one, grad_norm_two = (
        summed
    )
    return (
        output,
        input_grad,
        grad_query,
        grad_key,
        grad_value,
        grad_out,
        grad_up,
        grad_down,
        grad_norm_one,
        grad_norm_two,
        table_grad,
        rate_grad,
    )


def solution(mesh):
    devices = mesh.shape["head"] * mesh.shape["seq"]
    tiled = mesh.shape["head"] == 4 and 1024 // devices == 32
    return jax.shard_map(
        shards if tiled else general_shards,
        mesh=mesh,
        in_specs=(
            P(("seq", "head"), None),
            P(("seq", "head"), None),
            P(),
            P(("head", "seq"), None),
            P(("head", "seq"), None),
            P(("head", "seq"), None),
            P(("head", "seq"), None),
            P(("head", "seq"), None),
            P(("head", "seq"), None),
            P(("head", "seq")),
            P(("head", "seq")),
            P("head", None),
            P("head"),
        ),
        out_specs=(
            P(("seq", "head"), None),
            P(("seq", "head"), None),
            P(("head", "seq"), None),
            P(("head", "seq"), None),
            P(("head", "seq"), None),
            P(("head", "seq"), None),
            P(("head", "seq"), None),
            P(("head", "seq"), None),
            P(("head", "seq")),
            P(("head", "seq")),
            P("head", None),
            P("head"),
        ),
        check_vma=False,
    )
```

```python
import functools
import math

import jax
import jax.numpy as jnp
import numpy as np
from jax import lax
from jax.experimental import pallas as pl
from jax.experimental.pallas import tpu as pltpu
from jax.sharding import PartitionSpec as P

HD = 128
BUCKETS = 32
WIN = 512
TILE = 256

epsilon = 1e-06
negative = -1e30
state_scale = 1.0 / 1024.0
MESH = pl.DeviceIdType.MESH
f32 = jnp.float32
bf16 = jnp.bfloat16


def dot(a, b):
    return jnp.dot(a, b, preferred_element_type=f32)


def dot_t(a, b):
    return lax.dot_general(a, b, (((1,), (1,)), ((), ())), preferred_element_type=f32)


def t_dot(a, b):
    return lax.dot_general(a, b, (((0,), (0,)), ((), ())), preferred_element_type=f32)


class Place:
    def __init__(self):
        self.h = lax.axis_index("head")
        self.s = lax.axis_index("seq")
        self.n = lax.axis_size("seq")
        self.nz = self.n // 2
        self.z = self.s // 2
        self.core = self.s % 2
        x, y = self.h % 2, self.h // 2
        self.heads = [2 * y + 1 - x, 2 * (1 - y) + x, 2 * (1 - y) + 1 - x]

    def head_dev(self, k):
        return (self.heads[k], self.s)

    def z_to(self, k):
        return ((self.z + k) % self.nz) * 2 + self.core

    def z_from(self, k):
        return ((self.z + self.nz - k) % self.nz) * 2 + self.core

    def z_dev(self, k):
        return (self.h, self.z_to(k))

    def other(self):
        return self.z * 2 + 1 - self.core

    def core_dev(self):
        return (self.h, self.other())

    def seq_dev(self, by):
        return (self.h, (self.s + self.n + by) % self.n)


def greet(devices):
    barrier = pltpu.get_barrier_semaphore()
    for device in devices:
        pl.semaphore_signal(barrier, inc=1, device_id=device, device_id_type=MESH)
    pl.semaphore_wait(barrier, len(devices))


class Sends:
    def __init__(self, send_sems, recv_sems):
        self.send_sems, self.recv_sems = send_sems, recv_sems
        self.sent_at, self.recv_at, self.all = 0, 0, []

    def claim(self, count):
        self.recv_at += count
        return self.recv_at - count

    def copy(self, src, dst, device, send, recv):
        return pltpu.make_async_remote_copy(
            src_ref=src,
            dst_ref=dst,
            send_sem=self.send_sems.at[send],
            recv_sem=self.recv_sems.at[recv],
            device_id=device,
            device_id_type=MESH,
        )

    def put(self, src, dst, device, recv=None):
        recv = self.claim(1) if recv is None else recv
        copy = self.copy(src, dst, device, self.sent_at, recv)
        self.sent_at += 1
        self.all.append(copy)
        copy.start()
        return copy

    def sent(self, copies):
        for copy in copies:
            copy.wait_send()
        self.all = [c for c in self.all if not any(c is d for d in copies)]

    def finish(self):
        for copy in self.all:
            copy.wait_send()


class Line:
    def __init__(self, me, sends, place):
        self.me, self.sends, self.place = me, sends, place
        z = me.z
        inner = (z * (3 - z)) // 2
        self.near, self.next = 1 + z % 2, 2 * (1 - z % 2) + z // 2
        self.order = [self.near, self.next, 6 - z - self.near - self.next]
        self.piece, self.end = z + inner * (3 - 2 * z), 3 * (1 - z % 2)
        self.base = sends.claim(4)
        self.copies = []

    def put(self, src, chip, to):
        me = self.me
        device = (me.h, 2 * to + me.core)
        self.copies.append(self.sends.put(src, self.place(chip), device, self.base + chip))

    def start(self, own):
        for to in (self.near, self.next):
            self.put(own, self.me.z, to)

    def wait(self, i):
        chip = self.order[i]
        ref = self.place(chip)
        device = (self.me.h, 2 * chip + self.me.core)
        self.sends.copy(ref, ref, device, 0, self.base + chip).wait_recv()
        return ref

    def relay(self):
        ref = self.wait(0)
        self.put(self.place(self.piece), self.piece, self.end)
        return ref


class Square:
    def __init__(self, me, sends, block):
        self.me, self.sends, self.block = me, sends, block

    def start(self, own):
        me = self.me
        self.got = [
            self.sends.put(own, self.block(me.h, None), me.head_dev(k)) for k in range(2)
        ]
        self.halves = []

    def relay(self):
        me = self.me
        for k in range(2):
            self.got[k].wait_recv()
            ref = self.block(me.heads[k], k)
            self.halves.append(self.sends.put(ref, ref, me.head_dev(1 - k)))

    def last(self):
        for copy in self.halves:
            copy.wait_recv()


class SquareSum:
    def __init__(self, me, sends, give, land):
        self.me, self.sends, self.give, self.land = me, sends, give, land
        half = give(2).shape[0] // 2
        self.parts = [pl.ds(0, half), pl.ds(half, half)]
        self.half = half

    def first(self):
        me, give, land = self.me, self.give(2), self.land(2)
        self.halves = [
            self.sends.put(give.at[self.parts[k]], land.at[self.parts[k]], me.head_dev(k))
            for k in range(2)
        ]

    def second(self):
        me, land = self.me, self.land(2)
        self.copies = []
        for k in range(2):
            self.halves[k].wait_recv()
            give = self.give(1 - k)

            def add(i, _):
                at = pl.ds(pl.multiple_of(k * self.half + i * 32, 32), 32)
                give[at] = (give[at].astype(f32) + land[at].astype(f32)).astype(bf16)
                return 0

            lax.fori_loop(0, self.half // 32, add, 0)
        for k in range(2):
            self.copies.append(self.sends.put(self.give(k), self.land(k), me.head_dev(k)))

    def last(self):
        for copy in self.copies:
            copy.wait_recv()


def rms(x):
    return lax.rsqrt(jnp.mean(x * x, axis=-1, keepdims=True) + epsilon)


LOG2E = math.log2(math.e)
KEY_SCALE = LOG2E / math.sqrt(HD)


def bucket_starts():
    distance = np.arange(WIN)
    scaled = np.floor(np.log(np.maximum(distance, 1) / 16.0) / np.log(8.0) * 16.0)
    larger = np.minimum(16 + np.maximum(scaled, 0), BUCKETS - 1)
    bucket = np.where(distance < 16, distance, larger).astype(np.int32)
    return [int(np.argmax(bucket == b)) for b in range(BUCKETS)]


STARTS = bucket_starts()


def grid_of(axis, shape=(TILE, TILE)):
    return lax.broadcasted_iota(jnp.int32, shape, axis)


def column(row):
    eye = grid_of(0) == grid_of(1)
    return jnp.sum(jnp.where(eye, row, 0.0), axis=1, keepdims=True)


class Segs:
    def __init__(self, me, seg_ref, rows, cols):
        total = 4 * me.n
        self.rows, self.cols = rows, cols

        def row_at(offset):
            at = 2 * ((4 * me.s + total + offset) % total)
            pair = [seg_ref[pl.ds(at + i, 1)].astype(f32) for i in range(2)]
            return jnp.concatenate(pair, axis=1)

        for j in range(6):
            row = row_at(j - 2)
            rows[j] = row
            if j >= 2:
                cols[j - 2] = column(row)
        last = lambda offset: row_at(offset)[:, TILE - 1 : TILE]
        self.last = [last(j - 2) for j in range(6)]
        same = lambda a, b: (a == b).astype(f32)
        self.keep = [same(self.last[t + 2], self.last[t + 1]) for t in range(4)]
        self.keep_before = same(last(-1), last(-5))
        self.keep_after = same(last(7), last(3))

    def live(self, t):
        return (self.cols[t] == self.last[t + 1]).astype(f32)

    def kept(self, t):
        return (self.cols[t] == self.last[t + 2]).astype(f32)


def fill_tables(table_ref, decay_ref, near, far, decay, enter, leave):
    gap = grid_of(0) - grid_of(1)
    place = grid_of(0, (TILE, 1)).astype(f32)
    for head in range(2):
        rate = decay_ref[0, head]
        for out, shift in ((near, 0), (far, TILE)):
            bias = jnp.full((TILE, TILE), table_ref[head, 0] * LOG2E, f32)
            for b in range(1, BUCKETS):
                bias = jnp.where(gap + shift >= STARTS[b], table_ref[head, b] * LOG2E, bias)
            out[head] = jnp.where(gap + shift >= 0, bias, negative)
        fall = jnp.exp(-rate * jnp.maximum(gap, 0).astype(f32)) * state_scale
        decay[head] = jnp.where(gap >= 0, fall, 0.0)
        enter[head] = jnp.exp(-rate * (place + 1.0)) * state_scale
        leave[head] = jnp.exp(-rate * (TILE - 1.0 - place))


def power(rate, steps):
    return jnp.exp(jnp.full((1, HD), -rate * steps, f32))


def tile_scores(raw, head, t, table_ref, near, far, segs):
    col = segs.cols[t]
    same = [col == segs.rows[t + j] for j in range(3)]
    reach = grid_of(0) < grid_of(1)
    rest = table_ref[head, BUCKETS - 1] * LOG2E
    s0 = jnp.where(same[0] & reach, raw[:, :TILE] * KEY_SCALE + rest, negative)
    s1 = jnp.where(same[1], raw[:, TILE : 2 * TILE] * KEY_SCALE + far[head], negative)
    s2 = jnp.where(same[2], raw[:, 2 * TILE :] * KEY_SCALE + near[head], negative)
    return s0, s1, s2, same[2]


GELU_C = math.sqrt(2.0 / math.pi)
GELU_A = 0.044715


def part(i, size):
    return pl.ds(pl.multiple_of(i * size, size), size)


class Reduce:
    def __init__(self, me, sends, own, given, core_in, z_in, keep):
        self.me, self.sends = me, sends
        self.own, self.given, self.core_in, self.z_in, self.keep = own, given, core_in, z_in, keep
        self.width = keep.shape[-1]

    def start(self):
        self.core = self.sends.put(self.given, self.core_in, self.me.core_dev())

    def put(self, chunk, to, slot):
        me = self.me
        device = (me.h, 2 * to + me.core)
        src, dst = self.given.at[chunk], self.z_in.at[slot]
        self.copies.append(self.sends.put(src, dst, device, self.base + slot))

    def wait(self, slot):
        ref = self.z_in.at[slot]
        self.sends.copy(ref, ref, self.me.core_dev(), 0, self.base + slot).wait_recv()

    def join(self):
        me, lanes = self.me, pl.ds(0, self.width)
        z = me.z
        self.core.wait_recv()
        self.sends.sent([self.core])
        self.inner = (z * (3 - z)) // 2
        self.beside, self.across, self.far = z + 1 - 2 * (z % 2), (z + 2) % 4, 3 - z
        for chunk in (self.beside, self.across, self.far):

            def both(i, at):
                total = self.own[chunk, at, lanes] + self.core_in[chunk, at].astype(f32)
                self.given[chunk, at] = total.astype(bf16)

            each(128, 32, both)

        def mine(i, at):
            self.keep[at] = self.own[z, at, lanes] + self.core_in[z, at].astype(f32)

        each(128, 32, mine)

    def along(self):
        self.base, self.copies = self.sends.claim(3), []
        self.put(self.beside, self.beside, 0)
        to = self.inner * self.across + (1 - self.inner) * self.beside
        self.put(self.across, to, 2 - self.inner)

    def late(self):
        @pl.when(self.inner == 1)
        def _():
            self.wait(2)

            def add(i, at):
                total = self.given[self.far, at].astype(f32) + self.z_in[2, at].astype(f32)
                self.given[self.far, at] = total.astype(bf16)

            each(128, 32, add)

        self.put(self.far, self.far, 2 - self.inner)

    def total(self):
        for slot in range(2):
            self.wait(slot)

        def more(i, at):
            self.keep[at] += self.z_in[0, at].astype(f32) + self.z_in[1, at].astype(f32)

        each(128, 32, more)

        @pl.when(self.inner == 0)
        def _():
            self.wait(2)

            def add(i, at):
                self.keep[at] += self.z_in[2, at].astype(f32)

            each(128, 32, add)


def each(count, step, body):
    def one(i, _):
        body(i, part(i, step))
        return 0

    lax.fori_loop(0, count // step, one, 0)


def whole_kernel(ins, outs, b, send_sems, recv_sems):
    me = Place()
    nz, n = me.nz, me.n
    rows, tok = ins.w_out.shape[0], ins.tokens.shape[0]
    peers = [me.head_dev(k) for k in range(3)]
    greet(
        peers
        + [me.seq_dev(k) for k in range(1, n)]
    )
    sends = Sends(send_sems, recv_sems)
    core_dev = me.core_dev()
    half = pl.ds(me.core * nz, nz)
    wide = 6 * HD

    lane = lax.broadcasted_iota(jnp.int32, (rows, 128), 1)
    line = lax.broadcasted_iota(jnp.int32, (rows, 128), 0)
    group = 128 // rows
    gains = jnp.zeros((rows, 128), f32)
    for j, gain in enumerate((ins.norm_one, ins.norm_two)):
        row = jnp.concatenate([gain[...].astype(f32)] * group, axis=1)
        gains = jnp.where((lane // rows == me.s % group) & (line == j), row, gains)
    b.gains[...] = gains.astype(bf16)
    first = []
    parts = (ins.w_query, ins.w_key, ins.w_value)
    for k in range(3):
        for j, w in enumerate(parts):
            src = w.at[:, part(me.heads[k], 256)]
            first.append(sends.put(src, b.a1.at[me.h, :, j * 256 : j * 256 + 256], peers[k]))
        first.append(sends.put(b.gains, b.a1.at[me.h, :, wide:], peers[k]))

    def token_block(ref):
        def block(i, piece):
            if piece is None:
                return ref.at[part(i, tok)]
            return ref.at[part(2 * i + piece, tok // 2)]

        return block

    toks = Square(me, sends, token_block(b.x))
    toks.start(ins.tokens)
    first_up = []
    for k in range(3):
        src = ins.w_up.at[:, part(me.heads[k], 1024)]
        first_up.append(sends.put(src, b.u1.at[me.h], peers[k]))
    w_line = Line(me, sends, lambda z: b.wb.at[:, 2 * z + me.core])
    wo_line = Line(me, sends, lambda z: b.wo.at[me.h, 2 * z + me.core])
    up_line = Line(me, sends, lambda z: b.up.at[:, 2 * z + me.core])
    dn_line = Line(me, sends, lambda z: b.dn.at[2 * z + me.core])
    for j, w in enumerate(parts):
        b.a1[me.h, :, j * 256 : j * 256 + 256] = w[:, part(me.h, 256)]
    b.a1[me.h, :, wide:] = b.gains[...]
    for copy in first:
        copy.wait_recv()
    w_line.start(b.a1)
    w_c = [sends.put(b.a1, b.wb.at[:, me.s], core_dev)]
    b.wb[:, me.s] = b.a1[...]
    b.x[part(me.h, tok)] = ins.tokens[...]
    b.u1[me.h] = ins.w_up[:, part(me.h, 1024)]
    b.wo[me.h, me.s] = ins.w_out[...]
    b.dn[me.s] = ins.w_down[...]
    b.cots[part(me.h, tok)] = ins.cotangent[...]
    own = b.wo.at[me.h, me.s]
    w_c.append(sends.put((ref := w_line.relay()), ref, core_dev))
    wo_line.start(ins.w_out)
    wo_c = [sends.put(ins.w_out, own, core_dev)]
    toks.relay()
    cots = Square(me, sends, token_block(b.cots))
    cots.start(ins.cotangent)
    segs = Segs(me, ins.segments, b.rows, b.cols)
    fill_tables(ins.table, ins.decay, b.near, b.far, b.decay, b.enter, b.leave)
    for i in (1, 2):
        ref = w_line.wait(i)
        w_c.append(sends.put(ref, ref, core_dev))
    for copy in first_up:
        copy.wait_recv()
    up_line.start(b.u1)
    up_c = [sends.put(b.u1, b.up.at[:, me.s], core_dev)]
    b.up[:, me.s] = b.u1[...]
    wo_c.append(sends.put((ref := wo_line.relay()), ref, core_dev))
    for copy in w_c:
        copy.wait_recv()
    lanes = []
    for h in range(4):
        for s in range(0, n, group):
            lanes.append(sum(b.wb[h, s + i, :, wide:].astype(f32) for i in range(group)))
    gains = jnp.concatenate(lanes, axis=1)
    gain_one, gain_two = gains[0:1], gains[1:2]
    toks.last()

    def norm_one(i, at):
        x = b.x[at].astype(f32)
        b.hall[at] = (x * rms(x) * gain_one).astype(bf16)

    each(4 * tok, 32, norm_one)

    def project(t, _):
        at = part(t, tok)
        for j in range(3):
            w = b.wb[:, :, :, j * 256 : j * 256 + 256].reshape(1024, 256)
            out = dot(b.hall[at], w).astype(bf16)
            for head in range(2):
                mine = out[:, head * HD : head * HD + HD]
                if j == 0:
                    b.q[head, at] = mine
                else:
                    b.kvx[2 * (j - 1) + head, part(t + 2, tok)] = mine
        return 0

    lax.fori_loop(0, 4, project, 0)
    sends.sent(toks.halves)
    halo = sends.put(b.kvx.at[:, 4 * TILE :], b.kvx.at[:, : 2 * TILE], me.seq_dev(1))

    falls = [power(ins.decay[0, head], float(TILE)) for head in range(2)]
    for head in range(2):
        state = jnp.zeros((HD, HD), f32)
        for t in range(4):
            at = pl.ds((t + 2) * TILE, TILE)
            key = (b.kvx[head, at].astype(f32) * (b.leave[head] * segs.kept(t))).astype(bf16)
            add = t_dot(key, b.kvx[2 + head, at])
            b.local[4 * head + t] = add
            state = falls[head] * segs.keep[t] * state + add
        b.sent[head] = state.astype(bf16)
    carry = [sends.put(b.sent, b.got.at[k - 1], me.seq_dev(k)) for k in (1, 2)]
    up_c.append(sends.put((ref := up_line.relay()), ref, core_dev))
    for i in (1, 2):
        ref = wo_line.wait(i)
        wo_c.append(sends.put(ref, ref, core_dev))
    dn_line.start(ins.w_down)
    dn_c = [sends.put(ins.w_down, b.dn.at[me.s], core_dev)]
    cots.relay()
    for copy in wo_c:
        copy.wait_recv()

    def wo_block(i, piece):
        if piece is None:
            return b.wo.at[i, half]
        return b.wo.at[i, pl.ds(me.core * nz + piece * (nz // 2), nz // 2)]

    wo_square = Square(me, sends, wo_block)
    wo_square.start(b.wo.at[me.h, half])

    def forward(index, base):
        head, t = index // 2, base + index % 2
        at, own = part(t, TILE), part(t + 2, TILE)
        wide = pl.ds(pl.multiple_of(t * TILE, TILE), 3 * TILE)
        raw = dot_t(b.q[head, at], b.kvx[head, wide])
        s0, s1, s2, same = tile_scores(raw, head, t, ins.table, b.near, b.far, segs)
        top = jnp.maximum(jnp.maximum(s0, s1), s2).max(axis=1, keepdims=True)
        e0, e1, e2 = jnp.exp2(s0 - top), jnp.exp2(s1 - top), jnp.exp2(s2 - top)
        mass = (e0 + e1 + e2).sum(axis=1, keepdims=True)
        b.lse[4 * head + t] = top + jnp.log2(mass)
        mix = jnp.concatenate([e0.astype(bf16), e1.astype(bf16), e2.astype(bf16)], axis=1)
        att = dot(mix, b.kvx[2 + head, wide]) / mass
        weight = jnp.where(same, raw[:, 2 * TILE :] * b.decay[head], 0.0).astype(bf16)
        b.acc[head, at] = att + dot(weight, b.kvx[2 + head, own])
        return base

    lax.fori_loop(0, 4, forward, 2)
    halo.wait_recv()
    lax.fori_loop(0, 4, forward, 0)
    wo_square.relay()
    dn_c.append(sends.put((ref := dn_line.relay()), ref, core_dev))
    wo_square.last()
    for k in range(3):
        piece = b.wo.at[me.heads[k], half]
        wo_c.append(sends.put(piece, piece, core_dev))
    for copy in carry:
        copy.wait_recv()
    for head in range(2):
        past = power(ins.decay[0, head], 4.0 * TILE) * segs.keep_before
        state = b.got[0, head].astype(f32) + past * b.got[1, head].astype(f32)
        for t in range(4):
            at = pl.ds(t * TILE, TILE)
            b.state[4 * head + t] = state
            reach = b.enter[head] * segs.live(t)
            y = b.acc[head, at] + dot(b.q[head, at], state.astype(bf16)) * reach
            b.dyt[2 * t + head] = y.astype(bf16)
            state = falls[head] * segs.keep[t] * state + b.local[4 * head + t]
    ys = []
    for k in range(3):
        for head in range(2):
            src = b.dyt.at[2 * me.heads[k] + head]
            ys.append(sends.put(src, b.ymix.at[:, part(2 * me.h + head, HD)], peers[k]))
    for head in range(2):
        b.ymix[:, part(2 * me.h + head, HD)] = b.dyt[2 * me.h + head]
    for i in (1, 2):
        ref = up_line.wait(i)
        up_c.append(sends.put(ref, ref, core_dev))
    for copy in ys + wo_c[-3:]:
        copy.wait_recv()

    def out_tile(j, _):
        cols = part(j, 256)
        w = b.wo[:, :, :, cols].reshape(1024, 256)
        b.x1[:, cols] = ins.tokens[:, cols].astype(f32) + dot(b.ymix[...], w)
        return 0

    lax.fori_loop(0, 4, out_tile, 0)
    def norm_two(i, at):
        x = b.x1[at]
        b.h2all[pl.ds(pl.multiple_of(me.h * tok + i * 32, 32), 32)] = (x * rms(x) * gain_two).astype(bf16)
        b.base[at] = x

    each(tok, 32, norm_two)
    own = b.h2all.at[part(me.h, tok)]
    h2s = Square(me, sends, token_block(b.h2all))
    h2s.start(own)
    for i in (1, 2):
        ref = dn_line.wait(i)
        dn_c.append(sends.put(ref, ref, core_dev))
    cots.last()
    for copy in up_c + dn_c:
        copy.wait_recv()
    dn2_copies = []
    for k in range(-1, 3):
        at = part(me.h if k < 0 else me.heads[k], tok)
        if k == 0:
            h2s.relay()
        elif k == 2:
            h2s.last()

        def hidden(j, _):
            cols = part(j, 256)
            u = dot(b.h2all[at], b.up[:, :, :, cols].reshape(1024, 256))
            dg = dot_t(b.cots[at], b.dn[pl.ds(2 * j, 2)].reshape(256, 1024))
            uu = u * u
            t = jnp.tanh(GELU_C * u * (1.0 + GELU_A * uu))
            b.x[at, cols] = (0.5 * u * (1.0 + t)).astype(bf16)
            slope = 0.5 * (1.0 + t) + (0.5 * GELU_C) * u * (1.0 - t * t) * (1.0 + 3.0 * GELU_A * uu)
            b.du[at, cols] = (slope * dg).astype(bf16)
            return 0

        lax.fori_loop(0, 4, hidden, 0)

        def back(j, _):
            w = b.up[j].reshape(256, 1024)
            b.dn2s[k + 1, :, part(j, 256)] = dot_t(b.du[at], w).astype(bf16)
            return 0

        lax.fori_loop(0, 4, back, 0)
        if k >= 0:
            dn2_copies.append(sends.put(b.dn2s.at[k + 1], b.dnin.at[k], peers[k]))

        def ahead(j, _):
            cols = part(j, 256)
            out = dot(b.x[at], b.dn[:, :, cols].reshape(1024, 256))
            if k < 0:
                b.base[:, cols] = b.base[:, cols] + out
            else:
                b.outp[k, :, cols] = out.astype(bf16)
            return 0

        lax.fori_loop(0, 4, ahead, 0)

    def down_tile(j, _):
        b.tile[...] = t_dot(b.x[:, part(j, 256)], b.cots[...])
        b.own[j] = b.tile[part(me.core, 128)]
        b.given_a[j] = b.tile[part(1 - me.core, 128)].astype(bf16)
        return 0

    lax.fori_loop(0, 4, down_tile, 0)
    down = Reduce(me, sends, b.own, b.given_a, b.core_a, b.z_a, outs.grad_down)
    down.start()

    for copy in dn2_copies:
        copy.wait_recv()
    b.norms[...] = jnp.zeros_like(b.norms)

    def second_norm_back(i, at):
        dn2 = b.dn2s[0, at].astype(f32) + sum(b.dnin[k, at].astype(f32) for k in range(3))
        x = b.x1[at]
        scale = rms(x)
        n2 = x * scale
        b.norms[1:2] += jnp.sum(dn2 * n2, axis=0, keepdims=True)
        spread = dn2 * gain_two
        dx1 = ins.cotangent[at].astype(f32) + scale * (
            spread - n2 * jnp.mean(spread * n2, axis=-1, keepdims=True)
        )
        b.x1[at] = dx1
        b.da[at] = dx1.astype(bf16)

    each(tok, 32, second_norm_back)
    sends.sent(ys + dn2_copies + dn_c[1:] + dn_line.copies)

    def back_tile(j, _):
        out = dot_t(b.da[...], b.wo[j].reshape(256, 1024)).astype(bf16)
        b.dyt[2 * j] = out[:, :HD]
        b.dyt[2 * j + 1] = out[:, HD:]
        return 0

    lax.fori_loop(0, 4, back_tile, 0)
    dys = []
    for k in range(3):
        src = b.dyt.at[pl.ds(2 * me.heads[k], 2)]
        dys.append(sends.put(src, b.dyh.at[:, part(me.h, tok)], peers[k]))
    b.dyh[:, part(me.h, tok)] = b.dyt[pl.ds(2 * me.h, 2)]
    down.join()
    down.along()

    def up_tile(j, _):
        b.tile[...] = t_dot(b.h2all[:, part(j, 256)], b.du[...])
        for z in range(nz):
            b.own[z, part(j, 32)] = b.tile[part(2 * z + me.core, 32)]
            b.given_b[z, part(j, 32)] = b.tile[part(2 * z + 1 - me.core, 32)].astype(bf16)
        return 0

    lax.fori_loop(0, 4, up_tile, 0)
    up = Reduce(me, sends, b.own, b.given_b, b.core_b, b.z_b, b.up_sum)
    up.start()
    down.late()
    for copy in dys:
        copy.wait_recv()
    outp = SquareSum(me, sends, lambda k: b.outp.at[k], lambda k: b.dnin.at[k])
    outp.first()
    for zero in (b.sums, b.dks, b.dvs, b.diag, b.below, b.rest):
        zero[...] = jnp.zeros_like(zero)
    for head in range(2):
        grad = jnp.zeros((HD, HD), f32)
        for t in range(3, -1, -1):
            at = pl.ds(t * TILE, TILE)
            query = (b.q[head, at].astype(f32) * (b.enter[head] * segs.live(t))).astype(bf16)
            add = t_dot(query, b.dyh[head, at])
            b.local[4 * head + t] = add
            grad = falls[head] * segs.keep[t] * grad + add
        b.sent_back[head] = grad.astype(bf16)
    carry = [sends.put(b.sent_back, b.got_back.at[k - 1], me.seq_dev(-k)) for k in (1, 2)]
    up.join()

    def grad_out_tile(j, _):
        b.tile[...] = t_dot(b.ymix[:, part(j, 256)], b.da[...])
        for z in range(nz):
            b.own[j, part(z, 32)] = b.tile[part(2 * z + me.core, 32)]
            b.dn[j, part(z, 32)] = b.tile[part(2 * z + 1 - me.core, 32)].astype(bf16)
        return 0

    lax.fori_loop(0, 4, grad_out_tile, 0)
    o_core = sends.put(b.dn.at[0:4], b.core_o, core_dev)
    outp.second()

    gap = (grid_of(0) - grid_of(1)).astype(f32)

    def backward(index, base):
        head, t = index // 2, base + index % 2
        at, wide = part(t, TILE), pl.ds(pl.multiple_of(t * TILE, TILE), 3 * TILE)
        query, dy = b.q[head, at], b.dyh[head, at]
        keys, values = b.kvx[head, wide], b.kvx[2 + head, wide]
        raw = dot_t(query, keys)
        s0, s1, s2, same = tile_scores(raw, head, t, ins.table, b.near, b.far, segs)
        lse = b.lse[4 * head + t]
        p0, p1, p2 = jnp.exp2(s0 - lse), jnp.exp2(s1 - lse), jnp.exp2(s2 - lse)
        dp = dot_t(dy, values)
        dp0, dp1, dp2 = dp[:, :TILE], dp[:, TILE : 2 * TILE], dp[:, 2 * TILE :]
        mean = (p0 * dp0 + p1 * dp1 + p2 * dp2).sum(axis=1, keepdims=True)
        d0, d1, d2 = p0 * (dp0 - mean), p1 * (dp1 - mean), p2 * (dp2 - mean)
        b.diag[head] += d2[:HD, :HD] + d2[HD:, HD:]
        b.below[head] += d2[HD:, :HD] + d1[:HD, HD:]
        b.rest[head] += (
            (d0[:, :HD] + d0[:, HD:]).sum(axis=0, keepdims=True)
            + d1[:, :HD].sum(axis=0, keepdims=True)
            + d1[HD:, HD:].sum(axis=0, keepdims=True)
        )
        weight = jnp.where(same, b.decay[head], 0.0)
        mixed = weight * raw[:, 2 * TILE :]
        turn = weight * dp2
        slope = mixed * dp2 * gap
        b.sums[head] -= (slope[:, :HD] + slope[:, HD:]).sum(axis=0, keepdims=True)
        scale = 1.0 / math.sqrt(HD)
        x = jnp.concatenate(
            [(d0 * scale).astype(bf16), (d1 * scale).astype(bf16), (d2 * scale + turn).astype(bf16)],
            axis=1,
        )
        p = jnp.concatenate([p0.astype(bf16), p1.astype(bf16), (p2 + mixed).astype(bf16)], axis=1)
        b.acc[head, at] = dot(x, keys)
        b.dks[head, wide] += t_dot(x, query)
        b.dvs[head, wide] += t_dot(p, dy)
        return base

    lax.fori_loop(0, 4, backward, 0)
    sends.sent(dys)
    for head in range(2):
        for i in range(2):
            at = pl.ds(i * TILE, TILE)
            b.dyt[2 * head + i] = b.dks[head, at].astype(bf16)
            b.dyt[4 + 2 * head + i] = b.dvs[head, at].astype(bf16)
    halo = sends.put(b.dyt, b.halo_in, me.seq_dev(-1))
    up.along()
    o_core.wait_recv()
    sends.sent(down.copies)
    for k in range(3):
        to = me.heads[k]

        def chip_sum(i, at):
            both = b.own[to, at] + b.core_o[to, at].astype(f32)
            b.given_a[k, at] = both.astype(bf16)

        each(128, 32, chip_sum)
    o_square = SquareSum(me, sends, lambda k: b.given_a.at[k], lambda k: b.o_in.at[k])
    o_square.first()

    def keep(i, at):
        b.o_keep[at] = b.own[me.h, at] + b.core_o[me.h, at].astype(f32)

    each(128, 32, keep)
    lax.fori_loop(0, 4, backward, 2)
    o_square.second()
    up.late()
    for copy in carry:
        copy.wait_recv()
    place = grid_of(0, (TILE, 1)).astype(f32)
    halo.wait_recv()
    for head in range(2):
        past = power(ins.decay[0, head], 4.0 * TILE) * segs.keep_after
        grad = b.got_back[0, head].astype(f32) + past * b.got_back[1, head].astype(f32)
        fall = falls[head]
        total = jnp.zeros((1, HD), f32)
        for t in range(3, -1, -1):
            at = pl.ds(t * TILE, TILE)
            ext = pl.ds((t + 2) * TILE, TILE)
            low = grad.astype(bf16)
            state = b.state[4 * head + t]
            give = b.leave[head] * segs.kept(t)
            take = b.enter[head] * segs.live(t)
            query, key, value = b.q[head, at], b.kvx[head, ext], b.kvx[2 + head, ext]
            dq = dot_t(b.dyh[head, at], state.astype(bf16)) * take
            dv = dot(key, low) * give
            dk = dot_t(value, low) * give + b.dks[head, ext]
            slope = dq * query.astype(f32) * (place + 1.0)
            slope = slope + dv * value.astype(f32) * (TILE - 1.0 - place)
            crossing = fall * segs.keep[t]
            total = total - slope.sum(axis=0, keepdims=True)
            total = total - TILE * crossing * (grad * state).sum(axis=0, keepdims=True)
            dv = dv + b.dvs[head, ext]
            if t >= 2:
                dk = dk + b.halo_in[2 * head + t - 2].astype(f32)
                dv = dv + b.halo_in[4 + 2 * head + t - 2].astype(f32)
            for j, grads in enumerate((b.acc[head, at] + dq, dk, dv)):
                col = (2 * j + head) * HD
                b.x[at, col : col + HD] = grads.astype(bf16)
            grad = b.local[4 * head + t] + crossing * grad
        b.sums[head] += total

    backs = SquareSum(
        me, sends, lambda k: b.du.at[pl.ds(k * tok, tok)], lambda k: b.dn2s.at[k + 1]
    )
    for k in (2, 0, 1):
        at, to = part(me.heads[k], tok), pl.ds(k * tok, tok)

        def spread_back(j, _):
            w = b.wb[j, :, :, 0:wide].reshape(256, wide)
            b.du[to, part(j, 256)] = dot_t(b.x[at, 0:wide], w).astype(bf16)
            return 0

        lax.fori_loop(0, 4, spread_back, 0)
        if k == 2:
            backs.first()

    def grad_tile(j, _):
        tile = pl.ds(0, wide)
        b.tile[:, tile] = t_dot(b.hall[:, part(j, 256)], b.x[:, 0:wide])
        for z in range(nz):
            b.own[z, part(j, 32), tile] = b.tile[part(2 * z + me.core, 32), tile]
            b.dn[4 + z, part(j, 32), tile] = b.tile[part(2 * z + 1 - me.core, 32), tile].astype(bf16)
        return 0

    lax.fori_loop(0, 4, grad_tile, 0)
    grads = Reduce(me, sends, b.own, b.dn.at[4:8, :, 0:wide], b.core_q, b.z_q, b.q_sum)
    grads.start()
    backs.second()
    outp.last()

    def output(i, at):
        total = b.base[at] + sum(b.dnin[k, at].astype(f32) for k in range(2))
        outs.output[at] = total.astype(bf16)

    each(tok, 32, output)

    def own_back(j, _):
        w = b.wb[j, :, :, 0:wide].reshape(256, wide)
        b.base[:, part(j, 256)] = dot_t(b.x[part(me.h, tok), 0:wide], w)
        return 0

    lax.fori_loop(0, 4, own_back, 0)
    grads.join()
    grads.along()
    o_square.last()

    def grad_out_sum(i, at):
        total = b.o_keep[at] + sum(b.o_in[k, at].astype(f32) for k in range(2))
        b.o_keep[at] = total
        b.o_low[at] = total.astype(bf16)

    each(128, 32, grad_out_sum)
    o_z = []
    for k in range(1, nz):
        src = b.o_low.at[part((me.z + k) % nz, 32)]
        o_z.append(sends.put(src, b.o_z.at[k - 1], me.z_dev(k)))
    down.total()
    up.total()
    ups = []
    for k in range(3):
        src = b.up_sum.at[part(me.heads[k], 32)]
        ups.append(sends.put(src, outs.grad_up.at[:, part(me.h, 1024)], peers[k]))
    outs.grad_up[:, part(me.h, 1024)] = b.up_sum[part(me.h, 32)]
    gap_near = grid_of(0, (HD, HD)) - grid_of(1, (HD, HD))
    gap_far = gap_near + HD
    table = []
    for head in range(2):
        last = b.rest[head]
        for i in range(BUCKETS):
            up_to = STARTS[i + 1] if i + 1 < BUCKETS else 2 * WIN
            inside = lambda g: (g >= STARTS[i]) & (g < up_to)
            total = jnp.where(inside(gap_near), b.diag[head], 0.0)
            total = total + jnp.where(inside(gap_far), b.below[head], 0.0)
            total = total.sum(axis=0, keepdims=True)
            table.append(total + last if i == BUCKETS - 1 else total)
    table += [b.sums[0], b.sums[1], jnp.zeros((HD - 2 * BUCKETS - 2, HD), f32)]
    small = lax.dot_general(
        jnp.ones((8, HD), f32), jnp.concatenate(table, axis=0), (((1,), (1,)), ((), ())),
        precision=lax.Precision.HIGHEST, preferred_element_type=f32,
    )
    grads.late()
    backs.last()

    def first_norm_back(i, at):
        dn1 = b.base[at] + sum(b.dn2s[k + 1, at].astype(f32) for k in range(2))
        x = ins.tokens[at].astype(f32)
        scale = rms(x)
        n1 = x * scale
        b.norms[0:1] += jnp.sum(dn1 * n1, axis=0, keepdims=True)
        spread = dn1 * gain_one
        dx = b.x1[at] + scale * (spread - n1 * jnp.mean(spread * n1, axis=-1, keepdims=True))
        outs.input_grad[at] = dx.astype(bf16)

    each(tok, 32, first_norm_back)
    lines = [b.norms[j : j + 1, i * HD : i * HD + HD] for j in range(2) for i in range(8)]
    b.small[...] = jnp.concatenate(lines + [small], axis=0)
    n_seq = [sends.put(b.small, b.n_seq.at[k - 1], me.seq_dev(k)) for k in range(1, n)]
    grads.total()
    g_head = []
    for k in range(3):
        src = b.q_sum.at[part(me.heads[k], 32)]
        g_head.append(sends.put(src, b.q_in.at[me.h], peers[k]))
    b.q_in[me.h] = b.q_sum[part(me.h, 32)]
    total = b.small[...]
    for k in range(n - 1):
        n_seq[k].wait_recv()
        total = total + b.n_seq[k]
    b.n_line[...] = total
    n_head = [sends.put(b.n_line, b.n_head.at[k], peers[k]) for k in range(3)]
    outs.table[...] = jnp.concatenate([total[16:17, i * BUCKETS : (i + 1) * BUCKETS] for i in range(2)], axis=0)
    outs.rate[...] = total[16:17, 2 * BUCKETS : 2 * BUCKETS + 2]
    total = b.o_keep[part(me.z, 32)]
    for k in range(nz - 1):
        o_z[k].wait_recv()
        total = total + b.o_z[k].astype(f32)
    outs.grad_out[...] = total
    for copy in g_head:
        copy.wait_recv()
    for h in range(4):
        for j, out in enumerate((outs.grad_query, outs.grad_key, outs.grad_value)):
            out[:, h * 256 : h * 256 + 256] = b.q_in[h, :, j * 256 : j * 256 + 256]
    for copy in n_head + ups:
        copy.wait_recv()
    total = b.n_line[...] + sum(b.n_head[k] for k in range(3))
    b.norms[0:8, 0:HD], b.norms[0:8, HD : 2 * HD] = total[0:8], total[8:16]
    mine = b.norms[pl.ds(2 * me.h + me.s // group, 1), 0 : 2 * HD]
    for j, out in enumerate((outs.norm_one, outs.norm_two)):
        row = jnp.zeros((1, rows), f32)
        for i in range(group):
            cut = mine[:, j * HD + i * rows : j * HD + (i + 1) * rows]
            row = jnp.where(me.s % group == i, cut, row)
        out[...] = row
    sends.finish()


def placed(arrays):
    def kernel(*refs):
        count = len(refs) // 2
        copies = [
            pltpu.make_async_copy(refs[i], refs[count + i], refs[-1].at[i]) for i in range(count)
        ]
        for copy in copies:
            copy.start()
        for copy in copies:
            copy.wait()

    return pl.pallas_call(
        kernel,
        out_shape=[jax.ShapeDtypeStruct(a.shape, a.dtype) for a in arrays],
        in_specs=[pl.BlockSpec(memory_space=pltpu.VMEM)] * len(arrays),
        out_specs=[pl.BlockSpec(memory_space=pl.ANY)] * len(arrays),
        scratch_shapes=[pltpu.SemaphoreType.DMA((len(arrays),))],
        name="results",
    )(*arrays)


class Names:
    def __init__(self, names, values):
        self.__dict__.update(zip(names, values))


def shards(
    tokens, cotangent, segments, w_query, w_key, w_value, w_out, w_up, w_down,
    norm_one, norm_two, rel_table, decay_rate,
):
    n = lax.axis_size("seq")
    nz = n // 2
    tok, rows = tokens.shape[0], w_query.shape[0]
    block = 4 * tok
    wide = 6 * HD
    ins = dict(
        table=rel_table, decay=decay_rate.reshape(1, 2), segments=segments.reshape(-1, 128),
        tokens=tokens, cotangent=cotangent, w_query=w_query, w_key=w_key, w_value=w_value,
        w_out=w_out, w_up=w_up, w_down=w_down,
        norm_one=norm_one.reshape(1, rows), norm_two=norm_two.reshape(1, rows),
    )
    outs = dict(
        output=((tok, 1024), bf16), input_grad=((tok, 1024), bf16),
        grad_query=((rows, 1024), f32), grad_key=((rows, 1024), f32),
        grad_value=((rows, 1024), f32), grad_out=((rows, 1024), f32),
        grad_up=((rows, 4096), f32), grad_down=((128, 1024), f32),
        norm_one=((1, rows), f32), norm_two=((1, rows), f32),
        table=((2, BUCKETS), f32), rate=((1, 2), f32),
    )
    pieces = (4, n, rows, 1024)
    square = ((block, 1024), bf16)
    three = ((3, tok, 1024), bf16)
    tables = ((2, TILE, TILE), f32)
    column = ((2, TILE, 1), f32)
    heads = ((2, HD, HD), f32)
    four = ((nz, 128, 1024), bf16)
    room = dict(
        gains=((rows, 128), bf16), a1=((4, rows, wide + 128), bf16), u1=((4, rows, 1024), bf16),
        x=square, hall=square, wb=((4, n, rows, wide + 128), bf16), up=(pieces, bf16),
        dn=((n, 128, 1024), bf16), wo=(pieces, bf16), cots=square,
        q=((2, block, HD), bf16), kvx=((4, 6 * TILE, HD), bf16),
        near=tables, far=tables, decay=tables, enter=column, leave=column,
        rows=((6, 1, TILE), f32), cols=((4, TILE, 1), f32),
        acc=((2, block, HD), f32), local=((8, HD, HD), f32), state=((8, HD, HD), f32),
        lse=((8, TILE, 1), f32),
        sent=((2, HD, HD), bf16), got=((2, 2, HD, HD), bf16),
        sent_back=((2, HD, HD), bf16), got_back=((2, 2, HD, HD), bf16),
        ymix=((tok, 1024), bf16),
        x1=((tok, 1024), f32), base=((tok, 1024), f32), h2all=square, du=square,
        dn2s=((4, tok, 1024), bf16), dnin=three, outp=three,
        da=((tok, 1024), bf16), dyt=((8, tok, HD), bf16), dyh=((2, block, HD), bf16),
        tile=((256, 1024), f32), own=((nz, 128, 1024), f32), o_keep=((128, 1024), f32),
        given_a=four, core_a=four, z_a=((3, 128, 1024), bf16),
        given_b=four, core_b=four, z_b=((nz - 1, 128, 1024), bf16), up_sum=((128, 1024), f32),
        core_o=four, o_in=((3, 128, 1024), bf16), o_low=((128, 1024), bf16),
        o_z=((nz - 1, 32, 1024), bf16),
        core_q=((nz, 128, wide), bf16),
        z_q=((nz - 1, 128, wide), bf16), q_sum=((128, wide), f32), q_in=((4, 32, wide), f32),
        diag=heads, below=heads, rest=((2, 1, HD), f32), sums=((2, 1, HD), f32),
        dks=((2, 6 * TILE, HD), f32), dvs=((2, 6 * TILE, HD), f32),
        halo_in=((8, TILE, HD), bf16),
        norms=((8, 1024), f32), small=((24, HD), f32), n_seq=((n - 1, 24, HD), f32),
        n_line=((24, HD), f32), n_head=((3, 24, HD), f32),
    )
    copies = 150

    def kernel(*refs):
        i, o = len(ins), len(ins) + len(outs)
        r = o + len(room)
        whole_kernel(Names(ins, refs[:i]), Names(outs, refs[i:o]), Names(room, refs[o:r]), *refs[r:])

    results = pl.pallas_call(
        kernel,
        out_shape=[jax.ShapeDtypeStruct(shape, kind) for shape, kind in outs.values()],
        in_specs=[pl.BlockSpec(memory_space=pltpu.SMEM)] * 2
        + [pl.BlockSpec(memory_space=pltpu.VMEM)] * (len(ins) - 2),
        out_specs=[pl.BlockSpec(memory_space=pltpu.VMEM)] * len(outs),
        scratch_shapes=[pltpu.VMEM(shape, kind) for shape, kind in room.values()]
        + [pltpu.SemaphoreType.DMA((copies,)), pltpu.SemaphoreType.DMA((copies,))],
        compiler_params=pltpu.CompilerParams(
            collective_id=0, has_side_effects=True, vmem_limit_bytes=63 << 20
        ),
        name="block_layer",
    )(*ins.values())
    results = placed(results)
    *large, norm_one, norm_two, table, rate = results
    return (*large, norm_one.reshape(rows), norm_two.reshape(rows), table, rate.reshape(2))


highest = lax.Precision.HIGHEST


def from_behind(value, axis, by):
    size = lax.axis_size(axis)
    pairs = [(i, i + by) for i in range(size) if 0 <= i + by < size]
    return lax.ppermute(value, axis, pairs)


def prefix(value, axis, join, neutral, backward):
    count = lax.axis_size(axis)
    place = lax.axis_index(axis)
    ahead = count - 1 - place if backward else place
    gathered = jax.tree.map(
        lambda a, kind: lax.all_gather(a.astype(kind), axis), value, (jnp.bfloat16, jnp.bfloat16)
    )
    state = jax.tree.map(lambda a, e: jnp.zeros_like(a) + jnp.asarray(e, a.dtype), value, neutral)

    def one(lap, state):
        source = count - 1 - lap if backward else lap
        return join(
            state,
            jax.tree.map(
                lambda a, own: lax.dynamic_index_in_dim(a, source, 0, False).astype(own.dtype),
                gathered,
                value,
            ),
        )

    return lax.fori_loop(0, ahead, one, state)


def bucket_onehot(window_len, bucket_count):
    distance = np.arange(window_len)
    scaled = np.floor(np.log(np.maximum(distance, 1) / 16.0) / np.log(8.0) * 16.0)
    larger = np.minimum(16 + np.maximum(scaled, 0), bucket_count - 1)
    bucket = np.where(distance < 16, distance, larger).astype(np.int32)
    return (bucket[:, None] == np.arange(bucket_count)[None, :]).astype(np.float32)


def skewed(extended, row_count, col_count):
    head_count = extended.shape[0]
    span = row_count + col_count
    flipped = jnp.concatenate(
        [extended[:, ::-1], jnp.zeros((head_count, 1), extended.dtype)], axis=1
    )
    tiled = jnp.broadcast_to(flipped[:, None, :], (head_count, row_count, span)).reshape(
        head_count, row_count * span
    )
    tiled = tiled[:, : row_count * (span - 1)].reshape(head_count, row_count, span - 1)
    return tiled[:, :, row_count - 1 : row_count - 1 + col_count]


def rms_scale(values, gain):
    return values * lax.rsqrt(jnp.mean(values * values, axis=-1, keepdims=True) + epsilon) * gain


def times_transposed(left, right):
    return lax.dot_general(
        left, right, (((1,), (1,)), ((), ())), preferred_element_type=jnp.float32
    )


def transposed_times(left, right):
    return lax.dot_general(
        left, right, (((0,), (0,)), ((), ())), preferred_element_type=jnp.float32
    )


def compose(earlier, later):
    return (earlier[0] * later[0], later[0][:, None, None] * earlier[1] + later[1])


def group_state(carried_state, query_c, key_c, value_c, seg_group, seg_before, decay_rate):
    length_c = query_c.shape[0]
    position = jnp.arange(length_c).astype(jnp.float32)
    distance = position[:, None] - position[None, :]
    inside = (distance >= 0) & (seg_group[:, None] == seg_group[None, :])
    decay_w = jnp.where(
        inside[None], jnp.exp(-decay_rate[:, None, None] * jnp.maximum(distance, 0.0)[None]), 0.0
    )
    affinity = jnp.einsum("ihd,jhd->hij", query_c, key_c, precision=highest) * state_scale
    readout = jnp.einsum("hij,jhd->ihd", affinity * decay_w, value_c, precision=highest)
    live_mask = (seg_group == seg_before).astype(jnp.float32)
    entering = (
        jnp.exp(-decay_rate[None, :] * (position[:, None] + 1.0)) * live_mask[:, None] * state_scale
    )
    readout = (
        readout
        + jnp.einsum("ihd,hde->ihe", query_c, carried_state, precision=highest)
        * entering[:, :, None]
    )
    keeping = (seg_group == seg_group[-1]).astype(jnp.float32)
    leaving = (
        jnp.exp(-decay_rate[None, :] * (length_c - 1.0 - position[:, None])) * keeping[:, None]
    )
    carry_keep = jnp.exp(-decay_rate * length_c) * (seg_group[-1] == seg_before).astype(jnp.float32)
    updated = jnp.einsum("jhd,jhe->hde", key_c * leaving[:, :, None], value_c, precision=highest)
    updated = updated + carry_keep[:, None, None] * carried_state
    return (updated, readout)


def local_states(query_f, key_f, value_f, decay_rate, seg_block, seg_before):
    block_len, head_count, head_width = query_f.shape
    count = block_len // WIN
    items = (
        query_f.reshape(count, WIN, head_count, head_width),
        key_f.reshape(count, WIN, head_count, head_width),
        value_f.reshape(count, WIN, head_count, head_width),
        seg_block.reshape(count, WIN),
    )

    def step(carry, item):
        carried_state, prior = carry
        updated, readout = group_state(
            carried_state, item[0], item[1], item[2], item[3], prior, decay_rate
        )
        return ((updated, item[3][-1]), readout)

    start_carry = (jnp.zeros((head_count, head_width, head_width), jnp.float32), seg_before)
    (final_state, _), readouts = lax.scan(step, start_carry, items)
    return (readouts.reshape(block_len, head_count, head_width), final_state)


def general_shards(
    tokens,
    cotangent,
    segments,
    w_query,
    w_key,
    w_value,
    w_out,
    w_up,
    w_down,
    norm_one,
    norm_two,
    rel_table,
    decay_rate,
):
    heads_here = rel_table.shape[0]
    head_width = HD
    tok_here = tokens.shape[0]
    block_len = lax.axis_size("head") * tok_here
    block_count = block_len // WIN
    pair_width = heads_here * head_width
    scale = 1.0 / math.sqrt(head_width)
    gathered = (
        lax.all_gather(w_query, ("head", "seq"), axis=0, tiled=True),
        lax.all_gather(w_key, ("head", "seq"), axis=0, tiled=True),
        lax.all_gather(w_value, ("head", "seq"), axis=0, tiled=True),
        lax.all_gather(w_out, ("head", "seq"), axis=0, tiled=True),
        lax.all_gather(w_up, ("head", "seq"), axis=0, tiled=True),
        lax.all_gather(w_down, ("head", "seq"), axis=0, tiled=True),
        lax.all_gather(norm_one, ("head", "seq"), axis=0, tiled=True),
        lax.all_gather(norm_two, ("head", "seq"), axis=0, tiled=True),
    )
    full_query, full_key, full_value, full_out, full_up, full_down, gain_one, gain_two = gathered
    inputs_f = tokens.astype(jnp.float32)
    scaled_one, norm_back_one = jax.vjp(rms_scale, inputs_f, gain_one.astype(jnp.float32))
    normed = scaled_one.astype(jnp.bfloat16)
    projected = jnp.stack(
        [
            jnp.dot(normed, full_query, preferred_element_type=jnp.float32),
            jnp.dot(normed, full_key, preferred_element_type=jnp.float32),
            jnp.dot(normed, full_value, preferred_element_type=jnp.float32),
        ]
    ).astype(jnp.bfloat16)
    regrouped = lax.all_to_all(projected, "head", split_axis=2, concat_axis=1, tiled=True)
    prior_pairs = from_behind(regrouped[1:, block_len - WIN :], "seq", 1)
    pairs_ext = jnp.concatenate([prior_pairs, regrouped[1:]], axis=1)
    query_heads = regrouped[0].reshape(block_len, heads_here, head_width)
    key_ext = pairs_ext[0].reshape(block_len + WIN, heads_here, head_width)
    value_ext = pairs_ext[1].reshape(block_len + WIN, heads_here, head_width)
    block_base = lax.axis_index("seq") * block_len
    padded_segs = jnp.concatenate([jnp.full((WIN,), -1, jnp.int32), segments])
    seg_ext = lax.dynamic_slice_in_dim(padded_segs, block_base, block_len + WIN, 0)
    seg_block = seg_ext[WIN:]
    seg_before = seg_ext[WIN - 1]
    onehot_table = jnp.asarray(bucket_onehot(WIN, BUCKETS))
    by_distance = jnp.dot(rel_table, onehot_table.T, precision=highest)
    bias_ext = jnp.concatenate(
        [
            jnp.zeros((heads_here, WIN - 1), jnp.float32),
            by_distance,
            jnp.zeros((heads_here, WIN), jnp.float32),
        ],
        axis=1,
    )
    bias_full, skew_back = jax.vjp(lambda extended: skewed(extended, WIN, 2 * WIN), bias_ext)
    row_pos = jnp.arange(WIN, dtype=jnp.int32)[:, None]
    col_pos = jnp.arange(2 * WIN, dtype=jnp.int32)[None, :]
    near = (row_pos - col_pos + WIN >= 0) & (row_pos - col_pos + WIN < WIN)

    def block_inputs(number):
        start = number * WIN
        query_b = lax.dynamic_slice_in_dim(query_heads, start, WIN, 0)
        key_b = lax.dynamic_slice_in_dim(key_ext, start, 2 * WIN, 0)
        value_b = lax.dynamic_slice_in_dim(value_ext, start, 2 * WIN, 0)
        seg_q = lax.dynamic_slice_in_dim(seg_block, start, WIN, 0)
        seg_k = lax.dynamic_slice_in_dim(seg_ext, start, 2 * WIN, 0)
        visible = near & (seg_q[:, None] == seg_k[None, :])
        raw = jnp.einsum("ihd,jhd->hij", query_b, key_b, preferred_element_type=jnp.float32) * scale
        scores = jnp.where(visible[None], raw + bias_full, negative)
        return (query_b, key_b, value_b, scores)

    def forward_block(number):
        query_b, key_b, value_b, scores = block_inputs(number)
        top_score = jnp.max(scores, axis=-1, keepdims=True)
        exp_scores = jnp.exp(scores - top_score)
        total_mass = jnp.sum(exp_scores, axis=-1, keepdims=True)
        softmax_w = exp_scores / total_mass
        attended_b = jnp.einsum(
            "hij,jhd->ihd",
            softmax_w.astype(jnp.bfloat16),
            value_b,
            preferred_element_type=jnp.float32,
        )
        return (attended_b, (top_score + jnp.log(total_mass))[..., 0])

    numbers = jnp.arange(block_count, dtype=jnp.int32)
    attended_blocks, log_mass = lax.map(forward_block, numbers)
    attended = attended_blocks.reshape(block_len, heads_here, head_width)
    query_f = query_heads.astype(jnp.float32)
    key_f = key_ext[WIN:].astype(jnp.float32)
    value_f = value_ext[WIN:].astype(jnp.float32)

    def states_here(query_a, key_a, value_a, rates):
        return local_states(query_a, key_a, value_a, rates, seg_block, seg_before)

    (readout_local, state_local), states_back = jax.vjp(
        states_here, query_f, key_f, value_f, decay_rate
    )
    position = jnp.arange(block_len).astype(jnp.float32)
    live_mask = (seg_block == seg_before).astype(jnp.float32)
    enter_decay = (
        jnp.exp(-decay_rate[None, :] * (position[:, None] + 1.0)) * live_mask[:, None] * state_scale
    )
    carry_keep = jnp.exp(-decay_rate * block_len) * (seg_block[-1] == seg_before).astype(
        jnp.float32
    )
    identity = (jnp.ones_like(carry_keep), jnp.zeros_like(state_local))
    carried = prefix((carry_keep, state_local), "seq", compose, identity, False)
    carry_in = carried[1]
    carry_term = (
        jnp.einsum("ihd,hde->ihe", query_f, carry_in, precision=highest) * enter_decay[:, :, None]
    )
    mixed_heads = (
        (attended + readout_local + carry_term).astype(jnp.bfloat16).reshape(block_len, pair_width)
    )
    mixed_tok = lax.all_to_all(mixed_heads, "head", split_axis=0, concat_axis=1, tiled=True)
    resid_one = inputs_f + jnp.dot(mixed_tok, full_out, preferred_element_type=jnp.float32)
    scaled_two, norm_back_two = jax.vjp(rms_scale, resid_one, gain_two.astype(jnp.float32))
    normed_two = scaled_two.astype(jnp.bfloat16)
    up_proj = jnp.dot(normed_two, full_up, preferred_element_type=jnp.float32)
    activated, gelu_back = jax.vjp(jax.nn.gelu, up_proj)
    act_low = activated.astype(jnp.bfloat16)
    output = (resid_one + jnp.dot(act_low, full_down, preferred_element_type=jnp.float32)).astype(
        jnp.bfloat16
    )
    back_query, back_key, back_value = (full_query, full_key, full_value)
    back_out, back_up, back_down = (full_out, full_up, full_down)
    grad_down_w = transposed_times(act_low, cotangent)
    act_grad = times_transposed(cotangent, back_down)
    up_grad = gelu_back(act_grad)[0].astype(jnp.bfloat16)
    grad_up_w = transposed_times(normed_two, up_grad)
    normed_two_grad = times_transposed(up_grad, back_up)
    resid_grad_n, grad_gain_two = norm_back_two(normed_two_grad)
    resid_grad = cotangent.astype(jnp.float32) + resid_grad_n
    attn_grad = resid_grad.astype(jnp.bfloat16)
    grad_out_w = transposed_times(mixed_tok, attn_grad)
    mixed_grad = times_transposed(attn_grad, back_out).astype(jnp.bfloat16)
    heads_grad = lax.all_to_all(mixed_grad, "head", split_axis=1, concat_axis=0, tiled=True)
    heads_grad3 = heads_grad.reshape(block_len, heads_here, head_width)

    def backward_block(item):
        number, log_block = item
        query_b, key_b, value_b, scores = block_inputs(number)
        out_grad_b = lax.dynamic_slice_in_dim(heads_grad3, number * WIN, WIN, 0)
        softmax_w = jnp.exp(scores - log_block[..., None])
        prob_grad = jnp.einsum(
            "ihd,jhd->hij", out_grad_b, value_b, preferred_element_type=jnp.float32
        )
        score_grad = softmax_w * (
            prob_grad - jnp.sum(softmax_w * prob_grad, axis=-1, keepdims=True)
        )
        score_low = score_grad.astype(jnp.bfloat16)
        query_grad_b = (
            jnp.einsum("hij,jhd->ihd", score_low, key_b, preferred_element_type=jnp.float32) * scale
        )
        key_grad_b = (
            jnp.einsum("hij,ihd->jhd", score_low, query_b, preferred_element_type=jnp.float32)
            * scale
        )
        value_grad_b = jnp.einsum(
            "hij,ihd->jhd",
            softmax_w.astype(jnp.bfloat16),
            out_grad_b,
            preferred_element_type=jnp.float32,
        )
        ext_grad_b = skew_back(score_low.astype(jnp.float32))[0]
        return (query_grad_b, key_grad_b, value_grad_b, ext_grad_b)

    query_grads, key_grads, value_grads, ext_grads = lax.map(backward_block, (numbers, log_mass))
    query_grad_att = query_grads.reshape(block_len, heads_here, head_width)

    def fold_pairs(pieces):
        zero_edge = jnp.zeros_like(pieces[:1, :WIN])
        return jnp.concatenate([pieces[:, :WIN], zero_edge], axis=0) + jnp.concatenate(
            [zero_edge, pieces[:, WIN:]], axis=0
        )

    key_folded = fold_pairs(key_grads)
    value_folded = fold_pairs(value_grads)
    sent_pairs = jnp.stack([key_folded[0], value_folded[0]]).reshape(2, WIN, pair_width)
    received = from_behind(sent_pairs.astype(jnp.bfloat16), "seq", -1).astype(sent_pairs.dtype)
    tail_pairs = jnp.concatenate(
        [jnp.zeros((2, block_len - WIN, pair_width), jnp.float32), received], axis=1
    )
    tail_pairs = tail_pairs.reshape(2, block_len, heads_here, head_width)
    key_grad_att = key_folded[1:].reshape(block_len, heads_here, head_width) + tail_pairs[0]
    value_grad_att = value_folded[1:].reshape(block_len, heads_here, head_width) + tail_pairs[1]
    heads_grad_f = heads_grad3.astype(jnp.float32)
    grad_local = jnp.einsum(
        "ihd,ihe->hde", query_f * enter_decay[:, :, None], heads_grad_f, precision=highest
    )
    back_chain = prefix((carry_keep, grad_local), "seq", compose, identity, True)
    carry_out_grad = back_chain[1]
    query_grad_s, key_grad_s, value_grad_s, rate_grad_s = states_back(
        (heads_grad_f, carry_out_grad)
    )
    query_grad_c = (
        jnp.einsum("ihe,hde->ihd", heads_grad_f, carry_in, precision=highest)
        * enter_decay[:, :, None]
    )
    rate_grad_c = -jnp.sum(heads_grad_f * carry_term * (position[:, None, None] + 1.0), axis=(0, 2))
    rate_grad_a = -block_len * carry_keep * jnp.sum(carry_out_grad * carry_in, axis=(1, 2))
    rate_grad = rate_grad_s + rate_grad_c + rate_grad_a
    query_grad = query_grad_att + query_grad_s + query_grad_c
    key_grad = key_grad_att + key_grad_s
    value_grad = value_grad_att + value_grad_s
    triple_grad = (
        jnp.stack([query_grad, key_grad, value_grad])
        .reshape(3, block_len, pair_width)
        .astype(jnp.bfloat16)
    )
    token_grads = lax.all_to_all(triple_grad, "head", split_axis=1, concat_axis=2, tiled=True)
    grad_query_w = transposed_times(normed, token_grads[0])
    grad_key_w = transposed_times(normed, token_grads[1])
    grad_value_w = transposed_times(normed, token_grads[2])
    normed_grad = (
        times_transposed(token_grads[0], back_query)
        + times_transposed(token_grads[1], back_key)
        + times_transposed(token_grads[2], back_value)
    )
    input_grad_n, grad_gain_one = norm_back_one(normed_grad)
    input_grad = (resid_grad + input_grad_n).astype(jnp.bfloat16)
    ext_total = jnp.sum(ext_grads, axis=0)
    table_grad = jnp.dot(ext_total[:, WIN - 1 : 2 * WIN - 1], onehot_table, precision=highest)
    table_grad, rate_grad = lax.psum((table_grad, rate_grad), "seq")
    summed = (
        lax.psum_scatter(grad_query_w, ("head", "seq"), scatter_dimension=0, tiled=True),
        lax.psum_scatter(grad_key_w, ("head", "seq"), scatter_dimension=0, tiled=True),
        lax.psum_scatter(grad_value_w, ("head", "seq"), scatter_dimension=0, tiled=True),
        lax.psum_scatter(grad_out_w, ("head", "seq"), scatter_dimension=0, tiled=True),
        lax.psum_scatter(grad_up_w, ("head", "seq"), scatter_dimension=0, tiled=True),
        lax.psum_scatter(grad_down_w, ("head", "seq"), scatter_dimension=0, tiled=True),
        lax.psum_scatter(grad_gain_one, ("head", "seq"), scatter_dimension=0, tiled=True),
        lax.psum_scatter(grad_gain_two, ("head", "seq"), scatter_dimension=0, tiled=True),
    )
    grad_query, grad_key, grad_value, grad_out, grad_up, grad_down, grad_norm_one, grad_norm_two = (
        summed
    )
    return (
        output,
        input_grad,
        grad_query,
        grad_key,
        grad_value,
        grad_out,
        grad_up,
        grad_down,
        grad_norm_one,
        grad_norm_two,
        table_grad,
        rate_grad,
    )


def solution(mesh):
    devices = mesh.shape["head"] * mesh.shape["seq"]
    tiled = mesh.shape["head"] == 4 and 1024 // devices == 32
    return jax.shard_map(
        shards if tiled else general_shards,
        mesh=mesh,
        in_specs=(
            P(("seq", "head"), None),
            P(("seq", "head"), None),
            P(),
            P(("head", "seq"), None),
            P(("head", "seq"), None),
            P(("head", "seq"), None),
            P(("head", "seq"), None),
            P(("head", "seq"), None),
            P(("head", "seq"), None),
            P(("head", "seq")),
            P(("head", "seq")),
            P("head", None),
            P("head"),
        ),
        out_specs=(
            P(("seq", "head"), None),
            P(("seq", "head"), None),
            P(("head", "seq"), None),
            P(("head", "seq"), None),
            P(("head", "seq"), None),
            P(("head", "seq"), None),
            P(("head", "seq"), None),
            P(("head", "seq"), None),
            P(("head", "seq")),
            P(("head", "seq")),
            P("head", None),
            P("head"),
        ),
        check_vma=False,
    )
```

```python
import functools
import math

import jax
import jax.numpy as jnp
import numpy as np
from jax import lax
from jax.experimental import pallas as pl
from jax.experimental.pallas import tpu as pltpu
from jax.sharding import PartitionSpec as P

HD = 128
BUCKETS = 32
WIN = 512
TILE = 256

epsilon = 1e-06
negative = -1e30
state_scale = 1.0 / 1024.0
MESH = pl.DeviceIdType.MESH
f32 = jnp.float32
bf16 = jnp.bfloat16


def dot(a, b):
    return jnp.dot(a, b, preferred_element_type=f32)


def dot_t(a, b):
    return lax.dot_general(a, b, (((1,), (1,)), ((), ())), preferred_element_type=f32)


def t_dot(a, b):
    return lax.dot_general(a, b, (((0,), (0,)), ((), ())), preferred_element_type=f32)


class Place:
    def __init__(self):
        self.h = lax.axis_index("head")
        self.s = lax.axis_index("seq")
        self.n = lax.axis_size("seq")
        self.nz = self.n // 2
        self.z = self.s // 2
        self.core = self.s % 2
        x, y = self.h % 2, self.h // 2
        self.heads = [2 * y + 1 - x, 2 * (1 - y) + x, 2 * (1 - y) + 1 - x]

    def head_dev(self, k):
        return (self.heads[k], self.s)

    def z_to(self, k):
        return ((self.z + k) % self.nz) * 2 + self.core

    def z_from(self, k):
        return ((self.z + self.nz - k) % self.nz) * 2 + self.core

    def z_dev(self, k):
        return (self.h, self.z_to(k))

    def other(self):
        return self.z * 2 + 1 - self.core

    def core_dev(self):
        return (self.h, self.other())

    def seq_dev(self, by):
        return (self.h, (self.s + self.n + by) % self.n)


def greet(devices):
    barrier = pltpu.get_barrier_semaphore()
    for device in devices:
        pl.semaphore_signal(barrier, inc=1, device_id=device, device_id_type=MESH)
    pl.semaphore_wait(barrier, len(devices))


class Sends:
    def __init__(self, send_sems, recv_sems):
        self.send_sems, self.recv_sems = send_sems, recv_sems
        self.sent_at, self.recv_at, self.all = 0, 0, []

    def claim(self, count):
        self.recv_at += count
        return self.recv_at - count

    def copy(self, src, dst, device, send, recv):
        return pltpu.make_async_remote_copy(
            src_ref=src,
            dst_ref=dst,
            send_sem=self.send_sems.at[send],
            recv_sem=self.recv_sems.at[recv],
            device_id=device,
            device_id_type=MESH,
        )

    def put(self, src, dst, device, recv=None):
        recv = self.claim(1) if recv is None else recv
        copy = self.copy(src, dst, device, self.sent_at, recv)
        self.sent_at += 1
        self.all.append(copy)
        copy.start()
        return copy

    def sent(self, copies):
        for copy in copies:
            copy.wait_send()
        self.all = [c for c in self.all if not any(c is d for d in copies)]

    def finish(self):
        for copy in self.all:
            copy.wait_send()


class Line:
    def __init__(self, me, sends, place):
        self.me, self.sends, self.place = me, sends, place
        z = me.z
        inner = (z * (3 - z)) // 2
        self.near, self.next = 1 + z % 2, 2 * (1 - z % 2) + z // 2
        self.order = [self.near, self.next, 6 - z - self.near - self.next]
        self.piece, self.end = z + inner * (3 - 2 * z), 3 * (1 - z % 2)
        self.base = sends.claim(4)
        self.copies = []

    def put(self, src, chip, to):
        me = self.me
        device = (me.h, 2 * to + me.core)
        self.copies.append(self.sends.put(src, self.place(chip), device, self.base + chip))

    def start(self, own):
        for to in (self.near, self.next):
            self.put(own, self.me.z, to)

    def wait(self, i):
        chip = self.order[i]
        ref = self.place(chip)
        device = (self.me.h, 2 * chip + self.me.core)
        self.sends.copy(ref, ref, device, 0, self.base + chip).wait_recv()
        return ref

    def relay(self):
        ref = self.wait(0)
        self.put(self.place(self.piece), self.piece, self.end)
        return ref


class Square:
    def __init__(self, me, sends, block):
        self.me, self.sends, self.block = me, sends, block

    def start(self, own):
        me = self.me
        self.got = [
            self.sends.put(own, self.block(me.h, None), me.head_dev(k)) for k in range(2)
        ]
        self.halves = []

    def relay(self):
        me = self.me
        for k in range(2):
            self.got[k].wait_recv()
            ref = self.block(me.heads[k], k)
            self.halves.append(self.sends.put(ref, ref, me.head_dev(1 - k)))

    def last(self):
        for copy in self.halves:
            copy.wait_recv()


class SquareSum:
    def __init__(self, me, sends, give, land):
        self.me, self.sends, self.give, self.land = me, sends, give, land
        self.half = give(2).shape[0] // 2
        self.parts = [pl.ds(0, self.half), pl.ds(self.half, self.half)]
        self.copies = []

    def put(self, block, piece, to):
        at = self.parts[piece]
        device = self.me.head_dev(to)
        copy = self.sends.put(self.give(block).at[at], self.land(block).at[at], device)
        self.copies.append(copy)
        return copy

    def first(self):
        self.halves = [self.put(2, k, k) for k in range(2)]

    def early(self, k):
        self.put(k, k, k)

    def second(self):
        land = self.land(2)
        for k in range(2):
            self.halves[k].wait_recv()
            give = self.give(1 - k)

            def add(i, _):
                at = pl.ds(pl.multiple_of(k * self.half + i * 32, 32), 32)
                give[at] = (give[at].astype(f32) + land[at].astype(f32)).astype(bf16)
                return 0

            lax.fori_loop(0, self.half // 32, add, 0, unroll=True)
        for k in range(2):
            self.put(k, 1 - k, k)

    def last(self):
        for copy in self.copies:
            if not any(copy is half for half in self.halves):
                copy.wait_recv()


def rms(x):
    return lax.rsqrt(jnp.mean(x * x, axis=-1, keepdims=True) + epsilon)


LOG2E = math.log2(math.e)
KEY_SCALE = LOG2E / math.sqrt(HD)


def bucket_starts():
    distance = np.arange(WIN)
    scaled = np.floor(np.log(np.maximum(distance, 1) / 16.0) / np.log(8.0) * 16.0)
    larger = np.minimum(16 + np.maximum(scaled, 0), BUCKETS - 1)
    bucket = np.where(distance < 16, distance, larger).astype(np.int32)
    return [int(np.argmax(bucket == b)) for b in range(BUCKETS)]


STARTS = bucket_starts()


def grid_of(axis, shape=(TILE, TILE)):
    return lax.broadcasted_iota(jnp.int32, shape, axis)


def column(row):
    eye = grid_of(0) == grid_of(1)
    return jnp.sum(jnp.where(eye, row, 0.0), axis=1, keepdims=True)


class Segs:
    def __init__(self, me, seg_ref, rows, cols):
        total = 4 * me.n
        self.rows, self.cols = rows, cols

        def row_at(offset):
            at = 2 * ((4 * me.s + total + offset) % total)
            pair = [seg_ref[pl.ds(at + i, 1)].astype(f32) for i in range(2)]
            return jnp.concatenate(pair, axis=1)

        for j in range(6):
            row = row_at(j - 2)
            rows[j] = row
            if j >= 2:
                cols[j - 2] = column(row)
        last = lambda offset: row_at(offset)[:, TILE - 1 : TILE]
        self.last = [last(j - 2) for j in range(6)]
        same = lambda a, b: (a == b).astype(f32)
        self.keep = [same(self.last[t + 2], self.last[t + 1]) for t in range(4)]
        self.keep_before = same(last(-1), last(-5))
        self.keep_after = same(last(7), last(3))

    def live(self, t):
        return (self.cols[t] == self.last[t + 1]).astype(f32)

    def kept(self, t):
        return (self.cols[t] == self.last[t + 2]).astype(f32)


def fill_tables(table_ref, decay_ref, near, far, decay, enter, leave):
    gap = grid_of(0) - grid_of(1)
    place = grid_of(0, (TILE, 1)).astype(f32)
    for head in range(2):
        rate = decay_ref[0, head]
        for out, shift in ((near, 0), (far, TILE)):
            bias = jnp.full((TILE, TILE), table_ref[head, 0] * LOG2E, f32)
            for b in range(1, BUCKETS):
                bias = jnp.where(gap + shift >= STARTS[b], table_ref[head, b] * LOG2E, bias)
            out[head] = jnp.where(gap + shift >= 0, bias, negative)
        fall = jnp.exp(-rate * jnp.maximum(gap, 0).astype(f32)) * state_scale
        decay[head] = jnp.where(gap >= 0, fall, 0.0)
        enter[head] = jnp.exp(-rate * (place + 1.0)) * state_scale
        leave[head] = jnp.exp(-rate * (TILE - 1.0 - place))


def power(rate, steps):
    return jnp.exp(jnp.full((1, HD), -rate * steps, f32))


def tile_scores(raw, head, t, table_ref, near, far, segs):
    col = segs.cols[t]
    same = [col == segs.rows[t + j] for j in range(3)]
    reach = grid_of(0) < grid_of(1)
    rest = table_ref[head, BUCKETS - 1] * LOG2E
    s0 = jnp.where(same[0] & reach, raw[:, :TILE] * KEY_SCALE + rest, negative)
    s1 = jnp.where(same[1], raw[:, TILE : 2 * TILE] * KEY_SCALE + far[head], negative)
    s2 = jnp.where(same[2], raw[:, 2 * TILE :] * KEY_SCALE + near[head], negative)
    return s0, s1, s2, same[2]


GELU_C = math.sqrt(2.0 / math.pi)
GELU_A = 0.044715


def part(i, size):
    return pl.ds(pl.multiple_of(i * size, size), size)


class Reduce:
    def __init__(self, me, sends, own, given, core_in, z_in, keep):
        self.me, self.sends = me, sends
        self.own, self.given, self.core_in, self.z_in, self.keep = own, given, core_in, z_in, keep
        self.width = keep.shape[-1]

    def start(self):
        self.core = self.sends.put(self.given, self.core_in, self.me.core_dev())

    def put(self, chunk, to, slot):
        me = self.me
        device = (me.h, 2 * to + me.core)
        src, dst = self.given.at[chunk], self.z_in.at[slot]
        self.copies.append(self.sends.put(src, dst, device, self.base + slot))

    def wait(self, slot):
        ref = self.z_in.at[slot]
        self.sends.copy(ref, ref, self.me.core_dev(), 0, self.base + slot).wait_recv()

    def join(self):
        me, lanes = self.me, pl.ds(0, self.width)
        z = me.z
        self.core.wait_recv()
        self.sends.sent([self.core])
        self.inner = (z * (3 - z)) // 2
        self.beside, self.across, self.far = z + 1 - 2 * (z % 2), (z + 2) % 4, 3 - z
        for chunk in (self.beside, self.across, self.far):

            def both(i, at):
                total = self.own[chunk, at, lanes] + self.core_in[chunk, at].astype(f32)
                self.given[chunk, at] = total.astype(bf16)

            each(128, 32, both)

        def mine(i, at):
            self.keep[at] = self.own[z, at, lanes] + self.core_in[z, at].astype(f32)

        each(128, 32, mine)

    def along(self):
        self.base, self.copies = self.sends.claim(3), []
        self.put(self.beside, self.beside, 0)

    def on(self):
        to = self.inner * self.across + (1 - self.inner) * self.beside
        self.put(self.across, to, 2 - self.inner)

    def late(self):
        @pl.when(self.inner == 1)
        def _():
            self.wait(2)

            def add(i, at):
                total = self.given[self.far, at].astype(f32) + self.z_in[2, at].astype(f32)
                self.given[self.far, at] = total.astype(bf16)

            each(128, 32, add)

        self.put(self.far, self.far, 2 - self.inner)

    def total(self):
        for slot in range(2):
            self.wait(slot)

        def more(i, at):
            self.keep[at] += self.z_in[0, at].astype(f32) + self.z_in[1, at].astype(f32)

        each(128, 32, more)

        @pl.when(self.inner == 0)
        def _():
            self.wait(2)

            def add(i, at):
                self.keep[at] += self.z_in[2, at].astype(f32)

            each(128, 32, add)


def each(count, step, body, unroll=4):
    def one(i, _):
        body(i, part(i, step))
        return 0

    lax.fori_loop(0, count // step, one, 0, unroll=unroll)


def whole_kernel(ins, outs, b, send_sems, recv_sems):
    me = Place()
    nz, n = me.nz, me.n
    rows, tok = ins.w_out.shape[0], ins.tokens.shape[0]
    peers = [me.head_dev(k) for k in range(3)]
    greet(
        peers
        + [me.seq_dev(k) for k in range(1, n)]
    )
    sends = Sends(send_sems, recv_sems)
    core_dev = me.core_dev()
    half = pl.ds(me.core * nz, nz)
    wide = 6 * HD

    first = []
    parts = (ins.w_query, ins.w_key, ins.w_value)
    for k in range(3):
        for j, w in enumerate(parts):
            src = w.at[:, part(me.heads[k], 256)]
            first.append(sends.put(src, b.a1.at[me.h, :, j * 256 : j * 256 + 256], peers[k]))

    def token_block(ref):
        def block(i, piece):
            if piece is None:
                return ref.at[part(i, tok)]
            return ref.at[part(2 * i + piece, tok // 2)]

        return block

    toks = Square(me, sends, token_block(b.x))
    toks.start(ins.tokens)
    first_up = []
    for k in range(3):
        src = ins.w_up.at[:, part(me.heads[k], 1024)]
        first_up.append(sends.put(src, b.u1.at[me.h], peers[k]))
    w_line = Line(me, sends, lambda z: b.wb.at[:, 2 * z + me.core])
    wo_line = Line(me, sends, lambda z: b.wo.at[me.h, 2 * z + me.core])
    up_line = Line(me, sends, lambda z: b.up.at[:, 2 * z + me.core])
    dn_line = Line(me, sends, lambda z: b.dn.at[2 * z + me.core])
    for j, w in enumerate(parts):
        b.a1[me.h, :, j * 256 : j * 256 + 256] = w[:, part(me.h, 256)]
    lane = lax.broadcasted_iota(jnp.int32, (8, 128), 1)
    line = lax.broadcasted_iota(jnp.int32, (8, 128), 0)
    group = 128 // rows
    gains = jnp.zeros((8, 128), f32)
    for j, gain in enumerate((ins.norm_one, ins.norm_two)):
        row = jnp.concatenate([gain[...].astype(f32)] * group, axis=1)
        gains = jnp.where((lane // rows == me.s % group) & (line == j), row, gains)
    b.gains[me.h] = gains
    own = b.gains.at[me.h]
    first_gains = [sends.put(own, own, peers[k]) for k in range(3)]
    for copy in first:
        copy.wait_recv()
    w_line.start(b.a1)
    w_c = [sends.put(b.a1, b.wb.at[:, me.s], core_dev)]
    b.wb[:, me.s] = b.a1[...]
    b.x[part(me.h, tok)] = ins.tokens[...]
    b.u1[me.h] = ins.w_up[:, part(me.h, 1024)]
    b.wo[me.h, me.s] = ins.w_out[...]
    b.dn[me.s] = ins.w_down[...]
    b.cots[part(me.h, tok)] = ins.cotangent[...]
    w_c.append(sends.put((ref := w_line.relay()), ref, core_dev))
    for copy in first_gains:
        copy.wait_recv()
    b.all_gains[me.s] = b.gains[...]
    all_gains = []
    for k in range(1, n):
        all_gains.append(sends.put(b.gains, b.all_gains.at[me.s], me.seq_dev(k)))
    own = b.wo.at[me.h, me.s]
    wo_line.start(ins.w_out)
    wo_c = [sends.put(ins.w_out, own, core_dev)]
    toks.relay()
    cots = Square(me, sends, token_block(b.cots))
    cots.start(ins.cotangent)
    segs = Segs(me, ins.segments, b.rows, b.cols)
    fill_tables(ins.table, ins.decay, b.near, b.far, b.decay, b.enter, b.leave)
    for i in (1, 2):
        ref = w_line.wait(i)
        w_c.append(sends.put(ref, ref, core_dev))
    for copy in first_up:
        copy.wait_recv()
    up_line.start(b.u1)
    up_c = [sends.put(b.u1, b.up.at[:, me.s], core_dev)]
    b.up[:, me.s] = b.u1[...]
    wo_c.append(sends.put((ref := wo_line.relay()), ref, core_dev))
    for copy in w_c:
        copy.wait_recv()
    for copy in all_gains:
        copy.wait_recv()
    lanes = []
    for h in range(4):
        for s in range(0, n, group):
            lanes.append(sum(b.all_gains[s + i, h] for i in range(group)))
    gains = jnp.concatenate(lanes, axis=1)
    gain_one, gain_two = gains[0:1], gains[1:2]
    toks.last()
    for pair in (2, 0):

        def norm_one(i, _):
            at = pl.ds(pair * tok + i * 32, 32)
            x = b.x[at].astype(f32)
            b.hall[at] = (x * rms(x) * gain_one).astype(bf16)

        each(2 * tok, 32, norm_one)

        for t in (pair, pair + 1):
            at = pl.ds(t * tok, tok)
            for j in range(3):
                w = b.wb[:, :, :, j * 256 : j * 256 + 256].reshape(1024, 256)
                out = dot(b.hall[at], w).astype(bf16)
                for head in range(2):
                    mine = out[:, head * HD : head * HD + HD]
                    if j == 0:
                        b.q[head, at] = mine
                    else:
                        b.kvx[2 * (j - 1) + head, pl.ds((t + 2) * tok, tok)] = mine
        if pair == 2:
            halo = sends.put(b.kvx.at[:, 4 * TILE :], b.kvx.at[:, : 2 * TILE], me.seq_dev(1))
    sends.sent(toks.halves)

    falls = [power(ins.decay[0, head], float(TILE)) for head in range(2)]
    for head in range(2):
        state = jnp.zeros((HD, HD), f32)
        for t in range(4):
            at = pl.ds((t + 2) * TILE, TILE)
            key = (b.kvx[head, at].astype(f32) * (b.leave[head] * segs.kept(t))).astype(bf16)
            add = t_dot(key, b.kvx[2 + head, at])
            b.local[4 * head + t] = add
            state = falls[head] * segs.keep[t] * state + add
        b.sent[head] = state.astype(bf16)
    carry = [sends.put(b.sent, b.got.at[k - 1], me.seq_dev(k)) for k in (1, 2)]
    for i in (1, 2):
        ref = wo_line.wait(i)
        wo_c.append(sends.put(ref, ref, core_dev))
    cots.relay()
    for copy in wo_c:
        copy.wait_recv()

    def wo_block(i, piece):
        if piece is None:
            return b.wo.at[i, half]
        return b.wo.at[i, pl.ds(me.core * nz + piece * (nz // 2), nz // 2)]

    wo_square = Square(me, sends, wo_block)
    wo_square.start(b.wo.at[me.h, half])

    def forward(index, base):
        head, t = index // 2, base + index % 2
        at, own = part(t, TILE), part(t + 2, TILE)
        wide = pl.ds(pl.multiple_of(t * TILE, TILE), 3 * TILE)
        raw = dot_t(b.q[head, at], b.kvx[head, wide])
        s0, s1, s2, same = tile_scores(raw, head, t, ins.table, b.near, b.far, segs)
        top = jnp.maximum(jnp.maximum(s0, s1), s2).max(axis=1, keepdims=True)
        e0, e1, e2 = jnp.exp2(s0 - top), jnp.exp2(s1 - top), jnp.exp2(s2 - top)
        mass = (e0 + e1 + e2).sum(axis=1, keepdims=True)
        b.lse[4 * head + t] = top + jnp.log2(mass)
        mix = jnp.concatenate([e0.astype(bf16), e1.astype(bf16), e2.astype(bf16)], axis=1)
        att = dot(mix, b.kvx[2 + head, wide]) / mass
        weight = jnp.where(same, raw[:, 2 * TILE :] * b.decay[head], 0.0).astype(bf16)
        b.acc[head, at] = att + dot(weight, b.kvx[2 + head, own])
        return base

    lax.fori_loop(0, 4, forward, 2, unroll=2)
    halo.wait_recv()
    up_c.append(sends.put((ref := up_line.relay()), ref, core_dev))
    dn_line.start(ins.w_down)
    dn_c = [sends.put(ins.w_down, b.dn.at[me.s], core_dev)]
    wo_square.relay()
    lax.fori_loop(0, 4, forward, 0, unroll=2)
    wo_square.last()
    for k in range(3):
        piece = b.wo.at[me.heads[k], half]
        wo_c.append(sends.put(piece, piece, core_dev))
    for copy in carry:
        copy.wait_recv()
    for head in range(2):
        past = power(ins.decay[0, head], 4.0 * TILE) * segs.keep_before
        state = b.got[0, head].astype(f32) + past * b.got[1, head].astype(f32)
        for t in range(4):
            at = pl.ds(t * TILE, TILE)
            b.state[4 * head + t] = state
            reach = b.enter[head] * segs.live(t)
            y = b.acc[head, at] + dot(b.q[head, at], state.astype(bf16)) * reach
            b.dyt[2 * t + head] = y.astype(bf16)
            state = falls[head] * segs.keep[t] * state + b.local[4 * head + t]
    ys = []
    for k in range(3):
        for head in range(2):
            src = b.dyt.at[2 * me.heads[k] + head]
            ys.append(sends.put(src, b.ymix.at[:, part(2 * me.h + head, HD)], peers[k]))
    for head in range(2):
        b.ymix[:, part(2 * me.h + head, HD)] = b.dyt[2 * me.h + head]
    for copy in ys + wo_c[-3:]:
        copy.wait_recv()

    def out_tile(j, _):
        cols = part(j, 256)
        w = b.wo[:, :, :, cols].reshape(1024, 256)
        b.x1[:, cols] = ins.tokens[:, cols].astype(f32) + dot(b.ymix[...], w)
        return 0

    lax.fori_loop(0, 4, out_tile, 0, unroll=4)
    def norm_two(i, at):
        x = b.x1[at]
        b.h2all[pl.ds(pl.multiple_of(me.h * tok + i * 32, 32), 32)] = (x * rms(x) * gain_two).astype(bf16)
        b.base[at] = x

    each(tok, 32, norm_two)
    own = b.h2all.at[part(me.h, tok)]
    h2s = Square(me, sends, token_block(b.h2all))
    h2s.start(own)
    dn_c.append(sends.put((ref := dn_line.relay()), ref, core_dev))
    for i in (1, 2):
        ref = up_line.wait(i)
        up_c.append(sends.put(ref, ref, core_dev))
    for i in (1, 2):
        ref = dn_line.wait(i)
        dn_c.append(sends.put(ref, ref, core_dev))
    cots.last()
    for copy in up_c + dn_c:
        copy.wait_recv()
    dn2s = SquareSum(me, sends, lambda k: b.dn2s.at[k + 1], lambda k: b.dnin.at[k])
    for k in (0, 1, 2, -1):
        at = part(me.h if k < 0 else me.heads[k], tok)
        if k == 0:
            h2s.relay()
        elif k == 2:
            h2s.last()

        def hidden(j, _):
            cols = part(j, 256)
            u = dot(b.h2all[at], b.up[:, :, :, cols].reshape(1024, 256))
            dg = dot_t(b.cots[at], b.dn[pl.ds(2 * j, 2)].reshape(256, 1024))
            uu = u * u
            t = jnp.tanh(GELU_C * u * (1.0 + GELU_A * uu))
            b.x[at, cols] = (0.5 * u * (1.0 + t)).astype(bf16)
            slope = 0.5 * (1.0 + t) + (0.5 * GELU_C) * u * (1.0 - t * t) * (1.0 + 3.0 * GELU_A * uu)
            b.du[at, cols] = (slope * dg).astype(bf16)
            return 0

        lax.fori_loop(0, 4, hidden, 0, unroll=4)

        def back(j, _):
            w = b.up[j].reshape(256, 1024)
            b.dn2s[k + 1, :, part(j, 256)] = dot_t(b.du[at], w).astype(bf16)
            return 0

        lax.fori_loop(0, 4, back, 0, unroll=4)
        if k == 2:
            dn2s.first()
        elif k >= 0:
            dn2s.early(k)

        def ahead(j, _):
            cols = part(j, 256)
            out = dot(b.x[at], b.dn[:, :, cols].reshape(1024, 256))
            if k < 0:
                b.base[:, cols] = b.base[:, cols] + out
            else:
                b.outp[k, :, cols] = out.astype(bf16)
            return 0

        lax.fori_loop(0, 4, ahead, 0, unroll=4)

    def down_tile(j, _):
        b.tile[...] = t_dot(b.x[:, part(j, 256)], b.cots[...])
        b.own[j] = b.tile[part(me.core, 128)]
        b.given_a[j] = b.tile[part(1 - me.core, 128)].astype(bf16)
        return 0

    lax.fori_loop(0, 4, down_tile, 0, unroll=2)
    down = Reduce(me, sends, b.own, b.given_a, b.core_a, b.z_a, outs.grad_down)
    down.start()
    dn2s.second()
    down.join()
    down.along()
    down.on()

    def up_tile(j, _):
        b.tile[...] = t_dot(b.h2all[:, part(j, 256)], b.du[...])
        for z in range(nz):
            b.own[z, part(j, 32)] = b.tile[part(2 * z + me.core, 32)]
            b.given_b[z, part(j, 32)] = b.tile[part(2 * z + 1 - me.core, 32)].astype(bf16)
        return 0

    lax.fori_loop(0, 4, up_tile, 0, unroll=2)
    up = Reduce(me, sends, b.own, b.given_b, b.core_b, b.z_b, b.up_sum)
    up.start()
    dn2s.last()
    b.norms[...] = jnp.zeros_like(b.norms)

    def second_norm_back(i, at):
        dn2 = b.dn2s[0, at].astype(f32) + sum(b.dnin[k, at].astype(f32) for k in range(2))
        x = b.x1[at]
        scale = rms(x)
        n2 = x * scale
        b.norms[1:2] += jnp.sum(dn2 * n2, axis=0, keepdims=True)
        spread = dn2 * gain_two
        dx1 = ins.cotangent[at].astype(f32) + scale * (
            spread - n2 * jnp.mean(spread * n2, axis=-1, keepdims=True)
        )
        b.x1[at] = dx1
        b.da[at] = dx1.astype(bf16)

    each(tok, 32, second_norm_back)
    sends.sent(ys + dn2s.copies + dn_c[1:] + dn_line.copies)

    def back_tile(j, _):
        out = dot_t(b.da[...], b.wo[j].reshape(256, 1024)).astype(bf16)
        b.dyt[2 * j] = out[:, :HD]
        b.dyt[2 * j + 1] = out[:, HD:]
        return 0

    lax.fori_loop(0, 4, back_tile, 0, unroll=4)
    dys = []
    for k in range(3):
        src = b.dyt.at[pl.ds(2 * me.heads[k], 2)]
        dys.append(sends.put(src, b.dyh.at[:, part(me.h, tok)], peers[k]))
    b.dyh[:, part(me.h, tok)] = b.dyt[pl.ds(2 * me.h, 2)]
    down.late()
    for copy in dys:
        copy.wait_recv()
    outp = SquareSum(me, sends, lambda k: b.outp.at[k], lambda k: b.dnin.at[k])
    outp.first()
    outp.early(0)
    outp.early(1)
    for zero in (b.sums, b.dks, b.dvs, b.diag, b.below, b.rest):
        zero[...] = jnp.zeros_like(zero)
    for head in range(2):
        grad = jnp.zeros((HD, HD), f32)
        for t in range(3, -1, -1):
            at = pl.ds(t * TILE, TILE)
            query = (b.q[head, at].astype(f32) * (b.enter[head] * segs.live(t))).astype(bf16)
            add = t_dot(query, b.dyh[head, at])
            b.local[4 * head + t] = add
            grad = falls[head] * segs.keep[t] * grad + add
        b.sent_back[head] = grad.astype(bf16)
    carry = [sends.put(b.sent_back, b.got_back.at[k - 1], me.seq_dev(-k)) for k in (1, 2)]
    up.join()
    up.along()

    def grad_out_tile(j, _):
        b.tile[...] = t_dot(b.ymix[:, part(j, 256)], b.da[...])
        for z in range(nz):
            b.own[j, part(z, 32)] = b.tile[part(2 * z + me.core, 32)]
            b.dn[j, part(z, 32)] = b.tile[part(2 * z + 1 - me.core, 32)].astype(bf16)
        return 0

    lax.fori_loop(0, 4, grad_out_tile, 0, unroll=2)
    o_core = sends.put(b.dn.at[0:4], b.core_o, core_dev)

    gap = (grid_of(0) - grid_of(1)).astype(f32)

    def backward(index, base):
        head, t = index // 2, base + index % 2
        at, wide = part(t, TILE), pl.ds(pl.multiple_of(t * TILE, TILE), 3 * TILE)
        query, dy = b.q[head, at], b.dyh[head, at]
        keys, values = b.kvx[head, wide], b.kvx[2 + head, wide]
        raw = dot_t(query, keys)
        s0, s1, s2, same = tile_scores(raw, head, t, ins.table, b.near, b.far, segs)
        lse = b.lse[4 * head + t]
        p0, p1, p2 = jnp.exp2(s0 - lse), jnp.exp2(s1 - lse), jnp.exp2(s2 - lse)
        dp = dot_t(dy, values)
        dp0, dp1, dp2 = dp[:, :TILE], dp[:, TILE : 2 * TILE], dp[:, 2 * TILE :]
        mean = (p0 * dp0 + p1 * dp1 + p2 * dp2).sum(axis=1, keepdims=True)
        d0, d1, d2 = p0 * (dp0 - mean), p1 * (dp1 - mean), p2 * (dp2 - mean)
        b.diag[head] += d2[:HD, :HD] + d2[HD:, HD:]
        b.below[head] += d2[HD:, :HD] + d1[:HD, HD:]
        b.rest[head] += (
            (d0[:, :HD] + d0[:, HD:]).sum(axis=0, keepdims=True)
            + d1[:, :HD].sum(axis=0, keepdims=True)
            + d1[HD:, HD:].sum(axis=0, keepdims=True)
        )
        weight = jnp.where(same, b.decay[head], 0.0)
        mixed = weight * raw[:, 2 * TILE :]
        turn = weight * dp2
        slope = mixed * dp2 * gap
        b.sums[head] -= (slope[:, :HD] + slope[:, HD:]).sum(axis=0, keepdims=True)
        scale = 1.0 / math.sqrt(HD)
        x = jnp.concatenate(
            [(d0 * scale).astype(bf16), (d1 * scale).astype(bf16), (d2 * scale + turn).astype(bf16)],
            axis=1,
        )
        p = jnp.concatenate([p0.astype(bf16), p1.astype(bf16), (p2 + mixed).astype(bf16)], axis=1)
        b.acc[head, at] = dot(x, keys)
        b.dks[head, wide] += t_dot(x, query)
        b.dvs[head, wide] += t_dot(p, dy)
        return base

    lax.fori_loop(0, 4, backward, 0, unroll=2)
    outp.second()
    sends.sent(dys)
    for head in range(2):
        for i in range(2):
            at = pl.ds(i * TILE, TILE)
            b.dyt[2 * head + i] = b.dks[head, at].astype(bf16)
            b.dyt[4 + 2 * head + i] = b.dvs[head, at].astype(bf16)
    halo = sends.put(b.dyt, b.halo_in, me.seq_dev(-1))
    up.on()
    o_core.wait_recv()
    sends.sent(down.copies)
    for k in range(3):
        to = me.heads[k]

        def chip_sum(i, at):
            both = b.own[to, at] + b.core_o[to, at].astype(f32)
            b.given_a[k, at] = both.astype(bf16)

        each(128, 32, chip_sum)
    o_square = SquareSum(me, sends, lambda k: b.given_a.at[k], lambda k: b.o_in.at[k])
    o_square.first()
    o_square.early(0)
    o_square.early(1)

    def keep(i, at):
        b.o_keep[at] = b.own[me.h, at] + b.core_o[me.h, at].astype(f32)

    each(128, 32, keep)
    lax.fori_loop(0, 4, backward, 2, unroll=2)
    o_square.second()
    up.late()
    for copy in carry:
        copy.wait_recv()
    place = grid_of(0, (TILE, 1)).astype(f32)
    for head in range(2):
        past = power(ins.decay[0, head], 4.0 * TILE) * segs.keep_after
        grad = b.got_back[0, head].astype(f32) + past * b.got_back[1, head].astype(f32)
        fall = falls[head]
        total = jnp.zeros((1, HD), f32)
        for t in range(3, -1, -1):
            at = pl.ds(t * TILE, TILE)
            ext = pl.ds((t + 2) * TILE, TILE)
            low = grad.astype(bf16)
            state = b.state[4 * head + t]
            give = b.leave[head] * segs.kept(t)
            take = b.enter[head] * segs.live(t)
            query, key, value = b.q[head, at], b.kvx[head, ext], b.kvx[2 + head, ext]
            dq = dot_t(b.dyh[head, at], state.astype(bf16)) * take
            dv = dot(key, low) * give
            dk = dot_t(value, low) * give + b.dks[head, ext]
            slope = dq * query.astype(f32) * (place + 1.0)
            slope = slope + dv * value.astype(f32) * (TILE - 1.0 - place)
            crossing = fall * segs.keep[t]
            total = total - slope.sum(axis=0, keepdims=True)
            total = total - TILE * crossing * (grad * state).sum(axis=0, keepdims=True)
            dv = dv + b.dvs[head, ext]
            b.x[at, head * HD : head * HD + HD] = (b.acc[head, at] + dq).astype(bf16)
            if t >= 2:
                b.dks[head, ext], b.dvs[head, ext] = dk, dv
            else:
                for j, grad_tile in ((2, dk), (4, dv)):
                    b.x[at, (j + head) * HD : (j + head + 1) * HD] = grad_tile.astype(bf16)
            grad = b.local[4 * head + t] + crossing * grad
        b.sums[head] += total
    halo.wait_recv()
    for head in range(2):
        for t in (2, 3):
            at, ext = pl.ds(t * TILE, TILE), pl.ds((t + 2) * TILE, TILE)
            for j, ref in ((2, b.dks), (4, b.dvs)):
                total = ref[head, ext] + b.halo_in[2 * j - 4 + 2 * head + t - 2].astype(f32)
                b.x[at, (j + head) * HD : (j + head + 1) * HD] = total.astype(bf16)

    def grad_tile(j, _):
        tile = pl.ds(0, wide)
        b.tile[:, tile] = t_dot(b.hall[:, part(j, 256)], b.x[:, 0:wide])
        for z in range(nz):
            b.own[z, part(j, 32), tile] = b.tile[part(2 * z + me.core, 32), tile]
            b.dn[4 + z, part(j, 32), tile] = b.tile[part(2 * z + 1 - me.core, 32), tile].astype(bf16)
        return 0

    lax.fori_loop(0, 4, grad_tile, 0, unroll=2)
    grads = Reduce(me, sends, b.own, b.dn.at[4:8, :, 0:wide], b.core_q, b.z_q, b.q_sum)
    grads.start()
    backs = SquareSum(
        me, sends, lambda k: b.du.at[pl.ds(k * tok, tok)], lambda k: b.dn2s.at[k + 1]
    )
    for k in (2, 0, 1):
        at, to = part(me.heads[k], tok), pl.ds(k * tok, tok)

        def spread_back(j, _):
            w = b.wb[j, :, :, 0:wide].reshape(256, wide)
            b.du[to, part(j, 256)] = dot_t(b.x[at, 0:wide], w).astype(bf16)
            return 0

        lax.fori_loop(0, 4, spread_back, 0, unroll=4)
        if k == 2:
            backs.first()
        else:
            backs.early(k)

    outp.last()

    def output(i, at):
        total = b.base[at] + sum(b.dnin[k, at].astype(f32) for k in range(2))
        outs.output[at] = total.astype(bf16)

    each(tok, 32, output)

    def own_back(j, _):
        w = b.wb[j, :, :, 0:wide].reshape(256, wide)
        b.base[:, part(j, 256)] = dot_t(b.x[part(me.h, tok), 0:wide], w)
        return 0

    lax.fori_loop(0, 4, own_back, 0, unroll=4)

    grads.join()
    grads.along()
    grads.on()
    o_square.last()

    def grad_out_sum(i, at):
        total = b.o_keep[at] + sum(b.o_in[k, at].astype(f32) for k in range(2))
        b.o_keep[at] = total
        b.o_low[at] = total.astype(bf16)

    each(128, 32, grad_out_sum)
    o_z = []
    for k in range(1, nz):
        src = b.o_low.at[part((me.z + k) % nz, 32)]
        o_z.append(sends.put(src, b.o_z.at[k - 1], me.z_dev(k)))
    down.total()
    up.total()
    b.up_low[...] = b.up_sum[...].astype(bf16)
    ups = []
    for k in range(3):
        src = b.up_low.at[part(me.heads[k], 32)]
        ups.append(sends.put(src, b.up_in.at[k], peers[k]))
    outs.grad_up[:, part(me.h, 1024)] = b.up_sum[part(me.h, 32)]
    gap_near = grid_of(0, (HD, HD)) - grid_of(1, (HD, HD))
    gap_far = gap_near + HD
    table = []
    for head in range(2):
        last = b.rest[head]
        for i in range(BUCKETS):
            up_to = STARTS[i + 1] if i + 1 < BUCKETS else 2 * WIN
            inside = lambda g: (g >= STARTS[i]) & (g < up_to)
            total = jnp.where(inside(gap_near), b.diag[head], 0.0)
            total = total + jnp.where(inside(gap_far), b.below[head], 0.0)
            total = total.sum(axis=0, keepdims=True)
            table.append(total + last if i == BUCKETS - 1 else total)
    table += [b.sums[0], b.sums[1], jnp.zeros((HD - 2 * BUCKETS - 2, HD), f32)]
    small = lax.dot_general(
        jnp.ones((8, HD), f32), jnp.concatenate(table, axis=0), (((1,), (1,)), ((), ())),
        precision=lax.Precision.HIGHEST, preferred_element_type=f32,
    )
    backs.second()
    grads.late()
    backs.last()

    def first_norm_back(i, at):
        dn1 = b.base[at] + sum(b.dn2s[k + 1, at].astype(f32) for k in range(2))
        x = ins.tokens[at].astype(f32)
        scale = rms(x)
        n1 = x * scale
        b.norms[0:1] += jnp.sum(dn1 * n1, axis=0, keepdims=True)
        spread = dn1 * gain_one
        dx = b.x1[at] + scale * (spread - n1 * jnp.mean(spread * n1, axis=-1, keepdims=True))
        outs.input_grad[at] = dx.astype(bf16)

    each(tok, 32, first_norm_back)
    lines = [b.norms[j : j + 1, i * HD : i * HD + HD] for j in range(2) for i in range(8)]
    b.small[...] = jnp.concatenate(lines + [small], axis=0)
    n_seq = [sends.put(b.small, b.n_seq.at[k - 1], me.seq_dev(k)) for k in range(1, n)]
    grads.total()
    b.q_low[...] = b.q_sum[...].astype(bf16)
    g_head = []
    for k in range(3):
        src = b.q_low.at[part(me.heads[k], 32)]
        g_head.append(sends.put(src, b.q_in.at[k], peers[k]))
    total = b.small[...]
    for k in range(n - 1):
        n_seq[k].wait_recv()
        total = total + b.n_seq[k]
    b.n_line[...] = total
    n_head = [sends.put(b.n_line, b.n_head.at[k], peers[k]) for k in range(3)]
    outs.table[...] = jnp.concatenate([total[16:17, i * BUCKETS : (i + 1) * BUCKETS] for i in range(2)], axis=0)
    outs.rate[...] = total[16:17, 2 * BUCKETS : 2 * BUCKETS + 2]
    total = b.o_keep[part(me.z, 32)]
    for k in range(nz - 1):
        o_z[k].wait_recv()
        total = total + b.o_z[k].astype(f32)
    outs.grad_out[...] = total
    for copy in g_head:
        copy.wait_recv()
    weights = (outs.grad_query, outs.grad_key, outs.grad_value)
    for j, out in enumerate(weights):
        cols = pl.ds(j * 256, 256)
        out[:, part(me.h, 256)] = b.q_sum[part(me.h, 32), cols]
        for k in range(3):
            out[:, part(me.heads[k], 256)] = b.q_in[k, :, cols].astype(f32)
    for copy in n_head + ups:
        copy.wait_recv()
    for k in range(3):
        outs.grad_up[:, part(me.heads[k], 1024)] = b.up_in[k].astype(f32)
    total = b.n_line[...] + sum(b.n_head[k] for k in range(3))
    b.norms[0:8, 0:HD], b.norms[0:8, HD : 2 * HD] = total[0:8], total[8:16]
    mine = b.norms[pl.ds(2 * me.h + me.s // group, 1), 0 : 2 * HD]
    for j, out in enumerate((outs.norm_one, outs.norm_two)):
        row = jnp.zeros((1, rows), f32)
        for i in range(group):
            cut = mine[:, j * HD + i * rows : j * HD + (i + 1) * rows]
            row = jnp.where(me.s % group == i, cut, row)
        out[...] = row
    sends.finish()


def placed(arrays):
    def kernel(*refs):
        count = len(refs) // 2
        copies = [
            pltpu.make_async_copy(refs[i], refs[count + i], refs[-1].at[i]) for i in range(count)
        ]
        for copy in copies:
            copy.start()
        for copy in copies:
            copy.wait()

    return pl.pallas_call(
        kernel,
        out_shape=[jax.ShapeDtypeStruct(a.shape, a.dtype) for a in arrays],
        in_specs=[pl.BlockSpec(memory_space=pltpu.VMEM)] * len(arrays),
        out_specs=[pl.BlockSpec(memory_space=pl.ANY)] * len(arrays),
        scratch_shapes=[pltpu.SemaphoreType.DMA((len(arrays),))],
        name="results",
    )(*arrays)


class Names:
    def __init__(self, names, values):
        self.__dict__.update(zip(names, values))


def shards(
    tokens, cotangent, segments, w_query, w_key, w_value, w_out, w_up, w_down,
    norm_one, norm_two, rel_table, decay_rate,
):
    n = lax.axis_size("seq")
    nz = n // 2
    tok, rows = tokens.shape[0], w_query.shape[0]
    block = 4 * tok
    wide = 6 * HD
    ins = dict(
        table=rel_table, decay=decay_rate.reshape(1, 2), segments=segments.reshape(-1, 128),
        tokens=tokens, cotangent=cotangent, w_query=w_query, w_key=w_key, w_value=w_value,
        w_out=w_out, w_up=w_up, w_down=w_down,
        norm_one=norm_one.reshape(1, rows), norm_two=norm_two.reshape(1, rows),
    )
    outs = dict(
        output=((tok, 1024), bf16), input_grad=((tok, 1024), bf16),
        grad_query=((rows, 1024), f32), grad_key=((rows, 1024), f32),
        grad_value=((rows, 1024), f32), grad_out=((rows, 1024), f32),
        grad_up=((rows, 4096), f32), grad_down=((128, 1024), f32),
        norm_one=((1, rows), f32), norm_two=((1, rows), f32),
        table=((2, BUCKETS), f32), rate=((1, 2), f32),
    )
    pieces = (4, n, rows, 1024)
    square = ((block, 1024), bf16)
    three = ((3, tok, 1024), bf16)
    tables = ((2, TILE, TILE), f32)
    column = ((2, TILE, 1), f32)
    heads = ((2, HD, HD), f32)
    four = ((nz, 128, 1024), bf16)
    room = dict(
        gains=((4, 8, 128), f32), all_gains=((n, 4, 8, 128), f32), a1=((4, rows, wide), bf16), u1=((4, rows, 1024), bf16),
        x=square, hall=square, wb=((4, n, rows, wide), bf16), up=(pieces, bf16),
        dn=((n, 128, 1024), bf16), wo=(pieces, bf16), cots=square,
        q=((2, block, HD), bf16), kvx=((4, 6 * TILE, HD), bf16),
        near=tables, far=tables, decay=tables, enter=column, leave=column,
        rows=((6, 1, TILE), f32), cols=((4, TILE, 1), f32),
        acc=((2, block, HD), f32), local=((8, HD, HD), f32), state=((8, HD, HD), f32),
        lse=((8, TILE, 1), f32),
        sent=((2, HD, HD), bf16), got=((2, 2, HD, HD), bf16),
        sent_back=((2, HD, HD), bf16), got_back=((2, 2, HD, HD), bf16),
        ymix=((tok, 1024), bf16),
        x1=((tok, 1024), f32), base=((tok, 1024), f32), h2all=square, du=square,
        dn2s=((4, tok, 1024), bf16), dnin=three, outp=three,
        da=((tok, 1024), bf16), dyt=((8, tok, HD), bf16), dyh=((2, block, HD), bf16),
        tile=((256, 1024), f32), own=((nz, 128, 1024), f32), o_keep=((128, 1024), f32),
        given_a=four, core_a=four, z_a=((3, 128, 1024), bf16),
        given_b=four, core_b=four, z_b=((nz - 1, 128, 1024), bf16), up_sum=((128, 1024), f32),
        core_o=four, o_in=((3, 128, 1024), bf16), o_low=((128, 1024), bf16),
        o_z=((nz - 1, 32, 1024), bf16),
        core_q=((nz, 128, wide), bf16),
        z_q=((nz - 1, 128, wide), bf16), q_sum=((128, wide), f32), q_in=((3, 32, wide), bf16), q_low=((128, wide), bf16),
        up_low=((128, 1024), bf16), up_in=((3, 32, 1024), bf16),
        diag=heads, below=heads, rest=((2, 1, HD), f32), sums=((2, 1, HD), f32),
        dks=((2, 6 * TILE, HD), f32), dvs=((2, 6 * TILE, HD), f32),
        halo_in=((8, TILE, HD), bf16),
        norms=((8, 1024), f32), small=((24, HD), f32), n_seq=((n - 1, 24, HD), f32),
        n_line=((24, HD), f32), n_head=((3, 24, HD), f32),
    )
    copies = 150

    def kernel(*refs):
        i, o = len(ins), len(ins) + len(outs)
        r = o + len(room)
        whole_kernel(Names(ins, refs[:i]), Names(outs, refs[i:o]), Names(room, refs[o:r]), *refs[r:])

    results = pl.pallas_call(
        kernel,
        out_shape=[jax.ShapeDtypeStruct(shape, kind) for shape, kind in outs.values()],
        in_specs=[pl.BlockSpec(memory_space=pltpu.SMEM)] * 2
        + [pl.BlockSpec(memory_space=pltpu.VMEM)] * (len(ins) - 2),
        out_specs=[pl.BlockSpec(memory_space=pltpu.VMEM)] * len(outs),
        scratch_shapes=[pltpu.VMEM(shape, kind) for shape, kind in room.values()]
        + [pltpu.SemaphoreType.DMA((copies,)), pltpu.SemaphoreType.DMA((copies,))],
        compiler_params=pltpu.CompilerParams(
            collective_id=0, has_side_effects=True, vmem_limit_bytes=63 << 20
        ),
        name="block_layer",
    )(*ins.values())
    results = placed(results)
    *large, norm_one, norm_two, table, rate = results
    return (*large, norm_one.reshape(rows), norm_two.reshape(rows), table, rate.reshape(2))


highest = lax.Precision.HIGHEST


def from_behind(value, axis, by):
    size = lax.axis_size(axis)
    pairs = [(i, i + by) for i in range(size) if 0 <= i + by < size]
    return lax.ppermute(value, axis, pairs)


def prefix(value, axis, join, neutral, backward):
    count = lax.axis_size(axis)
    place = lax.axis_index(axis)
    ahead = count - 1 - place if backward else place
    gathered = jax.tree.map(
        lambda a, kind: lax.all_gather(a.astype(kind), axis), value, (jnp.bfloat16, jnp.bfloat16)
    )
    state = jax.tree.map(lambda a, e: jnp.zeros_like(a) + jnp.asarray(e, a.dtype), value, neutral)

    def one(lap, state):
        source = count - 1 - lap if backward else lap
        return join(
            state,
            jax.tree.map(
                lambda a, own: lax.dynamic_index_in_dim(a, source, 0, False).astype(own.dtype),
                gathered,
                value,
            ),
        )

    return lax.fori_loop(0, ahead, one, state)


def bucket_onehot(window_len, bucket_count):
    distance = np.arange(window_len)
    scaled = np.floor(np.log(np.maximum(distance, 1) / 16.0) / np.log(8.0) * 16.0)
    larger = np.minimum(16 + np.maximum(scaled, 0), bucket_count - 1)
    bucket = np.where(distance < 16, distance, larger).astype(np.int32)
    return (bucket[:, None] == np.arange(bucket_count)[None, :]).astype(np.float32)


def skewed(extended, row_count, col_count):
    head_count = extended.shape[0]
    span = row_count + col_count
    flipped = jnp.concatenate(
        [extended[:, ::-1], jnp.zeros((head_count, 1), extended.dtype)], axis=1
    )
    tiled = jnp.broadcast_to(flipped[:, None, :], (head_count, row_count, span)).reshape(
        head_count, row_count * span
    )
    tiled = tiled[:, : row_count * (span - 1)].reshape(head_count, row_count, span - 1)
    return tiled[:, :, row_count - 1 : row_count - 1 + col_count]


def rms_scale(values, gain):
    return values * lax.rsqrt(jnp.mean(values * values, axis=-1, keepdims=True) + epsilon) * gain


def times_transposed(left, right):
    return lax.dot_general(
        left, right, (((1,), (1,)), ((), ())), preferred_element_type=jnp.float32
    )


def transposed_times(left, right):
    return lax.dot_general(
        left, right, (((0,), (0,)), ((), ())), preferred_element_type=jnp.float32
    )


def compose(earlier, later):
    return (earlier[0] * later[0], later[0][:, None, None] * earlier[1] + later[1])


def group_state(carried_state, query_c, key_c, value_c, seg_group, seg_before, decay_rate):
    length_c = query_c.shape[0]
    position = jnp.arange(length_c).astype(jnp.float32)
    distance = position[:, None] - position[None, :]
    inside = (distance >= 0) & (seg_group[:, None] == seg_group[None, :])
    decay_w = jnp.where(
        inside[None], jnp.exp(-decay_rate[:, None, None] * jnp.maximum(distance, 0.0)[None]), 0.0
    )
    affinity = jnp.einsum("ihd,jhd->hij", query_c, key_c, precision=highest) * state_scale
    readout = jnp.einsum("hij,jhd->ihd", affinity * decay_w, value_c, precision=highest)
    live_mask = (seg_group == seg_before).astype(jnp.float32)
    entering = (
        jnp.exp(-decay_rate[None, :] * (position[:, None] + 1.0)) * live_mask[:, None] * state_scale
    )
    readout = (
        readout
        + jnp.einsum("ihd,hde->ihe", query_c, carried_state, precision=highest)
        * entering[:, :, None]
    )
    keeping = (seg_group == seg_group[-1]).astype(jnp.float32)
    leaving = (
        jnp.exp(-decay_rate[None, :] * (length_c - 1.0 - position[:, None])) * keeping[:, None]
    )
    carry_keep = jnp.exp(-decay_rate * length_c) * (seg_group[-1] == seg_before).astype(jnp.float32)
    updated = jnp.einsum("jhd,jhe->hde", key_c * leaving[:, :, None], value_c, precision=highest)
    updated = updated + carry_keep[:, None, None] * carried_state
    return (updated, readout)


def local_states(query_f, key_f, value_f, decay_rate, seg_block, seg_before):
    block_len, head_count, head_width = query_f.shape
    count = block_len // WIN
    items = (
        query_f.reshape(count, WIN, head_count, head_width),
        key_f.reshape(count, WIN, head_count, head_width),
        value_f.reshape(count, WIN, head_count, head_width),
        seg_block.reshape(count, WIN),
    )

    def step(carry, item):
        carried_state, prior = carry
        updated, readout = group_state(
            carried_state, item[0], item[1], item[2], item[3], prior, decay_rate
        )
        return ((updated, item[3][-1]), readout)

    start_carry = (jnp.zeros((head_count, head_width, head_width), jnp.float32), seg_before)
    (final_state, _), readouts = lax.scan(step, start_carry, items)
    return (readouts.reshape(block_len, head_count, head_width), final_state)


def general_shards(
    tokens,
    cotangent,
    segments,
    w_query,
    w_key,
    w_value,
    w_out,
    w_up,
    w_down,
    norm_one,
    norm_two,
    rel_table,
    decay_rate,
):
    heads_here = rel_table.shape[0]
    head_width = HD
    tok_here = tokens.shape[0]
    block_len = lax.axis_size("head") * tok_here
    block_count = block_len // WIN
    pair_width = heads_here * head_width
    scale = 1.0 / math.sqrt(head_width)
    gathered = (
        lax.all_gather(w_query, ("head", "seq"), axis=0, tiled=True),
        lax.all_gather(w_key, ("head", "seq"), axis=0, tiled=True),
        lax.all_gather(w_value, ("head", "seq"), axis=0, tiled=True),
        lax.all_gather(w_out, ("head", "seq"), axis=0, tiled=True),
        lax.all_gather(w_up, ("head", "seq"), axis=0, tiled=True),
        lax.all_gather(w_down, ("head", "seq"), axis=0, tiled=True),
        lax.all_gather(norm_one, ("head", "seq"), axis=0, tiled=True),
        lax.all_gather(norm_two, ("head", "seq"), axis=0, tiled=True),
    )
    full_query, full_key, full_value, full_out, full_up, full_down, gain_one, gain_two = gathered
    inputs_f = tokens.astype(jnp.float32)
    scaled_one, norm_back_one = jax.vjp(rms_scale, inputs_f, gain_one.astype(jnp.float32))
    normed = scaled_one.astype(jnp.bfloat16)
    projected = jnp.stack(
        [
            jnp.dot(normed, full_query, preferred_element_type=jnp.float32),
            jnp.dot(normed, full_key, preferred_element_type=jnp.float32),
            jnp.dot(normed, full_value, preferred_element_type=jnp.float32),
        ]
    ).astype(jnp.bfloat16)
    regrouped = lax.all_to_all(projected, "head", split_axis=2, concat_axis=1, tiled=True)
    prior_pairs = from_behind(regrouped[1:, block_len - WIN :], "seq", 1)
    pairs_ext = jnp.concatenate([prior_pairs, regrouped[1:]], axis=1)
    query_heads = regrouped[0].reshape(block_len, heads_here, head_width)
    key_ext = pairs_ext[0].reshape(block_len + WIN, heads_here, head_width)
    value_ext = pairs_ext[1].reshape(block_len + WIN, heads_here, head_width)
    block_base = lax.axis_index("seq") * block_len
    padded_segs = jnp.concatenate([jnp.full((WIN,), -1, jnp.int32), segments])
    seg_ext = lax.dynamic_slice_in_dim(padded_segs, block_base, block_len + WIN, 0)
    seg_block = seg_ext[WIN:]
    seg_before = seg_ext[WIN - 1]
    onehot_table = jnp.asarray(bucket_onehot(WIN, BUCKETS))
    by_distance = jnp.dot(rel_table, onehot_table.T, precision=highest)
    bias_ext = jnp.concatenate(
        [
            jnp.zeros((heads_here, WIN - 1), jnp.float32),
            by_distance,
            jnp.zeros((heads_here, WIN), jnp.float32),
        ],
        axis=1,
    )
    bias_full, skew_back = jax.vjp(lambda extended: skewed(extended, WIN, 2 * WIN), bias_ext)
    row_pos = jnp.arange(WIN, dtype=jnp.int32)[:, None]
    col_pos = jnp.arange(2 * WIN, dtype=jnp.int32)[None, :]
    near = (row_pos - col_pos + WIN >= 0) & (row_pos - col_pos + WIN < WIN)

    def block_inputs(number):
        start = number * WIN
        query_b = lax.dynamic_slice_in_dim(query_heads, start, WIN, 0)
        key_b = lax.dynamic_slice_in_dim(key_ext, start, 2 * WIN, 0)
        value_b = lax.dynamic_slice_in_dim(value_ext, start, 2 * WIN, 0)
        seg_q = lax.dynamic_slice_in_dim(seg_block, start, WIN, 0)
        seg_k = lax.dynamic_slice_in_dim(seg_ext, start, 2 * WIN, 0)
        visible = near & (seg_q[:, None] == seg_k[None, :])
        raw = jnp.einsum("ihd,jhd->hij", query_b, key_b, preferred_element_type=jnp.float32) * scale
        scores = jnp.where(visible[None], raw + bias_full, negative)
        return (query_b, key_b, value_b, scores)

    def forward_block(number):
        query_b, key_b, value_b, scores = block_inputs(number)
        top_score = jnp.max(scores, axis=-1, keepdims=True)
        exp_scores = jnp.exp(scores - top_score)
        total_mass = jnp.sum(exp_scores, axis=-1, keepdims=True)
        softmax_w = exp_scores / total_mass
        attended_b = jnp.einsum(
            "hij,jhd->ihd",
            softmax_w.astype(jnp.bfloat16),
            value_b,
            preferred_element_type=jnp.float32,
        )
        return (attended_b, (top_score + jnp.log(total_mass))[..., 0])

    numbers = jnp.arange(block_count, dtype=jnp.int32)
    attended_blocks, log_mass = lax.map(forward_block, numbers)
    attended = attended_blocks.reshape(block_len, heads_here, head_width)
    query_f = query_heads.astype(jnp.float32)
    key_f = key_ext[WIN:].astype(jnp.float32)
    value_f = value_ext[WIN:].astype(jnp.float32)

    def states_here(query_a, key_a, value_a, rates):
        return local_states(query_a, key_a, value_a, rates, seg_block, seg_before)

    (readout_local, state_local), states_back = jax.vjp(
        states_here, query_f, key_f, value_f, decay_rate
    )
    position = jnp.arange(block_len).astype(jnp.float32)
    live_mask = (seg_block == seg_before).astype(jnp.float32)
    enter_decay = (
        jnp.exp(-decay_rate[None, :] * (position[:, None] + 1.0)) * live_mask[:, None] * state_scale
    )
    carry_keep = jnp.exp(-decay_rate * block_len) * (seg_block[-1] == seg_before).astype(
        jnp.float32
    )
    identity = (jnp.ones_like(carry_keep), jnp.zeros_like(state_local))
    carried = prefix((carry_keep, state_local), "seq", compose, identity, False)
    carry_in = carried[1]
    carry_term = (
        jnp.einsum("ihd,hde->ihe", query_f, carry_in, precision=highest) * enter_decay[:, :, None]
    )
    mixed_heads = (
        (attended + readout_local + carry_term).astype(jnp.bfloat16).reshape(block_len, pair_width)
    )
    mixed_tok = lax.all_to_all(mixed_heads, "head", split_axis=0, concat_axis=1, tiled=True)
    resid_one = inputs_f + jnp.dot(mixed_tok, full_out, preferred_element_type=jnp.float32)
    scaled_two, norm_back_two = jax.vjp(rms_scale, resid_one, gain_two.astype(jnp.float32))
    normed_two = scaled_two.astype(jnp.bfloat16)
    up_proj = jnp.dot(normed_two, full_up, preferred_element_type=jnp.float32)
    activated, gelu_back = jax.vjp(jax.nn.gelu, up_proj)
    act_low = activated.astype(jnp.bfloat16)
    output = (resid_one + jnp.dot(act_low, full_down, preferred_element_type=jnp.float32)).astype(
        jnp.bfloat16
    )
    back_query, back_key, back_value = (full_query, full_key, full_value)
    back_out, back_up, back_down = (full_out, full_up, full_down)
    grad_down_w = transposed_times(act_low, cotangent)
    act_grad = times_transposed(cotangent, back_down)
    up_grad = gelu_back(act_grad)[0].astype(jnp.bfloat16)
    grad_up_w = transposed_times(normed_two, up_grad)
    normed_two_grad = times_transposed(up_grad, back_up)
    resid_grad_n, grad_gain_two = norm_back_two(normed_two_grad)
    resid_grad = cotangent.astype(jnp.float32) + resid_grad_n
    attn_grad = resid_grad.astype(jnp.bfloat16)
    grad_out_w = transposed_times(mixed_tok, attn_grad)
    mixed_grad = times_transposed(attn_grad, back_out).astype(jnp.bfloat16)
    heads_grad = lax.all_to_all(mixed_grad, "head", split_axis=1, concat_axis=0, tiled=True)
    heads_grad3 = heads_grad.reshape(block_len, heads_here, head_width)

    def backward_block(item):
        number, log_block = item
        query_b, key_b, value_b, scores = block_inputs(number)
        out_grad_b = lax.dynamic_slice_in_dim(heads_grad3, number * WIN, WIN, 0)
        softmax_w = jnp.exp(scores - log_block[..., None])
        prob_grad = jnp.einsum(
            "ihd,jhd->hij", out_grad_b, value_b, preferred_element_type=jnp.float32
        )
        score_grad = softmax_w * (
            prob_grad - jnp.sum(softmax_w * prob_grad, axis=-1, keepdims=True)
        )
        score_low = score_grad.astype(jnp.bfloat16)
        query_grad_b = (
            jnp.einsum("hij,jhd->ihd", score_low, key_b, preferred_element_type=jnp.float32) * scale
        )
        key_grad_b = (
            jnp.einsum("hij,ihd->jhd", score_low, query_b, preferred_element_type=jnp.float32)
            * scale
        )
        value_grad_b = jnp.einsum(
            "hij,ihd->jhd",
            softmax_w.astype(jnp.bfloat16),
            out_grad_b,
            preferred_element_type=jnp.float32,
        )
        ext_grad_b = skew_back(score_low.astype(jnp.float32))[0]
        return (query_grad_b, key_grad_b, value_grad_b, ext_grad_b)

    query_grads, key_grads, value_grads, ext_grads = lax.map(backward_block, (numbers, log_mass))
    query_grad_att = query_grads.reshape(block_len, heads_here, head_width)

    def fold_pairs(pieces):
        zero_edge = jnp.zeros_like(pieces[:1, :WIN])
        return jnp.concatenate([pieces[:, :WIN], zero_edge], axis=0) + jnp.concatenate(
            [zero_edge, pieces[:, WIN:]], axis=0
        )

    key_folded = fold_pairs(key_grads)
    value_folded = fold_pairs(value_grads)
    sent_pairs = jnp.stack([key_folded[0], value_folded[0]]).reshape(2, WIN, pair_width)
    received = from_behind(sent_pairs.astype(jnp.bfloat16), "seq", -1).astype(sent_pairs.dtype)
    tail_pairs = jnp.concatenate(
        [jnp.zeros((2, block_len - WIN, pair_width), jnp.float32), received], axis=1
    )
    tail_pairs = tail_pairs.reshape(2, block_len, heads_here, head_width)
    key_grad_att = key_folded[1:].reshape(block_len, heads_here, head_width) + tail_pairs[0]
    value_grad_att = value_folded[1:].reshape(block_len, heads_here, head_width) + tail_pairs[1]
    heads_grad_f = heads_grad3.astype(jnp.float32)
    grad_local = jnp.einsum(
        "ihd,ihe->hde", query_f * enter_decay[:, :, None], heads_grad_f, precision=highest
    )
    back_chain = prefix((carry_keep, grad_local), "seq", compose, identity, True)
    carry_out_grad = back_chain[1]
    query_grad_s, key_grad_s, value_grad_s, rate_grad_s = states_back(
        (heads_grad_f, carry_out_grad)
    )
    query_grad_c = (
        jnp.einsum("ihe,hde->ihd", heads_grad_f, carry_in, precision=highest)
        * enter_decay[:, :, None]
    )
    rate_grad_c = -jnp.sum(heads_grad_f * carry_term * (position[:, None, None] + 1.0), axis=(0, 2))
    rate_grad_a = -block_len * carry_keep * jnp.sum(carry_out_grad * carry_in, axis=(1, 2))
    rate_grad = rate_grad_s + rate_grad_c + rate_grad_a
    query_grad = query_grad_att + query_grad_s + query_grad_c
    key_grad = key_grad_att + key_grad_s
    value_grad = value_grad_att + value_grad_s
    triple_grad = (
        jnp.stack([query_grad, key_grad, value_grad])
        .reshape(3, block_len, pair_width)
        .astype(jnp.bfloat16)
    )
    token_grads = lax.all_to_all(triple_grad, "head", split_axis=1, concat_axis=2, tiled=True)
    grad_query_w = transposed_times(normed, token_grads[0])
    grad_key_w = transposed_times(normed, token_grads[1])
    grad_value_w = transposed_times(normed, token_grads[2])
    normed_grad = (
        times_transposed(token_grads[0], back_query)
        + times_transposed(token_grads[1], back_key)
        + times_transposed(token_grads[2], back_value)
    )
    input_grad_n, grad_gain_one = norm_back_one(normed_grad)
    input_grad = (resid_grad + input_grad_n).astype(jnp.bfloat16)
    ext_total = jnp.sum(ext_grads, axis=0)
    table_grad = jnp.dot(ext_total[:, WIN - 1 : 2 * WIN - 1], onehot_table, precision=highest)
    table_grad, rate_grad = lax.psum((table_grad, rate_grad), "seq")
    summed = (
        lax.psum_scatter(grad_query_w, ("head", "seq"), scatter_dimension=0, tiled=True),
        lax.psum_scatter(grad_key_w, ("head", "seq"), scatter_dimension=0, tiled=True),
        lax.psum_scatter(grad_value_w, ("head", "seq"), scatter_dimension=0, tiled=True),
        lax.psum_scatter(grad_out_w, ("head", "seq"), scatter_dimension=0, tiled=True),
        lax.psum_scatter(grad_up_w, ("head", "seq"), scatter_dimension=0, tiled=True),
        lax.psum_scatter(grad_down_w, ("head", "seq"), scatter_dimension=0, tiled=True),
        lax.psum_scatter(grad_gain_one, ("head", "seq"), scatter_dimension=0, tiled=True),
        lax.psum_scatter(grad_gain_two, ("head", "seq"), scatter_dimension=0, tiled=True),
    )
    grad_query, grad_key, grad_value, grad_out, grad_up, grad_down, grad_norm_one, grad_norm_two = (
        summed
    )
    return (
        output,
        input_grad,
        grad_query,
        grad_key,
        grad_value,
        grad_out,
        grad_up,
        grad_down,
        grad_norm_one,
        grad_norm_two,
        table_grad,
        rate_grad,
    )


def solution(mesh):
    devices = mesh.shape["head"] * mesh.shape["seq"]
    tiled = mesh.shape["head"] == 4 and 1024 // devices == 32
    return jax.shard_map(
        shards if tiled else general_shards,
        mesh=mesh,
        in_specs=(
            P(("seq", "head"), None),
            P(("seq", "head"), None),
            P(),
            P(("head", "seq"), None),
            P(("head", "seq"), None),
            P(("head", "seq"), None),
            P(("head", "seq"), None),
            P(("head", "seq"), None),
            P(("head", "seq"), None),
            P(("head", "seq")),
            P(("head", "seq")),
            P("head", None),
            P("head"),
        ),
        out_specs=(
            P(("seq", "head"), None),
            P(("seq", "head"), None),
            P(("head", "seq"), None),
            P(("head", "seq"), None),
            P(("head", "seq"), None),
            P(("head", "seq"), None),
            P(("head", "seq"), None),
            P(("head", "seq"), None),
            P(("head", "seq")),
            P(("head", "seq")),
            P("head", None),
            P("head"),
        ),
        check_vma=False,
    )
```

```python
import functools
import math

import jax
import jax.numpy as jnp
import numpy as np
from jax import lax
from jax.experimental import pallas as pl
from jax.experimental.pallas import tpu as pltpu
from jax.sharding import PartitionSpec as P

HD = 128
BUCKETS = 32
WIN = 512
TILE = 256

epsilon = 1e-06
negative = -1e30
state_scale = 1.0 / 1024.0
MESH = pl.DeviceIdType.MESH
f32 = jnp.float32
bf16 = jnp.bfloat16


def dot(a, b):
    return jnp.dot(a, b, preferred_element_type=f32)


def dot_t(a, b):
    return lax.dot_general(a, b, (((1,), (1,)), ((), ())), preferred_element_type=f32)


def t_dot(a, b):
    return lax.dot_general(a, b, (((0,), (0,)), ((), ())), preferred_element_type=f32)


class Place:
    def __init__(self):
        self.h = lax.axis_index("head")
        self.s = lax.axis_index("seq")
        self.n = lax.axis_size("seq")
        self.nz = self.n // 2
        self.z = self.s // 2
        self.core = self.s % 2
        x, y = self.h % 2, self.h // 2
        self.heads = [2 * y + 1 - x, 2 * (1 - y) + x, 2 * (1 - y) + 1 - x]

    def head_dev(self, k):
        return (self.heads[k], self.s)

    def z_to(self, k):
        return ((self.z + k) % self.nz) * 2 + self.core

    def z_from(self, k):
        return ((self.z + self.nz - k) % self.nz) * 2 + self.core

    def z_dev(self, k):
        return (self.h, self.z_to(k))

    def other(self):
        return self.z * 2 + 1 - self.core

    def core_dev(self):
        return (self.h, self.other())

    def seq_dev(self, by):
        return (self.h, (self.s + self.n + by) % self.n)


def greet(devices):
    barrier = pltpu.get_barrier_semaphore()
    for device in devices:
        pl.semaphore_signal(barrier, inc=1, device_id=device, device_id_type=MESH)
    pl.semaphore_wait(barrier, len(devices))


class Sends:
    def __init__(self, send_sems, recv_sems):
        self.send_sems, self.recv_sems = send_sems, recv_sems
        self.sent_at, self.recv_at, self.all = 0, 0, []

    def claim(self, count):
        self.recv_at += count
        return self.recv_at - count

    def copy(self, src, dst, device, send, recv):
        return pltpu.make_async_remote_copy(
            src_ref=src,
            dst_ref=dst,
            send_sem=self.send_sems.at[send],
            recv_sem=self.recv_sems.at[recv],
            device_id=device,
            device_id_type=MESH,
        )

    def put(self, src, dst, device, recv=None):
        recv = self.claim(1) if recv is None else recv
        copy = self.copy(src, dst, device, self.sent_at, recv)
        self.sent_at += 1
        self.all.append(copy)
        copy.start()
        return copy

    def sent(self, copies):
        for copy in copies:
            copy.wait_send()
        self.all = [c for c in self.all if not any(c is d for d in copies)]

    def finish(self):
        for copy in self.all:
            copy.wait_send()


class Line:
    def __init__(self, me, sends, place):
        self.me, self.sends, self.place = me, sends, place
        z = me.z
        inner = (z * (3 - z)) // 2
        self.near, self.next = 1 + z % 2, 2 * (1 - z % 2) + z // 2
        self.order = [self.near, self.next, 6 - z - self.near - self.next]
        self.piece, self.end = z + inner * (3 - 2 * z), 3 * (1 - z % 2)
        self.base = sends.claim(4)
        self.copies = []

    def put(self, src, chip, to):
        me = self.me
        device = (me.h, 2 * to + me.core)
        self.copies.append(self.sends.put(src, self.place(chip), device, self.base + chip))

    def start(self, own):
        for to in (self.near, self.next):
            self.put(own, self.me.z, to)

    def wait(self, i):
        chip = self.order[i]
        ref = self.place(chip)
        device = (self.me.h, 2 * chip + self.me.core)
        self.sends.copy(ref, ref, device, 0, self.base + chip).wait_recv()
        return ref

    def relay(self):
        ref = self.wait(0)
        self.put(self.place(self.piece), self.piece, self.end)
        return ref


class Square:
    def __init__(self, me, sends, block):
        self.me, self.sends, self.block = me, sends, block

    def start(self, own):
        me = self.me
        self.got = [
            self.sends.put(own, self.block(me.h, None), me.head_dev(k)) for k in range(2)
        ]
        self.halves = []

    def relay(self):
        me = self.me
        for k in range(2):
            self.got[k].wait_recv()
            ref = self.block(me.heads[k], k)
            self.halves.append(self.sends.put(ref, ref, me.head_dev(1 - k)))

    def last(self):
        for copy in self.halves:
            copy.wait_recv()


class SquareSum:
    def __init__(self, me, sends, give, land):
        self.me, self.sends, self.give, self.land = me, sends, give, land
        self.half = give(2).shape[0] // 2
        self.parts = [pl.ds(0, self.half), pl.ds(self.half, self.half)]
        self.copies = []

    def put(self, block, piece, to):
        at = self.parts[piece]
        device = self.me.head_dev(to)
        copy = self.sends.put(self.give(block).at[at], self.land(block).at[at], device)
        self.copies.append(copy)
        return copy

    def first(self):
        self.halves = [self.put(2, k, k) for k in range(2)]

    def early(self, k):
        self.put(k, k, k)

    def second(self):
        land = self.land(2)
        for k in range(2):
            self.halves[k].wait_recv()
            give = self.give(1 - k)

            def add(i, _):
                at = pl.ds(pl.multiple_of(k * self.half + i * 32, 32), 32)
                give[at] = (give[at].astype(f32) + land[at].astype(f32)).astype(bf16)
                return 0

            lax.fori_loop(0, self.half // 32, add, 0, unroll=True)
        for k in range(2):
            self.put(k, 1 - k, k)

    def last(self):
        for copy in self.copies:
            if not any(copy is half for half in self.halves):
                copy.wait_recv()


def rms(x):
    return lax.rsqrt(jnp.mean(x * x, axis=-1, keepdims=True) + epsilon)


LOG2E = math.log2(math.e)
KEY_SCALE = LOG2E / math.sqrt(HD)


def bucket_starts():
    distance = np.arange(WIN)
    scaled = np.floor(np.log(np.maximum(distance, 1) / 16.0) / np.log(8.0) * 16.0)
    larger = np.minimum(16 + np.maximum(scaled, 0), BUCKETS - 1)
    bucket = np.where(distance < 16, distance, larger).astype(np.int32)
    return [int(np.argmax(bucket == b)) for b in range(BUCKETS)]


STARTS = bucket_starts()


def grid_of(axis, shape=(TILE, TILE)):
    return lax.broadcasted_iota(jnp.int32, shape, axis)


def column(row):
    eye = grid_of(0) == grid_of(1)
    return jnp.sum(jnp.where(eye, row, 0.0), axis=1, keepdims=True)


class Segs:
    def __init__(self, me, seg_ref, rows, cols):
        total = 4 * me.n
        self.rows, self.cols = rows, cols

        def row_at(offset):
            at = 2 * ((4 * me.s + total + offset) % total)
            pair = [seg_ref[pl.ds(at + i, 1)].astype(f32) for i in range(2)]
            return jnp.concatenate(pair, axis=1)

        for j in range(6):
            row = row_at(j - 2)
            rows[j] = row
            if j >= 2:
                cols[j - 2] = column(row)
        last = lambda offset: row_at(offset)[:, TILE - 1 : TILE]
        self.last = [last(j - 2) for j in range(6)]
        same = lambda a, b: (a == b).astype(f32)
        self.keep = [same(self.last[t + 2], self.last[t + 1]) for t in range(4)]
        self.keep_before = same(last(-1), last(-5))
        self.keep_after = same(last(7), last(3))

    def live(self, t):
        return (self.cols[t] == self.last[t + 1]).astype(f32)

    def kept(self, t):
        return (self.cols[t] == self.last[t + 2]).astype(f32)


def fill_tables(table_ref, decay_ref, near, far, decay, enter, leave):
    gap = grid_of(0) - grid_of(1)
    place = grid_of(0, (TILE, 1)).astype(f32)
    for head in range(2):
        rate = decay_ref[0, head]
        for out, shift in ((near, 0), (far, TILE)):
            bias = jnp.full((TILE, TILE), table_ref[head, 0] * LOG2E, f32)
            for b in range(1, BUCKETS):
                bias = jnp.where(gap + shift >= STARTS[b], table_ref[head, b] * LOG2E, bias)
            out[head] = jnp.where(gap + shift >= 0, bias, negative)
        fall = jnp.exp(-rate * jnp.maximum(gap, 0).astype(f32)) * state_scale
        decay[head] = jnp.where(gap >= 0, fall, 0.0)
        enter[head] = jnp.exp(-rate * (place + 1.0)) * state_scale
        leave[head] = jnp.exp(-rate * (TILE - 1.0 - place))


def power(rate, steps):
    return jnp.exp(jnp.full((1, HD), -rate * steps, f32))


def tile_scores(raw, head, t, table_ref, near, far, segs):
    col = segs.cols[t]
    same = [col == segs.rows[t + j] for j in range(3)]
    reach = grid_of(0) < grid_of(1)
    rest = table_ref[head, BUCKETS - 1] * LOG2E
    s0 = jnp.where(same[0] & reach, raw[:, :TILE] * KEY_SCALE + rest, negative)
    s1 = jnp.where(same[1], raw[:, TILE : 2 * TILE] * KEY_SCALE + far[head], negative)
    s2 = jnp.where(same[2], raw[:, 2 * TILE :] * KEY_SCALE + near[head], negative)
    return s0, s1, s2, same[2]


GELU_C = math.sqrt(2.0 / math.pi)
GELU_A = 0.044715


def part(i, size):
    return pl.ds(pl.multiple_of(i * size, size), size)


class Reduce:
    def __init__(self, me, sends, own, given, core_in, z_in, keep):
        self.me, self.sends = me, sends
        self.own, self.given, self.core_in, self.z_in, self.keep = own, given, core_in, z_in, keep
        self.width = keep.shape[-1]

    def start(self):
        self.core = self.sends.put(self.given, self.core_in, self.me.core_dev())

    def put(self, chunk, to, slot):
        me = self.me
        device = (me.h, 2 * to + me.core)
        src, dst = self.given.at[chunk], self.z_in.at[slot]
        self.copies.append(self.sends.put(src, dst, device, self.base + slot))

    def wait(self, slot):
        ref = self.z_in.at[slot]
        self.sends.copy(ref, ref, self.me.core_dev(), 0, self.base + slot).wait_recv()

    def join(self):
        me, lanes = self.me, pl.ds(0, self.width)
        z = me.z
        self.core.wait_recv()
        self.sends.sent([self.core])
        self.inner = (z * (3 - z)) // 2
        self.beside, self.across, self.far = z + 1 - 2 * (z % 2), (z + 2) % 4, 3 - z
        for chunk in (self.beside, self.across, self.far):

            def both(i, at):
                total = self.own[chunk, at, lanes] + self.core_in[chunk, at].astype(f32)
                self.given[chunk, at] = total.astype(bf16)

            each(128, 32, both)

        def mine(i, at):
            self.keep[at] = self.own[z, at, lanes] + self.core_in[z, at].astype(f32)

        each(128, 32, mine)

    def along(self):
        self.base, self.copies = self.sends.claim(3), []
        self.put(self.beside, self.beside, 0)

    def on(self):
        to = self.inner * self.across + (1 - self.inner) * self.beside
        self.put(self.across, to, 2 - self.inner)

    def late(self):
        @pl.when(self.inner == 1)
        def _():
            self.wait(2)

            def add(i, at):
                total = self.given[self.far, at].astype(f32) + self.z_in[2, at].astype(f32)
                self.given[self.far, at] = total.astype(bf16)

            each(128, 32, add)

        self.put(self.far, self.far, 2 - self.inner)

    def total(self):
        for slot in range(2):
            self.wait(slot)

        def more(i, at):
            self.keep[at] += self.z_in[0, at].astype(f32) + self.z_in[1, at].astype(f32)

        each(128, 32, more)

        @pl.when(self.inner == 0)
        def _():
            self.wait(2)

            def add(i, at):
                self.keep[at] += self.z_in[2, at].astype(f32)

            each(128, 32, add)


def each(count, step, body, unroll=4):
    def one(i, _):
        body(i, part(i, step))
        return 0

    lax.fori_loop(0, count // step, one, 0, unroll=unroll)


def whole_kernel(ins, outs, b, send_sems, recv_sems):
    me = Place()
    nz, n = me.nz, me.n
    rows, tok = ins.w_out.shape[0], ins.tokens.shape[0]
    peers = [me.head_dev(k) for k in range(3)]
    greet(
        peers
        + [me.seq_dev(k) for k in range(1, n)]
    )
    sends = Sends(send_sems, recv_sems)
    core_dev = me.core_dev()
    wide = 6 * HD

    first = []
    parts = (ins.w_query, ins.w_key, ins.w_value)
    for k in range(3):
        for j, w in enumerate(parts):
            src = w.at[:, part(me.heads[k], 256)]
            first.append(sends.put(src, b.a1.at[me.h, :, j * 256 : j * 256 + 256], peers[k]))

    own = b.wo.at[me.h, me.z, me.core]
    wo_z = [sends.put(ins.w_out, own, me.z_dev(k)) for k in range(1, nz)]

    def token_block(ref):
        def block(i, piece):
            if piece is None:
                return ref.at[part(i, tok)]
            return ref.at[part(2 * i + piece, tok // 2)]

        return block

    toks = Square(me, sends, token_block(b.x))
    toks.start(ins.tokens)
    first_up = []
    for k in range(3):
        src = ins.w_up.at[:, part(me.heads[k], 1024)]
        first_up.append(sends.put(src, b.u1.at[me.h], peers[k]))
    up_line = Line(me, sends, lambda z: b.up.at[:, 2 * z + me.core])
    for j, w in enumerate(parts):
        b.a1[me.h, :, j * 256 : j * 256 + 256] = w[:, part(me.h, 256)]
    lane = lax.broadcasted_iota(jnp.int32, (8, 128), 1)
    line = lax.broadcasted_iota(jnp.int32, (8, 128), 0)
    group = 128 // rows
    gains = jnp.zeros((8, 128), f32)
    for j, gain in enumerate((ins.norm_one, ins.norm_two)):
        row = jnp.concatenate([gain[...].astype(f32)] * group, axis=1)
        gains = jnp.where((lane // rows == me.s % group) & (line == j), row, gains)
    b.gains[me.h] = gains
    own = b.gains.at[me.h]
    first_gains = [sends.put(own, own, peers[k]) for k in range(3)]
    for copy in first:
        copy.wait_recv()
    w_z = [sends.put(b.a1, b.wb.at[:, me.s], me.z_dev(k)) for k in range(1, nz)]
    w_c = [sends.put(b.a1, b.wb.at[:, me.s], core_dev)]
    b.wb[:, me.s] = b.a1[...]
    b.x[part(me.h, tok)] = ins.tokens[...]
    b.u1[me.h] = ins.w_up[:, part(me.h, 1024)]
    b.wo[me.h, me.z, me.core] = ins.w_out[...]
    b.dn[me.s] = ins.w_down[...]
    b.cots[part(me.h, tok)] = ins.cotangent[...]
    for copy in first_gains:
        copy.wait_recv()
    b.all_gains[me.s] = b.gains[...]
    all_gains = []
    for k in range(1, n):
        all_gains.append(sends.put(b.gains, b.all_gains.at[me.s], me.seq_dev(k)))
    toks.relay()
    for copy in wo_z:
        copy.wait_recv()

    def wo_block(i, piece):
        at = pl.ds(0, nz) if piece is None else pl.ds(piece * (nz // 2), nz // 2)
        return b.wo.at[i, at, me.core]

    wo_square = Square(me, sends, wo_block)
    wo_square.start(wo_block(me.h, None))
    cots = Square(me, sends, token_block(b.cots))
    cots.start(ins.cotangent)
    segs = Segs(me, ins.segments, b.rows, b.cols)
    fill_tables(ins.table, ins.decay, b.near, b.far, b.decay, b.enter, b.leave)
    for k in range(1, nz):
        w_z[k - 1].wait_recv()
        ref = b.wb.at[:, me.z_from(k)]
        w_c.append(sends.put(ref, ref, core_dev))
        if k == nz - 2:
            for copy in first_up:
                copy.wait_recv()
            up_line.start(b.u1)
    up_c = [sends.put(b.u1, b.up.at[:, me.s], core_dev)]
    b.up[:, me.s] = b.u1[...]
    for copy in w_c:
        copy.wait_recv()
    for copy in all_gains:
        copy.wait_recv()
    lanes = []
    for h in range(4):
        for s in range(0, n, group):
            lanes.append(sum(b.all_gains[s + i, h] for i in range(group)))
    gains = jnp.concatenate(lanes, axis=1)
    gain_one, gain_two = gains[0:1], gains[1:2]
    toks.last()
    for pair in (2, 0):

        def norm_one(i, _):
            at = pl.ds(pair * tok + i * 32, 32)
            x = b.x[at].astype(f32)
            b.hall[at] = (x * rms(x) * gain_one).astype(bf16)

        each(2 * tok, 32, norm_one)

        for t in (pair, pair + 1):
            at = pl.ds(t * tok, tok)
            for j in range(3):
                w = b.wb[:, :, :, j * 256 : j * 256 + 256].reshape(1024, 256)
                out = dot(b.hall[at], w).astype(bf16)
                for head in range(2):
                    mine = out[:, head * HD : head * HD + HD]
                    if j == 0:
                        b.q[head, at] = mine
                    else:
                        b.kvx[2 * (j - 1) + head, pl.ds((t + 2) * tok, tok)] = mine
        if pair == 2:
            halo = sends.put(b.kvx.at[:, 4 * TILE :], b.kvx.at[:, : 2 * TILE], me.seq_dev(1))
    sends.sent(toks.halves)

    falls = [power(ins.decay[0, head], float(TILE)) for head in range(2)]
    for head in range(2):
        state = jnp.zeros((HD, HD), f32)
        for t in range(4):
            at = pl.ds((t + 2) * TILE, TILE)
            key = (b.kvx[head, at].astype(f32) * (b.leave[head] * segs.kept(t))).astype(bf16)
            add = t_dot(key, b.kvx[2 + head, at])
            b.local[4 * head + t] = add
            state = falls[head] * segs.keep[t] * state + add
        b.sent[head] = state.astype(bf16)
    carry = [sends.put(b.sent, b.got.at[k - 1], me.seq_dev(k)) for k in (1, 2)]
    wo_square.relay()
    cots.relay()
    up_c.append(sends.put((ref := up_line.relay()), ref, core_dev))

    def forward(index, base):
        head, t = index // 2, base + index % 2
        at, own = part(t, TILE), part(t + 2, TILE)
        wide = pl.ds(pl.multiple_of(t * TILE, TILE), 3 * TILE)
        raw = dot_t(b.q[head, at], b.kvx[head, wide])
        s0, s1, s2, same = tile_scores(raw, head, t, ins.table, b.near, b.far, segs)
        top = jnp.maximum(jnp.maximum(s0, s1), s2).max(axis=1, keepdims=True)
        e0, e1, e2 = jnp.exp2(s0 - top), jnp.exp2(s1 - top), jnp.exp2(s2 - top)
        mass = (e0 + e1 + e2).sum(axis=1, keepdims=True)
        b.lse[4 * head + t] = top + jnp.log2(mass)
        mix = jnp.concatenate([e0.astype(bf16), e1.astype(bf16), e2.astype(bf16)], axis=1)
        att = dot(mix, b.kvx[2 + head, wide]) / mass
        weight = jnp.where(same, raw[:, 2 * TILE :] * b.decay[head], 0.0).astype(bf16)
        b.acc[head, at] += att + dot(weight, b.kvx[2 + head, own])
        return base

    for head in range(2):
        b.acc[head, 2 * TILE :] = jnp.zeros((2 * TILE, HD), f32)
    lax.fori_loop(0, 4, forward, 2, unroll=2)
    for copy in carry:
        copy.wait_recv()
    for head in range(2):
        past = power(ins.decay[0, head], 4.0 * TILE) * segs.keep_before
        state = b.got[0, head].astype(f32) + past * b.got[1, head].astype(f32)
        for t in range(4):
            at = pl.ds(t * TILE, TILE)
            b.state[4 * head + t] = state
            reach = b.enter[head] * segs.live(t)
            y = dot(b.q[head, at], state.astype(bf16)) * reach
            b.acc[head, at] = b.acc[head, at] + y if t >= 2 else y
            state = falls[head] * segs.keep[t] * state + b.local[4 * head + t]
    halo.wait_recv()
    own = b.dn.at[me.s]
    dn_z = [sends.put(ins.w_down, own, me.z_dev(k)) for k in range(1, nz)]
    dn_c = [sends.put(ins.w_down, own, core_dev)]
    wo_square.last()
    own = b.wo.at[:, :, me.core]
    wo_c = [sends.put(own, own, core_dev)]
    lax.fori_loop(0, 4, forward, 0, unroll=2)
    for t in range(4):
        for head in range(2):
            b.dyt[2 * t + head] = b.acc[head, pl.ds(t * TILE, TILE)].astype(bf16)
    ys = []
    for k in range(3):
        for head in range(2):
            src = b.dyt.at[2 * me.heads[k] + head]
            ys.append(sends.put(src, b.ymix.at[:, part(2 * me.h + head, HD)], peers[k]))
    for head in range(2):
        b.ymix[:, part(2 * me.h + head, HD)] = b.dyt[2 * me.h + head]
    for copy in ys + wo_c:
        copy.wait_recv()

    def out_tile(j, _):
        cols = part(j, 256)
        w = b.wo[:, :, :, :, cols].reshape(1024, 256)
        b.x1[:, cols] = ins.tokens[:, cols].astype(f32) + dot(b.ymix[...], w)
        return 0

    lax.fori_loop(0, 4, out_tile, 0, unroll=4)
    def norm_two(i, at):
        x = b.x1[at]
        b.h2all[pl.ds(pl.multiple_of(me.h * tok + i * 32, 32), 32)] = (x * rms(x) * gain_two).astype(bf16)
        b.base[at] = x

    each(tok, 32, norm_two)
    own = b.h2all.at[part(me.h, tok)]
    h2s = Square(me, sends, token_block(b.h2all))
    h2s.start(own)
    for i in (1, 2):
        ref = up_line.wait(i)
        up_c.append(sends.put(ref, ref, core_dev))
    for k in range(1, nz):
        dn_z[k - 1].wait_recv()
        ref = b.dn.at[me.z_from(k)]
        dn_c.append(sends.put(ref, ref, core_dev))
    cots.last()
    for copy in up_c + dn_c:
        copy.wait_recv()
    dn2s = SquareSum(me, sends, lambda k: b.dn2s.at[k + 1], lambda k: b.dnin.at[k])
    for k in (0, 1, 2, -1):
        at = part(me.h if k < 0 else me.heads[k], tok)
        if k == 0:
            h2s.relay()
        elif k == 2:
            h2s.last()

        def hidden(j, _):
            cols = part(j, 256)
            u = dot(b.h2all[at], b.up[:, :, :, cols].reshape(1024, 256))
            dg = dot_t(b.cots[at], b.dn[pl.ds(2 * j, 2)].reshape(256, 1024))
            uu = u * u
            t = jnp.tanh(GELU_C * u * (1.0 + GELU_A * uu))
            b.x[at, cols] = (0.5 * u * (1.0 + t)).astype(bf16)
            slope = 0.5 * (1.0 + t) + (0.5 * GELU_C) * u * (1.0 - t * t) * (1.0 + 3.0 * GELU_A * uu)
            b.du[at, cols] = (slope * dg).astype(bf16)
            return 0

        lax.fori_loop(0, 4, hidden, 0, unroll=4)

        def back(j, _):
            w = b.up[j].reshape(256, 1024)
            b.dn2s[k + 1, :, part(j, 256)] = dot_t(b.du[at], w).astype(bf16)
            return 0

        lax.fori_loop(0, 4, back, 0, unroll=4)
        if k == 2:
            dn2s.first()
        elif k >= 0:
            dn2s.early(k)

        def ahead(j, _):
            cols = part(j, 256)
            out = dot(b.x[at], b.dn[:, :, cols].reshape(1024, 256))
            if k < 0:
                b.base[:, cols] = b.base[:, cols] + out
            else:
                b.outp[k, :, cols] = out.astype(bf16)
            return 0

        lax.fori_loop(0, 4, ahead, 0, unroll=4)

    def down_tile(j, _):
        b.tile[...] = t_dot(b.x[:, part(j, 256)], b.cots[...])
        b.own[j] = b.tile[part(me.core, 128)]
        b.given_a[j] = b.tile[part(1 - me.core, 128)].astype(bf16)
        return 0

    lax.fori_loop(0, 4, down_tile, 0, unroll=2)
    down = Reduce(me, sends, b.own, b.given_a, b.core_a, b.z_a, outs.grad_down)
    down.start()
    dn2s.second()
    down.join()
    down.along()
    down.on()

    def up_tile(j, _):
        b.tile[...] = t_dot(b.h2all[:, part(j, 256)], b.du[...])
        for z in range(nz):
            b.own[z, part(j, 32)] = b.tile[part(2 * z + me.core, 32)]
            b.given_b[z, part(j, 32)] = b.tile[part(2 * z + 1 - me.core, 32)].astype(bf16)
        return 0

    lax.fori_loop(0, 4, up_tile, 0, unroll=2)
    up = Reduce(me, sends, b.own, b.given_b, b.core_b, b.z_b, b.up_sum)
    up.start()
    dn2s.last()
    b.norms[...] = jnp.zeros_like(b.norms)

    def second_norm_back(i, at):
        dn2 = b.dn2s[0, at].astype(f32) + sum(b.dnin[k, at].astype(f32) for k in range(2))
        x = b.x1[at]
        scale = rms(x)
        n2 = x * scale
        b.norms[1:2] += jnp.sum(dn2 * n2, axis=0, keepdims=True)
        spread = dn2 * gain_two
        dx1 = ins.cotangent[at].astype(f32) + scale * (
            spread - n2 * jnp.mean(spread * n2, axis=-1, keepdims=True)
        )
        b.x1[at] = dx1
        b.da[at] = dx1.astype(bf16)

    each(tok, 32, second_norm_back)
    sends.sent(ys + dn2s.copies + dn_c[1:])

    def back_tile(j, _):
        out = dot_t(b.da[...], b.wo[j].reshape(256, 1024)).astype(bf16)
        b.dyt[2 * j] = out[:, :HD]
        b.dyt[2 * j + 1] = out[:, HD:]
        return 0

    lax.fori_loop(0, 4, back_tile, 0, unroll=4)
    dys = []
    for k in range(3):
        src = b.dyt.at[pl.ds(2 * me.heads[k], 2)]
        dys.append(sends.put(src, b.dyh.at[:, part(me.h, tok)], peers[k]))
    b.dyh[:, part(me.h, tok)] = b.dyt[pl.ds(2 * me.h, 2)]
    down.late()
    for copy in dys:
        copy.wait_recv()
    outp = SquareSum(me, sends, lambda k: b.outp.at[k], lambda k: b.dnin.at[k])
    outp.first()
    outp.early(0)
    outp.early(1)
    for zero in (b.sums, b.dks, b.dvs, b.diag, b.below, b.rest):
        zero[...] = jnp.zeros_like(zero)
    for head in range(2):
        grad = jnp.zeros((HD, HD), f32)
        for t in range(3, -1, -1):
            at = pl.ds(t * TILE, TILE)
            query = (b.q[head, at].astype(f32) * (b.enter[head] * segs.live(t))).astype(bf16)
            add = t_dot(query, b.dyh[head, at])
            b.local[4 * head + t] = add
            grad = falls[head] * segs.keep[t] * grad + add
        b.sent_back[head] = grad.astype(bf16)
    carry = [sends.put(b.sent_back, b.got_back.at[k - 1], me.seq_dev(-k)) for k in (1, 2)]
    up.join()
    up.along()

    def grad_out_tile(j, _):
        b.tile[...] = t_dot(b.ymix[:, part(j, 256)], b.da[...])
        for z in range(nz):
            b.own[j, part(z, 32)] = b.tile[part(2 * z + me.core, 32)]
            b.dn[j, part(z, 32)] = b.tile[part(2 * z + 1 - me.core, 32)].astype(bf16)
        return 0

    lax.fori_loop(0, 4, grad_out_tile, 0, unroll=2)
    o_core = sends.put(b.dn.at[0:4], b.core_o, core_dev)

    gap = (grid_of(0) - grid_of(1)).astype(f32)

    def backward(index, base):
        head, t = index // 2, base + index % 2
        at, wide = part(t, TILE), pl.ds(pl.multiple_of(t * TILE, TILE), 3 * TILE)
        query, dy = b.q[head, at], b.dyh[head, at]
        keys, values = b.kvx[head, wide], b.kvx[2 + head, wide]
        raw = dot_t(query, keys)
        s0, s1, s2, same = tile_scores(raw, head, t, ins.table, b.near, b.far, segs)
        lse = b.lse[4 * head + t]
        p0, p1, p2 = jnp.exp2(s0 - lse), jnp.exp2(s1 - lse), jnp.exp2(s2 - lse)
        dp = dot_t(dy, values)
        dp0, dp1, dp2 = dp[:, :TILE], dp[:, TILE : 2 * TILE], dp[:, 2 * TILE :]
        mean = (p0 * dp0 + p1 * dp1 + p2 * dp2).sum(axis=1, keepdims=True)
        d0, d1, d2 = p0 * (dp0 - mean), p1 * (dp1 - mean), p2 * (dp2 - mean)
        b.diag[head] += d2[:HD, :HD] + d2[HD:, HD:]
        b.below[head] += d2[HD:, :HD] + d1[:HD, HD:]
        b.rest[head] += (
            (d0[:, :HD] + d0[:, HD:]).sum(axis=0, keepdims=True)
            + d1[:, :HD].sum(axis=0, keepdims=True)
            + d1[HD:, HD:].sum(axis=0, keepdims=True)
        )
        weight = jnp.where(same, b.decay[head], 0.0)
        mixed = weight * raw[:, 2 * TILE :]
        turn = weight * dp2
        slope = mixed * dp2 * gap
        b.sums[head] -= (slope[:, :HD] + slope[:, HD:]).sum(axis=0, keepdims=True)
        scale = 1.0 / math.sqrt(HD)
        x = jnp.concatenate(
            [(d0 * scale).astype(bf16), (d1 * scale).astype(bf16), (d2 * scale + turn).astype(bf16)],
            axis=1,
        )
        p = jnp.concatenate([p0.astype(bf16), p1.astype(bf16), (p2 + mixed).astype(bf16)], axis=1)
        b.acc[head, at] = dot(x, keys)
        b.dks[head, wide] += t_dot(x, query)
        b.dvs[head, wide] += t_dot(p, dy)
        return base

    lax.fori_loop(0, 4, backward, 0, unroll=2)
    outp.second()
    sends.sent(dys)
    for head in range(2):
        for i in range(2):
            at = pl.ds(i * TILE, TILE)
            b.dyt[2 * head + i] = b.dks[head, at].astype(bf16)
            b.dyt[4 + 2 * head + i] = b.dvs[head, at].astype(bf16)
    halo = sends.put(b.dyt, b.halo_in, me.seq_dev(-1))
    up.on()
    o_core.wait_recv()
    sends.sent(down.copies)
    for k in range(3):
        to = me.heads[k]

        def chip_sum(i, at):
            both = b.own[to, at] + b.core_o[to, at].astype(f32)
            b.given_a[k, at] = both.astype(bf16)

        each(128, 32, chip_sum)
    o_square = SquareSum(me, sends, lambda k: b.given_a.at[k], lambda k: b.o_in.at[k])
    o_square.first()
    o_square.early(0)
    o_square.early(1)

    def keep(i, at):
        b.o_keep[at] = b.own[me.h, at] + b.core_o[me.h, at].astype(f32)

    each(128, 32, keep)
    lax.fori_loop(0, 4, backward, 2, unroll=2)
    o_square.second()
    up.late()
    for copy in carry:
        copy.wait_recv()
    place = grid_of(0, (TILE, 1)).astype(f32)
    for head in range(2):
        past = power(ins.decay[0, head], 4.0 * TILE) * segs.keep_after
        grad = b.got_back[0, head].astype(f32) + past * b.got_back[1, head].astype(f32)
        fall = falls[head]
        total = jnp.zeros((1, HD), f32)
        for t in range(3, -1, -1):
            at = pl.ds(t * TILE, TILE)
            ext = pl.ds((t + 2) * TILE, TILE)
            low = grad.astype(bf16)
            state = b.state[4 * head + t]
            give = b.leave[head] * segs.kept(t)
            take = b.enter[head] * segs.live(t)
            query, key, value = b.q[head, at], b.kvx[head, ext], b.kvx[2 + head, ext]
            dq = dot_t(b.dyh[head, at], state.astype(bf16)) * take
            dv = dot(key, low) * give
            dk = dot_t(value, low) * give + b.dks[head, ext]
            slope = dq * query.astype(f32) * (place + 1.0)
            slope = slope + dv * value.astype(f32) * (TILE - 1.0 - place)
            crossing = fall * segs.keep[t]
            total = total - slope.sum(axis=0, keepdims=True)
            total = total - TILE * crossing * (grad * state).sum(axis=0, keepdims=True)
            dv = dv + b.dvs[head, ext]
            b.x[at, head * HD : head * HD + HD] = (b.acc[head, at] + dq).astype(bf16)
            if t >= 2:
                b.dks[head, ext], b.dvs[head, ext] = dk, dv
            else:
                for j, grad_tile in ((2, dk), (4, dv)):
                    b.x[at, (j + head) * HD : (j + head + 1) * HD] = grad_tile.astype(bf16)
            grad = b.local[4 * head + t] + crossing * grad
        b.sums[head] += total
    halo.wait_recv()
    for head in range(2):
        for t in (2, 3):
            at, ext = pl.ds(t * TILE, TILE), pl.ds((t + 2) * TILE, TILE)
            for j, ref in ((2, b.dks), (4, b.dvs)):
                total = ref[head, ext] + b.halo_in[2 * j - 4 + 2 * head + t - 2].astype(f32)
                b.x[at, (j + head) * HD : (j + head + 1) * HD] = total.astype(bf16)

    def grad_tile(j, _):
        tile = pl.ds(0, wide)
        b.tile[:, tile] = t_dot(b.hall[:, part(j, 256)], b.x[:, 0:wide])
        for z in range(nz):
            b.own[z, part(j, 32), tile] = b.tile[part(2 * z + me.core, 32), tile]
            b.dn[4 + z, part(j, 32), tile] = b.tile[part(2 * z + 1 - me.core, 32), tile].astype(bf16)
        return 0

    lax.fori_loop(0, 4, grad_tile, 0, unroll=2)
    grads = Reduce(me, sends, b.own, b.dn.at[4:8, :, 0:wide], b.core_q, b.z_q, b.q_sum)
    grads.start()
    backs = SquareSum(
        me, sends, lambda k: b.du.at[pl.ds(k * tok, tok)], lambda k: b.dn2s.at[k + 1]
    )
    for k in (2, 0, 1):
        at, to = part(me.heads[k], tok), pl.ds(k * tok, tok)

        def spread_back(j, _):
            w = b.wb[j, :, :, 0:wide].reshape(256, wide)
            b.du[to, part(j, 256)] = dot_t(b.x[at, 0:wide], w).astype(bf16)
            return 0

        lax.fori_loop(0, 4, spread_back, 0, unroll=4)
        if k == 2:
            backs.first()
        else:
            backs.early(k)

    outp.last()

    def output(i, at):
        total = b.base[at] + sum(b.dnin[k, at].astype(f32) for k in range(2))
        outs.output[at] = total.astype(bf16)

    each(tok, 32, output)

    def own_back(j, _):
        w = b.wb[j, :, :, 0:wide].reshape(256, wide)
        b.base[:, part(j, 256)] = dot_t(b.x[part(me.h, tok), 0:wide], w)
        return 0

    lax.fori_loop(0, 4, own_back, 0, unroll=4)

    grads.join()
    grads.along()
    grads.on()
    gap_near = grid_of(0, (HD, HD)) - grid_of(1, (HD, HD))
    gap_far = gap_near + HD
    table = []
    for head in range(2):
        last = b.rest[head]
        for i in range(BUCKETS):
            up_to = STARTS[i + 1] if i + 1 < BUCKETS else 2 * WIN
            inside = lambda g: (g >= STARTS[i]) & (g < up_to)
            total = jnp.where(inside(gap_near), b.diag[head], 0.0)
            total = total + jnp.where(inside(gap_far), b.below[head], 0.0)
            total = total.sum(axis=0, keepdims=True)
            table.append(total + last if i == BUCKETS - 1 else total)
    table += [b.sums[0], b.sums[1], jnp.zeros((HD - 2 * BUCKETS - 2, HD), f32)]
    small = lax.dot_general(
        jnp.ones((8, HD), f32), jnp.concatenate(table, axis=0), (((1,), (1,)), ((), ())),
        precision=lax.Precision.HIGHEST, preferred_element_type=f32,
    )
    backs.second()
    o_square.last()

    def grad_out_sum(i, at):
        total = b.o_keep[at] + sum(b.o_in[k, at].astype(f32) for k in range(2))
        b.o_keep[at] = total
        b.o_low[at] = total.astype(bf16)

    each(128, 32, grad_out_sum)
    o_z = []
    for k in range(1, nz):
        src = b.o_low.at[part((me.z + k) % nz, 32)]
        o_z.append(sends.put(src, b.o_z.at[k - 1], me.z_dev(k)))
    grads.late()
    backs.last()

    def first_norm_back(i, at):
        dn1 = b.base[at] + sum(b.dn2s[k + 1, at].astype(f32) for k in range(2))
        x = ins.tokens[at].astype(f32)
        scale = rms(x)
        n1 = x * scale
        b.norms[0:1] += jnp.sum(dn1 * n1, axis=0, keepdims=True)
        spread = dn1 * gain_one
        dx = b.x1[at] + scale * (spread - n1 * jnp.mean(spread * n1, axis=-1, keepdims=True))
        outs.input_grad[at] = dx.astype(bf16)

    each(tok, 32, first_norm_back)
    lines = [b.norms[j : j + 1, i * HD : i * HD + HD] for j in range(2) for i in range(8)]
    b.small[...] = jnp.concatenate(lines + [small], axis=0)
    n_seq = [sends.put(b.small, b.n_seq.at[k - 1], me.seq_dev(k)) for k in range(1, n)]
    up.total()
    b.up_low[...] = b.up_sum[...].astype(bf16)
    ups = []
    for k in range(3):
        src = b.up_low.at[part(me.heads[k], 32)]
        ups.append(sends.put(src, b.up_in.at[k], peers[k]))
    outs.grad_up[:, part(me.h, 1024)] = b.up_sum[part(me.h, 32)]
    grads.total()
    b.q_low[...] = b.q_sum[...].astype(bf16)
    g_head = []
    for k in range(3):
        src = b.q_low.at[part(me.heads[k], 32)]
        g_head.append(sends.put(src, b.q_in.at[k], peers[k]))
    total = b.small[...]
    for k in range(n - 1):
        n_seq[k].wait_recv()
        total = total + b.n_seq[k]
    b.n_line[...] = total
    n_head = [sends.put(b.n_line, b.n_head.at[k], peers[k]) for k in range(3)]
    outs.table[...] = jnp.concatenate([total[16:17, i * BUCKETS : (i + 1) * BUCKETS] for i in range(2)], axis=0)
    outs.rate[...] = total[16:17, 2 * BUCKETS : 2 * BUCKETS + 2]
    total = b.o_keep[part(me.z, 32)]
    for k in range(nz - 1):
        o_z[k].wait_recv()
        total = total + b.o_z[k].astype(f32)
    outs.grad_out[...] = total
    down.total()
    for copy in g_head:
        copy.wait_recv()
    weights = (outs.grad_query, outs.grad_key, outs.grad_value)
    for j, out in enumerate(weights):
        cols = pl.ds(j * 256, 256)
        out[:, part(me.h, 256)] = b.q_sum[part(me.h, 32), cols]
        for k in range(3):
            out[:, part(me.heads[k], 256)] = b.q_in[k, :, cols].astype(f32)
    for copy in n_head + ups:
        copy.wait_recv()
    for k in range(3):
        outs.grad_up[:, part(me.heads[k], 1024)] = b.up_in[k].astype(f32)
    total = b.n_line[...] + sum(b.n_head[k] for k in range(3))
    b.norms[0:8, 0:HD], b.norms[0:8, HD : 2 * HD] = total[0:8], total[8:16]
    mine = b.norms[pl.ds(2 * me.h + me.s // group, 1), 0 : 2 * HD]
    for j, out in enumerate((outs.norm_one, outs.norm_two)):
        row = jnp.zeros((1, rows), f32)
        for i in range(group):
            cut = mine[:, j * HD + i * rows : j * HD + (i + 1) * rows]
            row = jnp.where(me.s % group == i, cut, row)
        out[...] = row
    sends.finish()


def placed(arrays):
    def kernel(*refs):
        count = len(refs) // 2
        copies = [
            pltpu.make_async_copy(refs[i], refs[count + i], refs[-1].at[i]) for i in range(count)
        ]
        for copy in copies:
            copy.start()
        for copy in copies:
            copy.wait()

    return pl.pallas_call(
        kernel,
        out_shape=[jax.ShapeDtypeStruct(a.shape, a.dtype) for a in arrays],
        in_specs=[pl.BlockSpec(memory_space=pltpu.VMEM)] * len(arrays),
        out_specs=[pl.BlockSpec(memory_space=pl.ANY)] * len(arrays),
        scratch_shapes=[pltpu.SemaphoreType.DMA((len(arrays),))],
        name="results",
    )(*arrays)


class Names:
    def __init__(self, names, values):
        self.__dict__.update(zip(names, values))


def shards(
    tokens, cotangent, segments, w_query, w_key, w_value, w_out, w_up, w_down,
    norm_one, norm_two, rel_table, decay_rate,
):
    n = lax.axis_size("seq")
    nz = n // 2
    tok, rows = tokens.shape[0], w_query.shape[0]
    block = 4 * tok
    wide = 6 * HD
    ins = dict(
        table=rel_table, decay=decay_rate.reshape(1, 2), segments=segments.reshape(-1, 128),
        tokens=tokens, cotangent=cotangent, w_query=w_query, w_key=w_key, w_value=w_value,
        w_out=w_out, w_up=w_up, w_down=w_down,
        norm_one=norm_one.reshape(1, rows), norm_two=norm_two.reshape(1, rows),
    )
    outs = dict(
        output=((tok, 1024), bf16), input_grad=((tok, 1024), bf16),
        grad_query=((rows, 1024), f32), grad_key=((rows, 1024), f32),
        grad_value=((rows, 1024), f32), grad_out=((rows, 1024), f32),
        grad_up=((rows, 4096), f32), grad_down=((128, 1024), f32),
        norm_one=((1, rows), f32), norm_two=((1, rows), f32),
        table=((2, BUCKETS), f32), rate=((1, 2), f32),
    )
    pieces = (4, n, rows, 1024)
    square = ((block, 1024), bf16)
    three = ((3, tok, 1024), bf16)
    tables = ((2, TILE, TILE), f32)
    column = ((2, TILE, 1), f32)
    heads = ((2, HD, HD), f32)
    four = ((nz, 128, 1024), bf16)
    room = dict(
        gains=((4, 8, 128), f32), all_gains=((n, 4, 8, 128), f32), a1=((4, rows, wide), bf16), u1=((4, rows, 1024), bf16),
        x=square, hall=square, wb=((4, n, rows, wide), bf16), up=(pieces, bf16),
        dn=((n, 128, 1024), bf16), wo=((4, nz, 2, rows, 1024), bf16), cots=square,
        q=((2, block, HD), bf16), kvx=((4, 6 * TILE, HD), bf16),
        near=tables, far=tables, decay=tables, enter=column, leave=column,
        rows=((6, 1, TILE), f32), cols=((4, TILE, 1), f32),
        acc=((2, block, HD), f32), local=((8, HD, HD), f32), state=((8, HD, HD), f32),
        lse=((8, TILE, 1), f32),
        sent=((2, HD, HD), bf16), got=((2, 2, HD, HD), bf16),
        sent_back=((2, HD, HD), bf16), got_back=((2, 2, HD, HD), bf16),
        ymix=((tok, 1024), bf16),
        x1=((tok, 1024), f32), base=((tok, 1024), f32), h2all=square, du=square,
        dn2s=((4, tok, 1024), bf16), dnin=three, outp=three,
        da=((tok, 1024), bf16), dyt=((8, tok, HD), bf16), dyh=((2, block, HD), bf16),
        tile=((256, 1024), f32), own=((nz, 128, 1024), f32), o_keep=((128, 1024), f32),
        given_a=four, core_a=four, z_a=((3, 128, 1024), bf16),
        given_b=four, core_b=four, z_b=((nz - 1, 128, 1024), bf16), up_sum=((128, 1024), f32),
        core_o=four, o_in=((3, 128, 1024), bf16), o_low=((128, 1024), bf16),
        o_z=((nz - 1, 32, 1024), bf16),
        core_q=((nz, 128, wide), bf16),
        z_q=((nz - 1, 128, wide), bf16), q_sum=((128, wide), f32), q_in=((3, 32, wide), bf16), q_low=((128, wide), bf16),
        up_low=((128, 1024), bf16), up_in=((3, 32, 1024), bf16),
        diag=heads, below=heads, rest=((2, 1, HD), f32), sums=((2, 1, HD), f32),
        dks=((2, 6 * TILE, HD), f32), dvs=((2, 6 * TILE, HD), f32),
        halo_in=((8, TILE, HD), bf16),
        norms=((8, 1024), f32), small=((24, HD), f32), n_seq=((n - 1, 24, HD), f32),
        n_line=((24, HD), f32), n_head=((3, 24, HD), f32),
    )
    copies = 150

    def kernel(*refs):
        i, o = len(ins), len(ins) + len(outs)
        r = o + len(room)
        whole_kernel(Names(ins, refs[:i]), Names(outs, refs[i:o]), Names(room, refs[o:r]), *refs[r:])

    results = pl.pallas_call(
        kernel,
        out_shape=[jax.ShapeDtypeStruct(shape, kind) for shape, kind in outs.values()],
        in_specs=[pl.BlockSpec(memory_space=pltpu.SMEM)] * 2
        + [pl.BlockSpec(memory_space=pltpu.VMEM)] * (len(ins) - 2),
        out_specs=[pl.BlockSpec(memory_space=pltpu.VMEM)] * len(outs),
        scratch_shapes=[pltpu.VMEM(shape, kind) for shape, kind in room.values()]
        + [pltpu.SemaphoreType.DMA((copies,)), pltpu.SemaphoreType.DMA((copies,))],
        compiler_params=pltpu.CompilerParams(
            collective_id=0, has_side_effects=True, vmem_limit_bytes=63 << 20
        ),
        name="block_layer",
    )(*ins.values())
    results = placed(results)
    *large, norm_one, norm_two, table, rate = results
    return (*large, norm_one.reshape(rows), norm_two.reshape(rows), table, rate.reshape(2))


highest = lax.Precision.HIGHEST


def from_behind(value, axis, by):
    size = lax.axis_size(axis)
    pairs = [(i, i + by) for i in range(size) if 0 <= i + by < size]
    return lax.ppermute(value, axis, pairs)


def prefix(value, axis, join, neutral, backward):
    count = lax.axis_size(axis)
    place = lax.axis_index(axis)
    ahead = count - 1 - place if backward else place
    gathered = jax.tree.map(
        lambda a, kind: lax.all_gather(a.astype(kind), axis), value, (jnp.bfloat16, jnp.bfloat16)
    )
    state = jax.tree.map(lambda a, e: jnp.zeros_like(a) + jnp.asarray(e, a.dtype), value, neutral)

    def one(lap, state):
        source = count - 1 - lap if backward else lap
        return join(
            state,
            jax.tree.map(
                lambda a, own: lax.dynamic_index_in_dim(a, source, 0, False).astype(own.dtype),
                gathered,
                value,
            ),
        )

    return lax.fori_loop(0, ahead, one, state)


def bucket_onehot(window_len, bucket_count):
    distance = np.arange(window_len)
    scaled = np.floor(np.log(np.maximum(distance, 1) / 16.0) / np.log(8.0) * 16.0)
    larger = np.minimum(16 + np.maximum(scaled, 0), bucket_count - 1)
    bucket = np.where(distance < 16, distance, larger).astype(np.int32)
    return (bucket[:, None] == np.arange(bucket_count)[None, :]).astype(np.float32)


def skewed(extended, row_count, col_count):
    head_count = extended.shape[0]
    span = row_count + col_count
    flipped = jnp.concatenate(
        [extended[:, ::-1], jnp.zeros((head_count, 1), extended.dtype)], axis=1
    )
    tiled = jnp.broadcast_to(flipped[:, None, :], (head_count, row_count, span)).reshape(
        head_count, row_count * span
    )
    tiled = tiled[:, : row_count * (span - 1)].reshape(head_count, row_count, span - 1)
    return tiled[:, :, row_count - 1 : row_count - 1 + col_count]


def rms_scale(values, gain):
    return values * lax.rsqrt(jnp.mean(values * values, axis=-1, keepdims=True) + epsilon) * gain


def times_transposed(left, right):
    return lax.dot_general(
        left, right, (((1,), (1,)), ((), ())), preferred_element_type=jnp.float32
    )


def transposed_times(left, right):
    return lax.dot_general(
        left, right, (((0,), (0,)), ((), ())), preferred_element_type=jnp.float32
    )


def compose(earlier, later):
    return (earlier[0] * later[0], later[0][:, None, None] * earlier[1] + later[1])


def group_state(carried_state, query_c, key_c, value_c, seg_group, seg_before, decay_rate):
    length_c = query_c.shape[0]
    position = jnp.arange(length_c).astype(jnp.float32)
    distance = position[:, None] - position[None, :]
    inside = (distance >= 0) & (seg_group[:, None] == seg_group[None, :])
    decay_w = jnp.where(
        inside[None], jnp.exp(-decay_rate[:, None, None] * jnp.maximum(distance, 0.0)[None]), 0.0
    )
    affinity = jnp.einsum("ihd,jhd->hij", query_c, key_c, precision=highest) * state_scale
    readout = jnp.einsum("hij,jhd->ihd", affinity * decay_w, value_c, precision=highest)
    live_mask = (seg_group == seg_before).astype(jnp.float32)
    entering = (
        jnp.exp(-decay_rate[None, :] * (position[:, None] + 1.0)) * live_mask[:, None] * state_scale
    )
    readout = (
        readout
        + jnp.einsum("ihd,hde->ihe", query_c, carried_state, precision=highest)
        * entering[:, :, None]
    )
    keeping = (seg_group == seg_group[-1]).astype(jnp.float32)
    leaving = (
        jnp.exp(-decay_rate[None, :] * (length_c - 1.0 - position[:, None])) * keeping[:, None]
    )
    carry_keep = jnp.exp(-decay_rate * length_c) * (seg_group[-1] == seg_before).astype(jnp.float32)
    updated = jnp.einsum("jhd,jhe->hde", key_c * leaving[:, :, None], value_c, precision=highest)
    updated = updated + carry_keep[:, None, None] * carried_state
    return (updated, readout)


def local_states(query_f, key_f, value_f, decay_rate, seg_block, seg_before):
    block_len, head_count, head_width = query_f.shape
    count = block_len // WIN
    items = (
        query_f.reshape(count, WIN, head_count, head_width),
        key_f.reshape(count, WIN, head_count, head_width),
        value_f.reshape(count, WIN, head_count, head_width),
        seg_block.reshape(count, WIN),
    )

    def step(carry, item):
        carried_state, prior = carry
        updated, readout = group_state(
            carried_state, item[0], item[1], item[2], item[3], prior, decay_rate
        )
        return ((updated, item[3][-1]), readout)

    start_carry = (jnp.zeros((head_count, head_width, head_width), jnp.float32), seg_before)
    (final_state, _), readouts = lax.scan(step, start_carry, items)
    return (readouts.reshape(block_len, head_count, head_width), final_state)


def general_shards(
    tokens,
    cotangent,
    segments,
    w_query,
    w_key,
    w_value,
    w_out,
    w_up,
    w_down,
    norm_one,
    norm_two,
    rel_table,
    decay_rate,
):
    heads_here = rel_table.shape[0]
    head_width = HD
    tok_here = tokens.shape[0]
    block_len = lax.axis_size("head") * tok_here
    block_count = block_len // WIN
    pair_width = heads_here * head_width
    scale = 1.0 / math.sqrt(head_width)
    gathered = (
        lax.all_gather(w_query, ("head", "seq"), axis=0, tiled=True),
        lax.all_gather(w_key, ("head", "seq"), axis=0, tiled=True),
        lax.all_gather(w_value, ("head", "seq"), axis=0, tiled=True),
        lax.all_gather(w_out, ("head", "seq"), axis=0, tiled=True),
        lax.all_gather(w_up, ("head", "seq"), axis=0, tiled=True),
        lax.all_gather(w_down, ("head", "seq"), axis=0, tiled=True),
        lax.all_gather(norm_one, ("head", "seq"), axis=0, tiled=True),
        lax.all_gather(norm_two, ("head", "seq"), axis=0, tiled=True),
    )
    full_query, full_key, full_value, full_out, full_up, full_down, gain_one, gain_two = gathered
    inputs_f = tokens.astype(jnp.float32)
    scaled_one, norm_back_one = jax.vjp(rms_scale, inputs_f, gain_one.astype(jnp.float32))
    normed = scaled_one.astype(jnp.bfloat16)
    projected = jnp.stack(
        [
            jnp.dot(normed, full_query, preferred_element_type=jnp.float32),
            jnp.dot(normed, full_key, preferred_element_type=jnp.float32),
            jnp.dot(normed, full_value, preferred_element_type=jnp.float32),
        ]
    ).astype(jnp.bfloat16)
    regrouped = lax.all_to_all(projected, "head", split_axis=2, concat_axis=1, tiled=True)
    prior_pairs = from_behind(regrouped[1:, block_len - WIN :], "seq", 1)
    pairs_ext = jnp.concatenate([prior_pairs, regrouped[1:]], axis=1)
    query_heads = regrouped[0].reshape(block_len, heads_here, head_width)
    key_ext = pairs_ext[0].reshape(block_len + WIN, heads_here, head_width)
    value_ext = pairs_ext[1].reshape(block_len + WIN, heads_here, head_width)
    block_base = lax.axis_index("seq") * block_len
    padded_segs = jnp.concatenate([jnp.full((WIN,), -1, jnp.int32), segments])
    seg_ext = lax.dynamic_slice_in_dim(padded_segs, block_base, block_len + WIN, 0)
    seg_block = seg_ext[WIN:]
    seg_before = seg_ext[WIN - 1]
    onehot_table = jnp.asarray(bucket_onehot(WIN, BUCKETS))
    by_distance = jnp.dot(rel_table, onehot_table.T, precision=highest)
    bias_ext = jnp.concatenate(
        [
            jnp.zeros((heads_here, WIN - 1), jnp.float32),
            by_distance,
            jnp.zeros((heads_here, WIN), jnp.float32),
        ],
        axis=1,
    )
    bias_full, skew_back = jax.vjp(lambda extended: skewed(extended, WIN, 2 * WIN), bias_ext)
    row_pos = jnp.arange(WIN, dtype=jnp.int32)[:, None]
    col_pos = jnp.arange(2 * WIN, dtype=jnp.int32)[None, :]
    near = (row_pos - col_pos + WIN >= 0) & (row_pos - col_pos + WIN < WIN)

    def block_inputs(number):
        start = number * WIN
        query_b = lax.dynamic_slice_in_dim(query_heads, start, WIN, 0)
        key_b = lax.dynamic_slice_in_dim(key_ext, start, 2 * WIN, 0)
        value_b = lax.dynamic_slice_in_dim(value_ext, start, 2 * WIN, 0)
        seg_q = lax.dynamic_slice_in_dim(seg_block, start, WIN, 0)
        seg_k = lax.dynamic_slice_in_dim(seg_ext, start, 2 * WIN, 0)
        visible = near & (seg_q[:, None] == seg_k[None, :])
        raw = jnp.einsum("ihd,jhd->hij", query_b, key_b, preferred_element_type=jnp.float32) * scale
        scores = jnp.where(visible[None], raw + bias_full, negative)
        return (query_b, key_b, value_b, scores)

    def forward_block(number):
        query_b, key_b, value_b, scores = block_inputs(number)
        top_score = jnp.max(scores, axis=-1, keepdims=True)
        exp_scores = jnp.exp(scores - top_score)
        total_mass = jnp.sum(exp_scores, axis=-1, keepdims=True)
        softmax_w = exp_scores / total_mass
        attended_b = jnp.einsum(
            "hij,jhd->ihd",
            softmax_w.astype(jnp.bfloat16),
            value_b,
            preferred_element_type=jnp.float32,
        )
        return (attended_b, (top_score + jnp.log(total_mass))[..., 0])

    numbers = jnp.arange(block_count, dtype=jnp.int32)
    attended_blocks, log_mass = lax.map(forward_block, numbers)
    attended = attended_blocks.reshape(block_len, heads_here, head_width)
    query_f = query_heads.astype(jnp.float32)
    key_f = key_ext[WIN:].astype(jnp.float32)
    value_f = value_ext[WIN:].astype(jnp.float32)

    def states_here(query_a, key_a, value_a, rates):
        return local_states(query_a, key_a, value_a, rates, seg_block, seg_before)

    (readout_local, state_local), states_back = jax.vjp(
        states_here, query_f, key_f, value_f, decay_rate
    )
    position = jnp.arange(block_len).astype(jnp.float32)
    live_mask = (seg_block == seg_before).astype(jnp.float32)
    enter_decay = (
        jnp.exp(-decay_rate[None, :] * (position[:, None] + 1.0)) * live_mask[:, None] * state_scale
    )
    carry_keep = jnp.exp(-decay_rate * block_len) * (seg_block[-1] == seg_before).astype(
        jnp.float32
    )
    identity = (jnp.ones_like(carry_keep), jnp.zeros_like(state_local))
    carried = prefix((carry_keep, state_local), "seq", compose, identity, False)
    carry_in = carried[1]
    carry_term = (
        jnp.einsum("ihd,hde->ihe", query_f, carry_in, precision=highest) * enter_decay[:, :, None]
    )
    mixed_heads = (
        (attended + readout_local + carry_term).astype(jnp.bfloat16).reshape(block_len, pair_width)
    )
    mixed_tok = lax.all_to_all(mixed_heads, "head", split_axis=0, concat_axis=1, tiled=True)
    resid_one = inputs_f + jnp.dot(mixed_tok, full_out, preferred_element_type=jnp.float32)
    scaled_two, norm_back_two = jax.vjp(rms_scale, resid_one, gain_two.astype(jnp.float32))
    normed_two = scaled_two.astype(jnp.bfloat16)
    up_proj = jnp.dot(normed_two, full_up, preferred_element_type=jnp.float32)
    activated, gelu_back = jax.vjp(jax.nn.gelu, up_proj)
    act_low = activated.astype(jnp.bfloat16)
    output = (resid_one + jnp.dot(act_low, full_down, preferred_element_type=jnp.float32)).astype(
        jnp.bfloat16
    )
    back_query, back_key, back_value = (full_query, full_key, full_value)
    back_out, back_up, back_down = (full_out, full_up, full_down)
    grad_down_w = transposed_times(act_low, cotangent)
    act_grad = times_transposed(cotangent, back_down)
    up_grad = gelu_back(act_grad)[0].astype(jnp.bfloat16)
    grad_up_w = transposed_times(normed_two, up_grad)
    normed_two_grad = times_transposed(up_grad, back_up)
    resid_grad_n, grad_gain_two = norm_back_two(normed_two_grad)
    resid_grad = cotangent.astype(jnp.float32) + resid_grad_n
    attn_grad = resid_grad.astype(jnp.bfloat16)
    grad_out_w = transposed_times(mixed_tok, attn_grad)
    mixed_grad = times_transposed(attn_grad, back_out).astype(jnp.bfloat16)
    heads_grad = lax.all_to_all(mixed_grad, "head", split_axis=1, concat_axis=0, tiled=True)
    heads_grad3 = heads_grad.reshape(block_len, heads_here, head_width)

    def backward_block(item):
        number, log_block = item
        query_b, key_b, value_b, scores = block_inputs(number)
        out_grad_b = lax.dynamic_slice_in_dim(heads_grad3, number * WIN, WIN, 0)
        softmax_w = jnp.exp(scores - log_block[..., None])
        prob_grad = jnp.einsum(
            "ihd,jhd->hij", out_grad_b, value_b, preferred_element_type=jnp.float32
        )
        score_grad = softmax_w * (
            prob_grad - jnp.sum(softmax_w * prob_grad, axis=-1, keepdims=True)
        )
        score_low = score_grad.astype(jnp.bfloat16)
        query_grad_b = (
            jnp.einsum("hij,jhd->ihd", score_low, key_b, preferred_element_type=jnp.float32) * scale
        )
        key_grad_b = (
            jnp.einsum("hij,ihd->jhd", score_low, query_b, preferred_element_type=jnp.float32)
            * scale
        )
        value_grad_b = jnp.einsum(
            "hij,ihd->jhd",
            softmax_w.astype(jnp.bfloat16),
            out_grad_b,
            preferred_element_type=jnp.float32,
        )
        ext_grad_b = skew_back(score_low.astype(jnp.float32))[0]
        return (query_grad_b, key_grad_b, value_grad_b, ext_grad_b)

    query_grads, key_grads, value_grads, ext_grads = lax.map(backward_block, (numbers, log_mass))
    query_grad_att = query_grads.reshape(block_len, heads_here, head_width)

    def fold_pairs(pieces):
        zero_edge = jnp.zeros_like(pieces[:1, :WIN])
        return jnp.concatenate([pieces[:, :WIN], zero_edge], axis=0) + jnp.concatenate(
            [zero_edge, pieces[:, WIN:]], axis=0
        )

    key_folded = fold_pairs(key_grads)
    value_folded = fold_pairs(value_grads)
    sent_pairs = jnp.stack([key_folded[0], value_folded[0]]).reshape(2, WIN, pair_width)
    received = from_behind(sent_pairs.astype(jnp.bfloat16), "seq", -1).astype(sent_pairs.dtype)
    tail_pairs = jnp.concatenate(
        [jnp.zeros((2, block_len - WIN, pair_width), jnp.float32), received], axis=1
    )
    tail_pairs = tail_pairs.reshape(2, block_len, heads_here, head_width)
    key_grad_att = key_folded[1:].reshape(block_len, heads_here, head_width) + tail_pairs[0]
    value_grad_att = value_folded[1:].reshape(block_len, heads_here, head_width) + tail_pairs[1]
    heads_grad_f = heads_grad3.astype(jnp.float32)
    grad_local = jnp.einsum(
        "ihd,ihe->hde", query_f * enter_decay[:, :, None], heads_grad_f, precision=highest
    )
    back_chain = prefix((carry_keep, grad_local), "seq", compose, identity, True)
    carry_out_grad = back_chain[1]
    query_grad_s, key_grad_s, value_grad_s, rate_grad_s = states_back(
        (heads_grad_f, carry_out_grad)
    )
    query_grad_c = (
        jnp.einsum("ihe,hde->ihd", heads_grad_f, carry_in, precision=highest)
        * enter_decay[:, :, None]
    )
    rate_grad_c = -jnp.sum(heads_grad_f * carry_term * (position[:, None, None] + 1.0), axis=(0, 2))
    rate_grad_a = -block_len * carry_keep * jnp.sum(carry_out_grad * carry_in, axis=(1, 2))
    rate_grad = rate_grad_s + rate_grad_c + rate_grad_a
    query_grad = query_grad_att + query_grad_s + query_grad_c
    key_grad = key_grad_att + key_grad_s
    value_grad = value_grad_att + value_grad_s
    triple_grad = (
        jnp.stack([query_grad, key_grad, value_grad])
        .reshape(3, block_len, pair_width)
        .astype(jnp.bfloat16)
    )
    token_grads = lax.all_to_all(triple_grad, "head", split_axis=1, concat_axis=2, tiled=True)
    grad_query_w = transposed_times(normed, token_grads[0])
    grad_key_w = transposed_times(normed, token_grads[1])
    grad_value_w = transposed_times(normed, token_grads[2])
    normed_grad = (
        times_transposed(token_grads[0], back_query)
        + times_transposed(token_grads[1], back_key)
        + times_transposed(token_grads[2], back_value)
    )
    input_grad_n, grad_gain_one = norm_back_one(normed_grad)
    input_grad = (resid_grad + input_grad_n).astype(jnp.bfloat16)
    ext_total = jnp.sum(ext_grads, axis=0)
    table_grad = jnp.dot(ext_total[:, WIN - 1 : 2 * WIN - 1], onehot_table, precision=highest)
    table_grad, rate_grad = lax.psum((table_grad, rate_grad), "seq")
    summed = (
        lax.psum_scatter(grad_query_w, ("head", "seq"), scatter_dimension=0, tiled=True),
        lax.psum_scatter(grad_key_w, ("head", "seq"), scatter_dimension=0, tiled=True),
        lax.psum_scatter(grad_value_w, ("head", "seq"), scatter_dimension=0, tiled=True),
        lax.psum_scatter(grad_out_w, ("head", "seq"), scatter_dimension=0, tiled=True),
        lax.psum_scatter(grad_up_w, ("head", "seq"), scatter_dimension=0, tiled=True),
        lax.psum_scatter(grad_down_w, ("head", "seq"), scatter_dimension=0, tiled=True),
        lax.psum_scatter(grad_gain_one, ("head", "seq"), scatter_dimension=0, tiled=True),
        lax.psum_scatter(grad_gain_two, ("head", "seq"), scatter_dimension=0, tiled=True),
    )
    grad_query, grad_key, grad_value, grad_out, grad_up, grad_down, grad_norm_one, grad_norm_two = (
        summed
    )
    return (
        output,
        input_grad,
        grad_query,
        grad_key,
        grad_value,
        grad_out,
        grad_up,
        grad_down,
        grad_norm_one,
        grad_norm_two,
        table_grad,
        rate_grad,
    )


def solution(mesh):
    devices = mesh.shape["head"] * mesh.shape["seq"]
    tiled = mesh.shape["head"] == 4 and 1024 // devices == 32
    return jax.shard_map(
        shards if tiled else general_shards,
        mesh=mesh,
        in_specs=(
            P(("seq", "head"), None),
            P(("seq", "head"), None),
            P(),
            P(("head", "seq"), None),
            P(("head", "seq"), None),
            P(("head", "seq"), None),
            P(("head", "seq"), None),
            P(("head", "seq"), None),
            P(("head", "seq"), None),
            P(("head", "seq")),
            P(("head", "seq")),
            P("head", None),
            P("head"),
        ),
        out_specs=(
            P(("seq", "head"), None),
            P(("seq", "head"), None),
            P(("head", "seq"), None),
            P(("head", "seq"), None),
            P(("head", "seq"), None),
            P(("head", "seq"), None),
            P(("head", "seq"), None),
            P(("head", "seq"), None),
            P(("head", "seq")),
            P(("head", "seq")),
            P("head", None),
            P("head"),
        ),
        check_vma=False,
    )
```
